32 devices in a mesh: dp: 8 (over z, x), head: 4 (over y, core).
Axes of the slice: x: 2, y: 2, z: 4, core: 2. Of those that a mesh axis runs over, the one named last changes fastest.
Arguments:
- patches: bfloat16 [12608, 768], P(('dp', 'head'))
- selected: int32 [64, 197], P(('dp', 'head')), may hold values from 0 to 1, as said below
- out_grad: bfloat16 [12608, 768], P(('dp', 'head')), may hold values from -6 to 6
- gain_one: bfloat16 [768], replicated, may hold values from 0.5 to 1.5
- shift_one: bfloat16 [768], replicated, may hold values from -1.5 to 1.5
- router_w: bfloat16 [768], replicated, may hold values from -0.21875 to 0.21875
- w_query: bfloat16 [768, 768], P('dp', 'head'), may hold values from -0.21875 to 0.21875
- b_query: bfloat16 [768], P('head'), may hold values from -1.5 to 1.5
- w_key: bfloat16 [768, 768], P('dp', 'head'), may hold values from -0.21875 to 0.21875
- w_value: bfloat16 [768, 768], P('dp', 'head'), may hold values from -0.21875 to 0.21875
- b_value: bfloat16 [768], P('head'), may hold values from -1.5 to 1.5
- w_out: bfloat16 [768, 768], P('head', 'dp'), may hold values from -0.875 to 0.875
- b_out: bfloat16 [768], replicated, may hold values from -1.5 to 1.5
- gain_two: bfloat16 [768], replicated, may hold values from 0.5 to 1.5
- shift_two: bfloat16 [768], replicated, may hold values from -1.5 to 1.5
- w_up: bfloat16 [768, 3072], P('dp', 'head'), may hold values from -0.21875 to 0.21875
- b_up: bfloat16 [3072], P('head'), may hold values from -1.5 to 1.5
- w_down: bfloat16 [3072, 768], P('head', 'dp'), may hold values from -0.109375 to 0.109375
- b_down: bfloat16 [768], replicated, may hold values from -1.5 to 1.5
Outputs:
- out_tokens: bfloat16 [12608, 768], P(('dp', 'head'))
- grad_patches: bfloat16 [12608, 768], P(('dp', 'head'))
- grad_gain_one: float32 [768], replicated
- grad_shift_one: float32 [768], replicated
- grad_router: float32 [768], replicated
- grad_query: float32 [768, 768], P('dp', 'head')
- grad_query_bias: float32 [768], P('head')
- grad_key: float32 [768, 768], P('dp', 'head')
- grad_value: float32 [768, 768], P('dp', 'head')
- grad_value_bias: float32 [768], P('head')
- grad_out: float32 [768, 768], P('head', 'dp')
- grad_out_bias: float32 [768], replicated
- grad_gain_two: float32 [768], replicated
- grad_shift_two: float32 [768], replicated
- grad_up: float32 [768, 3072], P('dp', 'head')
- grad_up_bias: float32 [3072], P('head')
- grad_down: float32 [3072, 768], P('head', 'dp')
- grad_down_bias: float32 [768], replicated
The draws below stay inside these ranges and needn't reach their ends.
Inputs may be any that keep to these rules, and one draw needn't show every extreme that they name: Each image has between 40 and 157 selected patches; some image has exactly 40, and all images of some device have 157, so that the most selected patches on one device is 314.
All inputs are finite; a program needn't handle non-finite values.
Results may differ from the reference program's by a relative error of at most 0.013.
Values may be sent and summed in bfloat16 or wider, within the bound.
No kernel may reach another device: no remote copies, remote signals or barrier semaphores. Data moves between devices by JAX's collectives and lax.ppermute only.
A program may use at most 128 MiB of HBM per device.

```python
import math
import jax
import jax.numpy as jnp
from jax import lax

D = 768
HEADS = 12
HEAD_DIM = 64
FF = 3072
SEQ = 197
IMG_DEV = 2
SEL_LO = 40
SEL_HI = 157
IMAGES = 64
TOKENS = 12608
N_DP = 8
N_HEAD = 4


def draw_patches(key, part):
    key = jax.random.fold_in(key, 11)
    key_rows, key_cols, key_vals = jax.random.split(key, 3)
    row_scale = 0.3 * jnp.exp(jax.random.uniform(key_rows, (TOKENS, 1), jnp.float32, 0.0, math.log(10.0)))
    col_scale = jnp.exp(jax.random.uniform(key_cols, (1, D), jnp.float32, -0.5, 0.5))
    values = jax.random.normal(key_vals, (TOKENS, D), jnp.float32)
    return (values * row_scale * col_scale).astype(jnp.bfloat16)


def draw_selected(key, part):
    key = jax.random.fold_in(key, 23)
    key_base, key_jitter, key_full, key_least, key_order = jax.random.split(key, 5)
    devices_all = IMAGES // IMG_DEV
    count_span = SEL_HI - SEL_LO
    base_level = jax.random.randint(key_base, (devices_all, 1), 0, count_span + 1)
    jitter = jax.random.randint(key_jitter, (devices_all, IMG_DEV), 0, count_span + 1)
    counts = (SEL_LO + (3 * base_level + jitter) // 4).reshape(IMAGES)
    owner_dev = jnp.arange(IMAGES, dtype=jnp.int32) // IMG_DEV
    busiest = jax.random.randint(key_full, (), 0, devices_all)
    counts = jnp.where(owner_dev == busiest, SEL_HI, counts)
    lightest = (busiest * IMG_DEV + IMG_DEV + jax.random.randint(key_least, (), 0, IMAGES - IMG_DEV)) % IMAGES
    counts = jnp.where(jnp.arange(IMAGES, dtype=jnp.int32) == lightest, SEL_LO, counts)
    order_keys = jax.random.randint(key_order, (IMAGES, SEQ), 0, 1 << 20) * SEQ + jnp.arange(SEQ, dtype=jnp.int32)[None, :]
    patch_rank = jnp.argsort(jnp.argsort(order_keys, axis=1), axis=1)
    return (patch_rank < counts[:, None]).astype(jnp.int32)


def levels(key, shape, cuts, smallest, largest):
    def one(dim, parts):
        steps = jax.random.uniform(jax.random.fold_in(jax.random.fold_in(key, 6), dim), (parts,), jnp.float32, smallest / len(cuts), largest / len(cuts))
        return jnp.repeat(jnp.exp(steps), shape[dim] // parts).reshape((-1,) + (1,) * (len(shape) - dim - 1))

    loudness = one(*cuts[0])
    for cut in cuts[1:]:
        loudness = loudness * one(*cut)
    return loudness


def bell_draw(key, dims, width, most, cuts=(), kind=jnp.bfloat16):
    gain = levels(key, dims, cuts, -0.22, 0.18) if cuts else 1.0
    values = jax.random.normal(key, dims, jnp.float32) * width * gain
    return jnp.minimum(jnp.maximum(values, -most), most).astype(kind)


def setup_inputs(seed: int = 0) -> dict:
    key_list = jax.random.split(jax.random.key(seed), 20)
    patches = draw_patches(jax.random.fold_in(key_list[19], 71), 0)
    selected = draw_selected(jax.random.fold_in(key_list[19], 71), 0)
    out_grad = bell_draw(key_list[2], (TOKENS, D), 1.0, 6.0, ((0, 32),))
    gain_one = jnp.clip(1.0 + 0.1 * jax.random.normal(key_list[3], (D,), jnp.float32), 0.5, 1.5).astype(jnp.bfloat16)
    shift_one = bell_draw(key_list[4], (D,), 0.3, 1.5)
    router_w = bell_draw(key_list[5], (D,), D ** -0.5, 0.21875)
    w_query = bell_draw(key_list[6], (D, D), D ** -0.5, 0.21875, ((0, 8), (1, 4)))
    b_query = bell_draw(key_list[7], (D,), 0.3, 1.5, ((0, 4),))
    w_key = bell_draw(key_list[8], (D, D), D ** -0.5, 0.21875, ((0, 8), (1, 4)))
    w_value = bell_draw(key_list[9], (D, D), D ** -0.5, 0.21875, ((0, 8), (1, 4)))
    b_value = bell_draw(key_list[10], (D,), 0.3, 1.5, ((0, 4),))
    w_out = bell_draw(key_list[11], (D, D), (D // 16) ** -0.5, 0.875, ((0, 4), (1, 8)))
    b_out = bell_draw(key_list[12], (D,), 0.3, 1.5)
    gain_two = jnp.clip(1.0 + 0.1 * jax.random.normal(key_list[13], (D,), jnp.float32), 0.5, 1.5).astype(jnp.bfloat16)
    shift_two = bell_draw(key_list[14], (D,), 0.3, 1.5)
    w_up = bell_draw(key_list[15], (D, FF), D ** -0.5, 0.21875, ((0, 8), (1, 4)))
    b_up = bell_draw(key_list[16], (FF,), 0.3, 1.5, ((0, 4),))
    w_down = bell_draw(key_list[17], (FF, D), FF ** -0.5, 0.109375, ((0, 4), (1, 8)))
    b_down = bell_draw(key_list[18], (D,), 0.3, 1.5)
    return dict(patches=patches, selected=selected, out_grad=out_grad, gain_one=gain_one, shift_one=shift_one, router_w=router_w, w_query=w_query, b_query=b_query, w_key=w_key, w_value=w_value, b_value=b_value, w_out=w_out, b_out=b_out, gain_two=gain_two, shift_two=shift_two, w_up=w_up, b_up=b_up, w_down=w_down, b_down=b_down)


epsilon = 1e-06
highest = lax.Precision.HIGHEST

@jax.custom_vjp
def low(v):
    return lax.optimization_barrier(v.astype(jnp.bfloat16)).astype(jnp.float32)

@jax.custom_vjp
def low_back(v):
    return v

def low_keep(v):
    return (low(v), None)

def low_pass(kept, grad):
    return (grad,)

def back_keep(v):
    return (v, None)

def back_low(kept, grad):
    return (low(grad),)
low.defvjp(low_keep, low_pass)
low_back.defvjp(back_keep, back_low)

def layer_norm(inputs, gain_vec, shift_vec):
    center = inputs - lax.optimization_barrier(jnp.mean(inputs, axis=-1, keepdims=True))
    spread = lax.optimization_barrier(jnp.mean(center * center, axis=-1, keepdims=True))
    return center * lax.rsqrt(spread + epsilon) * gain_vec + shift_vec

def block_forward(params, inputs, chosen):
    gain_one, shift_one, router_w, w_query, b_query, w_key, w_value, b_value, w_out, b_out, gain_two, shift_two, w_up, b_up, w_down, b_down = params
    images_in = inputs.shape[0]
    head_shape = (images_in, SEQ, HEADS, HEAD_DIM)
    normed = layer_norm(inputs, gain_one, shift_one)
    gate_vals = jax.nn.sigmoid(jnp.einsum('gsd,d->gs', normed, router_w, precision=highest))
    rows_low = low(normed)
    queries = low(low_back(jnp.einsum('gsd,de->gse', rows_low, w_query, precision=highest)) + b_query)
    key_vecs = low(low_back(jnp.einsum('gsd,de->gse', rows_low, w_key, precision=highest)))
    value_vecs = low(low_back(jnp.einsum('gsd,de->gse', rows_low, w_value, precision=highest)) + b_value)
    raw_scores = low_back(jnp.einsum('gqhd,gkhd->ghqk', queries.reshape(head_shape), key_vecs.reshape(head_shape), precision=highest)) * HEAD_DIM ** (-0.5)
    allowed = (chosen > 0.5)[:, None, None, :]
    masked = jnp.where(allowed, raw_scores, -1e+30)
    shifted = masked - lax.optimization_barrier(jnp.max(masked, axis=-1, keepdims=True))
    exp_vals = jnp.exp(shifted)
    soft_probs = low(exp_vals / lax.optimization_barrier(jnp.sum(exp_vals, axis=-1, keepdims=True)))
    context_mix = jnp.einsum('ghqk,gkhd->gqhd', soft_probs, value_vecs.reshape(head_shape), precision=highest).reshape(images_in, SEQ, D)
    context_mix = low(low_back(context_mix))
    attended = low_back(jnp.einsum('gsd,de->gse', context_mix, w_out, precision=highest)) + b_out
    mixed_rows = inputs + (chosen * gate_vals)[..., None] * attended
    mlp_in = low(layer_norm(mixed_rows, gain_two, shift_two))
    upper_pre = low_back(jnp.einsum('gsd,df->gsf', mlp_in, w_up, precision=highest)) + b_up
    active = low(jax.nn.gelu(upper_pre, approximate=False))
    return mixed_rows + low_back(jnp.einsum('gsf,fd->gsd', active, w_down, precision=highest)) + b_down

def reference(patches, selected, out_grad, gain_one, shift_one, router_w, w_query, b_query, w_key, w_value, b_value, w_out, b_out, gain_two, shift_two, w_up, b_up, w_down, b_down):
    params = tuple((param_arr.astype(jnp.float32) for param_arr in (gain_one, shift_one, router_w, w_query, b_query, w_key, w_value, b_value, w_out, b_out, gain_two, shift_two, w_up, b_up, w_down, b_down)))
    group_size = IMG_DEV * N_HEAD
    shaped = (N_DP, group_size, SEQ, D)

    def one_group(totals, pieces):
        inputs_grp, chosen_grp, grad_grp = pieces
        chosen = chosen_grp.astype(jnp.float32)

        def forward(params_in, inputs_in):
            return block_forward(params_in, inputs_in, chosen)
        result, pullback = jax.vjp(forward, params, inputs_grp.astype(jnp.float32))
        param_grads, input_grads = pullback(grad_grp.astype(jnp.float32))
        totals = jax.tree.map(jnp.add, totals, param_grads)
        return (totals, (result.astype(jnp.bfloat16), input_grads.astype(jnp.bfloat16)))
    zero_acc = jax.tree.map(jnp.zeros_like, params)
    totals, outputs = lax.scan(one_group, zero_acc, (patches.reshape(shaped), selected.reshape(N_DP, group_size, SEQ), out_grad.reshape(shaped)))
    return (outputs[0].reshape(TOKENS, D), outputs[1].reshape(TOKENS, D), totals[0], totals[1], totals[2], totals[3], totals[4], totals[5], totals[6], totals[7], totals[8], totals[9], totals[10], totals[11], totals[12], totals[13], totals[14], totals[15])
```

```python
import math

import jax
import jax.numpy as jnp
from jax import lax
from jax.experimental import pallas as pl
from jax.experimental.pallas import tpu as pltpu
from jax.sharding import PartitionSpec as P

HEADS = 12
EPS = 1e-06
F32 = jnp.float32
BF16 = jnp.bfloat16
VMEM = pl.BlockSpec(memory_space=pltpu.VMEM)
SMEM = pl.BlockSpec(memory_space=pltpu.SMEM)
ANYS = pl.BlockSpec(memory_space=pl.ANY)
LIMIT = 48 * 1024 * 1024
INV_SQRT2 = 0.7071067811865476
INV_SQRT2PI = 0.3989422804014327

NN = (((1,), (0,)), ((), ()))
NT = (((1,), (1,)), ((), ()))
TN = (((0,), (0,)), ((), ()))


def dot(a, b, dims=NN):
    return lax.dot_general(a, b, dims, preferred_element_type=F32)


def sds(shape, dtype):
    return jax.ShapeDtypeStruct(shape, dtype)


def call(body, outs, ins, scratch=(), flops=0, nbytes=0, trans=0, name=None):
    return pl.pallas_call(
        body,
        out_shape=[o for o, _ in outs],
        in_specs=[s for _, s in ins],
        out_specs=[s for _, s in outs],
        scratch_shapes=list(scratch),
        compiler_params=pltpu.CompilerParams(vmem_limit_bytes=LIMIT),
        cost_estimate=pl.CostEstimate(
            flops=int(flops), bytes_accessed=int(nbytes), transcendentals=int(trans)
        ),
        name=name,
    )(*[a for a, _ in ins])


def norm_parts(v):
    center = v - jnp.mean(v, axis=-1, keepdims=True)
    spread = jnp.mean(center * center, axis=-1, keepdims=True)
    rstd = lax.rsqrt(spread + EPS)
    return center * rstd, rstd


def norm_back(u, xhat, rstd):
    return rstd * (
        u
        - jnp.mean(u, axis=-1, keepdims=True)
        - xhat * jnp.mean(u * xhat, axis=-1, keepdims=True)
    )


class Plan:
    def __init__(self, rows, seq, images, width, hidden, dp, head):
        self.rows, self.seq, self.images, self.width = rows, seq, images, width
        self.dp, self.head = dp, head
        self.pairs = head // 2
        self.cols = width // head
        self.hid = hidden // head
        self.hd = width // HEADS
        self.local_heads = HEADS // head
        self.piece = width // dp
        self.fast = dp == 8 and head == 4 and self.piece % 16 == 0
        self.base = [seq * i // 16 * 16 for i in range(images)]
        self.win = max(-(-(seq * (i + 1) - self.base[i]) // 16) * 16 for i in range(images))
        self.pad = self.base[-1] + self.win
        self.off = self.cols // 128 * 128
        self.lo = self.cols - self.off
        self.nq = 4 * self.cols - self.off
        self.cw = -(-self.cols // 128) * 128
        self.scale = 1.0 / math.sqrt(self.hd)


def source_rows(p, pos_ref, zz, xx):
    z, x = pos_ref[0], pos_ref[1]
    part = ((z - zz) & 3) * 2 + (x ^ xx)
    return pl.multiple_of(part * p.piece, p.piece)


def piece_list(p, pos_ref, other):
    core = pos_ref[2] ^ other
    found = []
    for b3 in range(2):
        for b2 in range(2):
            yy = jnp.where(core == 0, b3, b2)
            xx = jnp.where(core == 0, b2, b3)
            for zz in range(4):
                found.append((b3, b2, zz, yy, source_rows(p, pos_ref, zz, xx)))
    return found


def load_start(p, refs, buf, sem, pos_ref, other):
    if not p.fast:
        copy = pltpu.make_async_copy(refs[0], buf, sem.at[0])
        copy.start()
        return [copy]
    copies = []
    for i, (b3, b2, zz, yy, row) in enumerate(piece_list(p, pos_ref, other)):
        copy = pltpu.make_async_copy(
            refs[b3].at[b2, zz], buf.at[yy, pl.ds(row, p.piece)], sem.at[i]
        )
        copy.start()
        copies.append(copy)
    return copies


def store_start(p, buf, refs, sem, pos_ref, other):
    if not p.fast:
        copy = pltpu.make_async_copy(buf, refs[0], sem.at[0])
        copy.start()
        return [copy]
    copies = []
    for i, (b3, b2, zz, yy, row) in enumerate(piece_list(p, pos_ref, other)):
        copy = pltpu.make_async_copy(
            buf.at[yy, pl.ds(row, p.piece)], refs[b3].at[b2, zz], sem.at[i]
        )
        copy.start()
        copies.append(copy)
    return copies


def wait_all(copies):
    for copy in copies:
        copy.wait()


def piece_shapes(p):
    if p.fast:
        return [sds((2, 4, p.piece, p.width), BF16)] * 2
    return [sds((2, p.width, p.width), BF16)]


def n_sem(p):
    return 16 if p.fast else 1


def entry_kernel(p, patches, out_grad, gain_one, shift_one, router):
    def body(x_ref, og_ref, g_ref, s_ref, r_ref, low_ref, gate_ref, down_ref):
        xhat, _ = norm_parts(x_ref[...].astype(F32))
        normed = xhat * g_ref[...] + s_ref[...]
        low_ref[...] = normed.astype(BF16)
        logit = jnp.sum(normed * r_ref[...], axis=-1, keepdims=True)
        gate_ref[...] = 1.0 / (1.0 + jnp.exp(-logit))
        down_ref[...] = jnp.sum(og_ref[...].astype(F32), axis=0, keepdims=True)

    return call(
        body,
        [
            (sds((p.pad, p.width), BF16), VMEM),
            (sds((p.pad, 1), F32), VMEM),
            (sds((1, p.width), F32), VMEM),
        ],
        [(a, VMEM) for a in (patches, out_grad, gain_one, shift_one, router)],
        flops=p.pad * p.width * 10,
        nbytes=p.pad * p.width * 6,
        name="entry",
    )


def attention_forward(p, pos, weights, other, rows_low, bias, key_mask, carry, tail):
    last = tail is not None
    win, pad, lh, hd = p.win, p.pad, p.local_heads, p.hd

    def body(*refs):
        nw = len(weights)
        pos_ref, w_refs = refs[0], refs[1 : 1 + nw]
        rest = list(refs[1 + nw :])
        low_ref, bias_ref, mask_ref = rest[:3]
        rest = rest[3:]
        carry_ref = None
        if carry is not None:
            carry_ref, rest = rest[0], rest[1:]
        if last:
            x_ref, sg_ref, bo_ref, g2_ref, s2_ref = rest[:5]
            rest = rest[5:]
            qkv_ref, prob_ref, ctx_ref, att_ref, mixed_ref, in_ref = rest[:6]
            rest = rest[6:]
        else:
            qkv_ref, prob_ref, ctx_ref, att_ref = rest[:4]
            rest = rest[4:]
        wbuf, ctx, sem = rest
        wait_all(load_start(p, w_refs, wbuf, sem, pos_ref, other))
        low = low_ref[...]
        total = None
        for b in range(2):
            qkv = dot(low, wbuf[b, :, p.off :]) + bias_ref[b]
            qkv_ref[b] = qkv.astype(BF16)
            ctx[...] = jnp.zeros((pad, p.cw), F32)
            for img in range(p.images):
                first = p.base[img]
                at = lax.broadcasted_iota(jnp.int32, (win, 1), 0) + first
                valid = (at >= p.seq * img) & (at < p.seq * (img + 1))
                seen = mask_ref[img] > 0.0
                got = []
                for j in range(lh):
                    qs = p.lo + hd * j
                    q = qkv_ref[b, first : first + win, qs : qs + hd]
                    k = qkv_ref[b, first : first + win, qs + p.cols : qs + p.cols + hd]
                    v = qkv_ref[b, first : first + win, qs + 2 * p.cols : qs + 2 * p.cols + hd]
                    s = dot(q, k, NT) * p.scale
                    s = jnp.where(seen, s, -1e30)
                    e = jnp.exp(s - jnp.max(s, axis=-1, keepdims=True))
                    prob = e * (1.0 / jnp.sum(e, axis=-1, keepdims=True))
                    prob = jnp.where(valid, prob, 0.0).astype(BF16)
                    prob_ref[(b * p.images + img) * lh + j] = prob
                    got.append(dot(prob, v))
                if p.cw > p.cols:
                    got.append(jnp.zeros((win, p.cw - p.cols), F32))
                ctx[first : first + win, :] += jnp.concatenate(got, axis=1)
            mix = ctx[...].astype(BF16)
            ctx_ref[b] = mix
            part = dot(mix, wbuf[b, :, : p.cw], NT)
            total = part if total is None else total + part
        if carry_ref is not None:
            total = total + carry_ref[...]
        if not last:
            att_ref[...] = total
            return
        attended = total + bo_ref[...]
        att_ref[...] = attended
        mixed = x_ref[...].astype(F32) + sg_ref[...] * attended
        mixed_ref[...] = mixed
        xhat, _ = norm_parts(mixed)
        in_ref[...] = (xhat * g2_ref[...] + s2_ref[...]).astype(BF16)

    ins = [(pos, SMEM)] + [(w, ANYS) for w in weights]
    ins += [(a, VMEM) for a in (rows_low, bias, key_mask)]
    if carry is not None:
        ins.append((carry, VMEM))
    if last:
        ins += [(a, VMEM) for a in tail]
    outs = [
        (sds((2, pad, p.nq), BF16), VMEM),
        (sds((2 * p.images * lh, win, win), BF16), VMEM),
        (sds((2, pad, p.cw), BF16), VMEM),
        (sds((pad, p.width), F32), VMEM),
    ]
    if last:
        outs += [(sds((pad, p.width), F32), VMEM), (sds((pad, p.width), BF16), VMEM)]
    return call(
        body,
        outs,
        ins,
        [
            pltpu.VMEM((2, p.width, 4 * p.cols), BF16),
            pltpu.VMEM((pad, p.cw), F32),
            pltpu.SemaphoreType.DMA((n_sem(p),)),
        ],
        flops=2 * (2 * pad * p.width * (p.nq + p.cw) + p.images * lh * win * win * hd * 4),
        nbytes=2 * 2 * p.width * p.width + pad * p.width * 10,
        trans=2 * p.images * lh * win * win,
        name="attn_fwd",
    )


def up_kernel(p, pos, weights, other, mlp_in, bias):
    def body(*refs):
        nw = len(weights)
        pos_ref, w_refs = refs[0], refs[1 : 1 + nw]
        in_ref, b_ref, act_ref, slope_ref, wbuf, sem = refs[1 + nw :]
        wait_all(load_start(p, w_refs, wbuf, sem, pos_ref, other))
        rows = in_ref[...]
        for b in range(2):
            pre = dot(rows, wbuf[b]) + b_ref[b]
            phi = 0.5 * (1.0 + lax.erf(pre * INV_SQRT2))
            act_ref[b] = (pre * phi).astype(BF16)
            slope_ref[b] = (phi + pre * (jnp.exp(-0.5 * pre * pre) * INV_SQRT2PI)).astype(BF16)

    return call(
        body,
        [(sds((2, p.pad, p.hid), BF16), VMEM)] * 2,
        [(pos, SMEM)] + [(w, ANYS) for w in weights] + [(mlp_in, VMEM), (bias, VMEM)],
        [pltpu.VMEM((2, p.width, p.hid), BF16), pltpu.SemaphoreType.DMA((n_sem(p),))],
        flops=2 * 2 * p.pad * p.width * p.hid,
        nbytes=4 * p.width * p.hid + 10 * p.pad * p.hid,
        trans=2 * p.pad * p.hid * 2,
        name="up",
    )


def weight_grad(p, pos, other, lhs, rhs, received, name):
    def body(*refs):
        pos_ref, l_ref, r_ref = refs[:3]
        rest = list(refs[3:])
        nr = len(received) if received is not None else 0
        got_refs, rest = rest[:nr], rest[nr:]
        no = len(piece_shapes(p))
        out_refs, rest = rest[:no], rest[no:]
        if nr:
            gbuf, rbuf, sem, rsem = rest
            loads = load_start(p, got_refs, rbuf, rsem, pos_ref, other)
        else:
            gbuf, sem = rest
        left = l_ref[...]
        for b in range(2):
            g = dot(left, r_ref[b], TN)
            if nr:
                if b == 0:
                    wait_all(loads)
                g = g + rbuf[b].astype(F32)
            gbuf[b] = g.astype(BF16)
        wait_all(store_start(p, gbuf, out_refs, sem, pos_ref, other))

    scratch = [pltpu.VMEM((2, p.width, p.hid), BF16)]
    if received is not None:
        scratch.append(pltpu.VMEM((2, p.width, p.hid), BF16))
    scratch.append(pltpu.SemaphoreType.DMA((n_sem(p),)))
    if received is not None:
        scratch.append(pltpu.SemaphoreType.DMA((n_sem(p),)))
    return call(
        body,
        [(s, ANYS) for s in piece_shapes(p)],
        [(pos, SMEM), (lhs, VMEM), (rhs, VMEM)] + [(r, ANYS) for r in received or ()],
        scratch,
        flops=2 * 2 * p.pad * p.width * p.hid,
        nbytes=8 * p.width * p.hid + 6 * p.pad * p.hid,
        name=name,
    )


def down_kernel(p, pos, w_up, w_down, other, active, slope, out_grad, carry):
    def body(*refs):
        nw = len(w_up)
        pos_ref, u_refs, d_refs = refs[0], refs[1 : 1 + nw], refs[1 + nw : 1 + 2 * nw]
        act_ref, slope_ref, og_ref = refs[1 + 2 * nw : 4 + 2 * nw]
        rest = list(refs[4 + 2 * nw :])
        if carry is not None:
            out_in, back_in = rest[:2]
            rest = rest[2:]
        out_ref, back_ref, low_ref, bias_ref, ubuf, dbuf, usem, dsem = rest
        d_copies = load_start(p, d_refs, dbuf, dsem, pos_ref, other)
        u_copies = load_start(p, u_refs, ubuf, usem, pos_ref, other)
        wait_all(d_copies)
        og = og_ref[...]
        for b in range(2):
            grad = dot(og, dbuf[b]) * slope_ref[b].astype(F32)
            bias_ref[b] = jnp.sum(grad, axis=0, keepdims=True)
            low = grad.astype(BF16)
            low_ref[b] = low
            if b == 0:
                wait_all(u_copies)
            back = dot(low, ubuf[b], NT)
            out = dot(act_ref[b], dbuf[b], NT)
            if b == 0 and carry is not None:
                back_ref[...] = back_in[...] + back
                out_ref[...] = out_in[...] + out
            elif b == 0:
                back_ref[...] = back
                out_ref[...] = out
            else:
                back_ref[...] += back
                out_ref[...] += out

    ins = [(pos, SMEM)] + [(w, ANYS) for w in tuple(w_up) + tuple(w_down)]
    ins += [(a, VMEM) for a in (active, slope, out_grad)]
    if carry is not None:
        ins += [(a, VMEM) for a in carry]
    return call(
        body,
        [
            (sds((p.pad, p.width), F32), VMEM),
            (sds((p.pad, p.width), F32), VMEM),
            (sds((2, p.pad, p.hid), BF16), VMEM),
            (sds((2, 1, p.hid), F32), VMEM),
        ],
        ins,
        [
            pltpu.VMEM((2, p.width, p.hid), BF16),
            pltpu.VMEM((2, p.width, p.hid), BF16),
            pltpu.SemaphoreType.DMA((n_sem(p),)),
            pltpu.SemaphoreType.DMA((n_sem(p),)),
        ],
        flops=2 * 2 * p.pad * p.width * p.hid * 3,
        nbytes=8 * p.width * p.hid + 12 * p.pad * p.hid + 16 * p.pad * p.width,
        name="down",
    )


def middle_kernel(p, patches, out_grad, mixed, out_sum, back_sum, attended, gate, sel, vecs):
    gain_one, shift_one, gain_two, b_down = vecs

    def body(
        x_ref, og_ref, mix_ref, out_ref, back_ref, att_ref, gate_ref, sel_ref,
        g1_ref, s1_ref, g2_ref, bd_ref,
        tok_ref, mg_ref, br_ref, logit_ref, gg_ref, gs_ref, gb_ref, gr_ref,
    ):
        mixed = mix_ref[...]
        tok_ref[...] = (mixed + out_ref[...] + bd_ref[...])[: p.rows].astype(BF16)
        xhat, rstd = norm_parts(mixed)
        back = back_ref[...]
        gg_ref[...] = jnp.sum(back * xhat, axis=0, keepdims=True)
        gs_ref[...] = jnp.sum(back, axis=0, keepdims=True)
        mg = og_ref[...].astype(F32) + norm_back(back * g2_ref[...], xhat, rstd)
        mg_ref[...] = mg
        gate, sel = gate_ref[...], sel_ref[...]
        branch = (gate * sel) * mg
        gb_ref[...] = jnp.sum(branch, axis=0, keepdims=True)
        br_ref[...] = branch.astype(BF16)
        logit = sel * jnp.sum(mg * att_ref[...], axis=-1, keepdims=True) * gate * (1.0 - gate)
        logit_ref[...] = logit
        first, _ = norm_parts(x_ref[...].astype(F32))
        normed = first * g1_ref[...] + s1_ref[...]
        gr_ref[...] = jnp.sum(normed * logit, axis=0, keepdims=True)

    vec = (sds((1, p.width), F32), VMEM)
    return call(
        body,
        [
            (sds((p.rows, p.width), BF16), VMEM),
            (sds((p.pad, p.width), F32), VMEM),
            (sds((p.pad, p.width), BF16), VMEM),
            (sds((p.pad, 1), F32), VMEM),
            vec, vec, vec, vec,
        ],
        [
            (a, VMEM)
            for a in (
                patches, out_grad, mixed, out_sum, back_sum, attended, gate, sel,
                gain_one, shift_one, gain_two, b_down,
            )
        ],
        flops=p.pad * p.width * 30,
        nbytes=p.pad * p.width * 28,
        name="middle",
    )


def attention_backward(p, pos, weights, other, branch, rows_low, qkv, probs, ctx, received, carry):
    win, pad, lh, hd, cols = p.win, p.pad, p.local_heads, p.hd, p.cols

    def body(*refs):
        nw = len(weights)
        pos_ref, w_refs = refs[0], refs[1 : 1 + nw]
        br_ref, low_ref, qkv_ref, prob_ref, ctx_ref = refs[1 + nw : 6 + nw]
        rest = list(refs[6 + nw :])
        nr = len(received) if received is not None else 0
        got_refs, rest = rest[:nr], rest[nr:]
        if carry is not None:
            carry_ref, rest = rest[0], rest[1:]
        no = len(piece_shapes(p))
        out_refs, rest = rest[:no], rest[no:]
        n1_ref, bias_ref, wbuf, gbuf, gq, dc, wsem, sem = rest[:8]
        loads = load_start(p, w_refs, wbuf, wsem, pos_ref, other)
        if nr:
            rbuf, rsem = rest[8:]
            got = load_start(p, got_refs, rbuf, rsem, pos_ref, other)
        wait_all(loads)
        branch_low, low = br_ref[...], low_ref[...]
        total = None
        for b in range(2):
            dc[...] = dot(branch_low, wbuf[b, :, : p.cw]).astype(BF16)
            gq[...] = jnp.zeros((pad, p.nq), F32)
            for img in range(p.images):
                first = p.base[img]
                here = slice(first, first + win)
                dqs, dks, dvs = [], [], []
                for j in range(lh):
                    qs = p.lo + hd * j
                    q = qkv_ref[b, here, qs : qs + hd]
                    k = qkv_ref[b, here, qs + cols : qs + cols + hd]
                    v = qkv_ref[b, here, qs + 2 * cols : qs + 2 * cols + hd]
                    d = dc[here, hd * j : hd * j + hd]
                    prob = prob_ref[(b * p.images + img) * lh + j]
                    soft = prob.astype(F32)
                    pg = dot(d, v, NT)
                    row = jnp.sum(soft * pg, axis=-1, keepdims=True)
                    s = (soft * (pg - row) * p.scale).astype(BF16)
                    dqs.append(dot(s, k))
                    dks.append(dot(s, q, TN))
                    dvs.append(dot(prob, d, TN))
                lead = [jnp.zeros((win, p.lo), F32)] if p.lo else []
                gq[here, :] += jnp.concatenate(lead + dqs + dks + dvs, axis=1)
            full = gq[...]
            bias_ref[b] = jnp.sum(full, axis=0, keepdims=True)
            gl = full.astype(BF16)
            part = dot(gl, wbuf[b, :, p.off :], NT)
            total = part if total is None else total + part
            g_out = dot(branch_low, ctx_ref[b], TN)
            g_qkv = dot(low, gl, TN)
            g = jnp.concatenate(
                [
                    g_out[:, : p.off],
                    g_out[:, p.off : p.cw] + g_qkv[:, : p.cw - p.off],
                    g_qkv[:, p.cw - p.off :],
                ],
                axis=1,
            )
            if nr:
                if b == 0:
                    wait_all(got)
                g = g + rbuf[b].astype(F32)
            gbuf[b] = g.astype(BF16)
        if carry is not None:
            total = total + carry_ref[...]
        n1_ref[...] = total
        wait_all(store_start(p, gbuf, out_refs, sem, pos_ref, other))

    ins = [(pos, SMEM)] + [(w, ANYS) for w in weights]
    ins += [(a, VMEM) for a in (branch, rows_low, qkv, probs, ctx)]
    ins += [(r, ANYS) for r in received or ()]
    if carry is not None:
        ins.append((carry, VMEM))
    scratch = [
        pltpu.VMEM((2, p.width, 4 * cols), BF16),
        pltpu.VMEM((2, p.width, 4 * cols), BF16),
        pltpu.VMEM((pad, p.nq), F32),
        pltpu.VMEM((pad, p.cw), BF16),
        pltpu.SemaphoreType.DMA((n_sem(p),)),
        pltpu.SemaphoreType.DMA((n_sem(p),)),
    ]
    if received is not None:
        scratch += [
            pltpu.VMEM((2, p.width, 4 * cols), BF16),
            pltpu.SemaphoreType.DMA((n_sem(p),)),
        ]
    return call(
        body,
        [(s, ANYS) for s in piece_shapes(p)]
        + [(sds((pad, p.width), F32), VMEM), (sds((2, 1, p.nq), F32), VMEM)],
        ins,
        scratch,
        flops=2 * 2 * pad * p.width * 2 * (p.nq + p.cw) + 2 * p.images * lh * win * win * hd * 8,
        nbytes=12 * p.width * p.width + pad * p.width * 20,
        name="attn_bwd",
    )


def exit_kernel(p, patches, back, logit, router, gain_one, mixed_grad):
    def body(x_ref, n_ref, l_ref, r_ref, g_ref, mg_ref, out_ref, gg_ref, gs_ref):
        xhat, rstd = norm_parts(x_ref[...].astype(F32))
        grad = n_ref[...] + l_ref[...] * r_ref[...]
        gg_ref[...] = jnp.sum(grad * xhat, axis=0, keepdims=True)
        gs_ref[...] = jnp.sum(grad, axis=0, keepdims=True)
        total = mg_ref[...] + norm_back(grad * g_ref[...], xhat, rstd)
        out_ref[...] = total[: p.rows].astype(BF16)

    vec = (sds((1, p.width), F32), VMEM)
    return call(
        body,
        [(sds((p.rows, p.width), BF16), VMEM), vec, vec],
        [(a, VMEM) for a in (patches, back, logit, router, gain_one, mixed_grad)],
        flops=p.pad * p.width * 20,
        nbytes=p.pad * p.width * 12,
        name="exit",
    )


def flat(z, x, y, c):
    return ((z * 2 + x) * 2 + y) * 2 + c


def table(move):
    pairs = []
    for z in range(4):
        for x in range(2):
            for y in range(2):
                for c in range(2):
                    pairs.append((flat(z, x, y, c), flat(*move(z, x, y, c))))
    return pairs


def send(v, move):
    return lax.ppermute(v, ("dp", "head"), table(move))


def along_z(shift):
    return lambda z, x, y, c: ((z + shift) % 4, x, y, c)


def near(z, x, y, c):
    return (z, x ^ 1, y, c) if c == 0 else (z, x, y ^ 1, c)


def far(z, x, y, c):
    return (z, x, y ^ 1, c) if c == 0 else (z, x ^ 1, y, c)


def core(z, x, y, c):
    return (z, x, y, c ^ 1)


def add(a, b):
    return (a.astype(F32) + b.astype(F32)).astype(BF16)


def gather_pieces(p, shard):
    if not p.fast:
        full = lax.all_gather(lax.all_gather(shard, "dp", axis=0, tiled=True), "head", axis=0)
        return [(full[2 * i : 2 * i + 2],) for i in range(p.pairs)]
    own = jnp.stack([shard] + [send(shard, along_z(s)) for s in (1, 2, 3)])
    eight = jnp.stack([own, send(own, near)])
    rest = send(eight, far)
    return [(eight, rest), (send(eight, core), send(rest, core))]


def scatter_pieces(p, grads):
    if not p.fast:
        stacked = jnp.concatenate(grads, axis=0)
        part = lax.psum_scatter(stacked, "head", scatter_dimension=0, tiled=False)
        return lax.psum_scatter(part, "dp", scatter_dimension=0, tiled=True).astype(F32)
    keep, away = grads
    got = send(away, far)
    other = add(keep[1], got[1])
    mine = keep[0]
    got2 = send(other, near)
    pieces = [add(add(mine[s], got[0, s]), got2[s]) for s in range(4)]
    total = pieces[0].astype(F32)
    for s in (1, 2, 3):
        total = total + send(pieces[s], along_z(-s)).astype(F32)
    return total


def gather_head(p, vector):
    if not p.fast:
        return lax.all_gather(vector, "head", axis=0)
    pair = jnp.stack([vector, send(vector, lambda z, x, y, c: (z, x, y ^ 1, c))])
    return jnp.concatenate([pair, send(pair, core)], axis=0)


def sum_vectors(p, common, owned):
    n = common.shape[0]
    if not p.fast:
        total = lax.psum(common, ("dp", "head"))
        mine = lax.psum_scatter(owned, "head", scatter_dimension=0, tiled=False)
        return total, lax.psum(mine, "dp")
    got = send(jnp.concatenate([common, owned[2], owned[3]]), core)
    m = owned.shape[1]
    vec = jnp.concatenate([common, owned[0], owned[1]]) + got
    keep = vec[: n + m]
    got = send(jnp.concatenate([vec[:n], vec[n + m :]]), lambda z, x, y, c: (z, x, y ^ 1, c))
    keep = keep + got
    keep = keep + send(keep, lambda z, x, y, c: (z, x ^ 1, y, c))
    keep = keep + send(keep, lambda z, x, y, c: (z ^ 1, x, y, c))
    keep = keep + send(keep, lambda z, x, y, c: (z ^ 2, x, y, c))
    return keep[:n], keep[n:]


def on_device(
    patches, selected, out_grad, gain_one, shift_one, router_w, w_query, b_query, w_key, w_value,
    b_value, w_out, b_out, gain_two, shift_two, w_up, b_up, w_down, b_down,
):
    images, seq = selected.shape
    rows, width = patches.shape
    dp, head = lax.axis_size("dp"), lax.axis_size("head")
    p = Plan(rows, seq, images, width, b_up.shape[0] * head, dp, head)
    cols, hid = p.cols, p.hid

    dp_pos, head_pos = lax.axis_index("dp"), lax.axis_index("head")
    pos = jnp.stack([dp_pos // 2, dp_pos % 2, head_pos % 2]).astype(jnp.int32)

    attn_shard = jnp.concatenate([w_out.T, w_query, w_key, w_value], axis=1)
    attn_w = gather_pieces(p, attn_shard)
    up_w = gather_pieces(p, w_up)
    down_w = gather_pieces(p, w_down.T)
    biases = gather_head(p, jnp.concatenate([b_query, b_value, b_up])).astype(F32)
    zeros = jnp.zeros((head, cols), F32)
    qkv_bias = jnp.concatenate(
        [zeros[:, : p.lo], biases[:, :cols], zeros, biases[:, cols : 2 * cols]], axis=1
    )[:, None, :]
    up_bias = biases[:, 2 * cols :][:, None, :]

    def row(v):
        return v.astype(F32)[None, :]

    more = p.pad - rows
    x_pad = jnp.pad(patches, ((0, more), (0, 0)))
    og_pad = jnp.pad(out_grad, ((0, more), (0, 0)))
    sel = selected.astype(F32)
    sel_col = jnp.pad(sel.reshape(rows, 1), ((0, more), (0, 0)))
    key_mask = jnp.stack(
        [
            jnp.pad(sel[i], (seq * i - p.base[i], p.win - seq - (seq * i - p.base[i])))
            for i in range(images)
        ]
    )[:, None, :]
    gain_one, shift_one, gain_two, shift_two = map(row, (gain_one, shift_one, gain_two, shift_two))
    router, b_out, b_down = row(router_w), row(b_out), row(b_down)

    rows_low, gate, g_down_bias = entry_kernel(p, x_pad, og_pad, gain_one, shift_one, router)
    sel_gate = gate * sel_col

    qkvs, probs, ctxs, carry = [], [], [], None
    for i in range(p.pairs):
        tail = (x_pad, sel_gate, b_out, gain_two, shift_two) if i == p.pairs - 1 else None
        got = attention_forward(
            p, pos, attn_w[i], i, rows_low, qkv_bias[2 * i : 2 * i + 2], key_mask, carry, tail
        )
        qkvs.append(got[0])
        probs.append(got[1])
        ctxs.append(got[2])
        carry = got[3]
    attended, mixed, mlp_in = got[3], got[4], got[5]

    acts, slopes = [], []
    for i in range(p.pairs):
        act, slope = up_kernel(p, pos, up_w[i], i, mlp_in, up_bias[2 * i : 2 * i + 2])
        acts.append(act)
        slopes.append(slope)

    def reduced(lhs, rhs, name):
        if not p.fast:
            blocks = [weight_grad(p, pos, 0, lhs, r, None, name)[0] for r in rhs]
            return scatter_pieces(p, blocks)
        other = weight_grad(p, pos, 1, lhs, rhs[1], None, name)
        got = [send(o, core) for o in other]
        return scatter_pieces(p, weight_grad(p, pos, 0, lhs, rhs[0], got, name))

    grad_down = reduced(og_pad, acts, "grad_down")

    carry, lows, up_sums = None, [], []
    for i in range(p.pairs):
        got = down_kernel(p, pos, up_w[i], down_w[i], i, acts[i], slopes[i], og_pad, carry)
        carry = (got[0], got[1])
        lows.append(got[2])
        up_sums.append(got[3][:, 0])
    grad_up = reduced(mlp_in, lows, "grad_up")

    tokens, mixed_grad, branch, logit, g_gain2, g_shift2, g_out_bias, g_router = middle_kernel(
        p, x_pad, og_pad, mixed, carry[0], carry[1], attended, gate, sel_col,
        (gain_one, shift_one, gain_two, b_down),
    )

    carry, blocks, sums, received = None, [None] * p.pairs, [None] * p.pairs, None
    for i in reversed(range(p.pairs)):
        got = attention_backward(
            p, pos, attn_w[i], i if p.fast else 0, branch, rows_low, qkvs[i], probs[i], ctxs[i],
            received, carry,
        )
        pieces, carry, sums[i] = got[:-2], got[-2], got[-1][:, 0]
        blocks[i] = pieces
        if p.fast and i == 1:
            received = [send(o, core) for o in pieces]
    grad_attn = scatter_pieces(p, blocks[0] if p.fast else [b[0] for b in blocks])
    grad_patches, g_gain1, g_shift1 = exit_kernel(
        p, x_pad, carry, logit, router, gain_one, mixed_grad
    )

    qkv_sums = jnp.concatenate(sums, axis=0)
    owned = jnp.concatenate(
        [
            qkv_sums[:, p.lo : p.lo + cols],
            qkv_sums[:, p.lo + 2 * cols :],
            jnp.concatenate(up_sums, axis=0),
        ],
        axis=1,
    )
    common = jnp.concatenate(
        [g_gain1, g_shift1, g_router, g_out_bias, g_gain2, g_shift2, g_down_bias], axis=1
    )[0]
    common, owned = sum_vectors(p, common, owned)
    vecs = [common[i * width : (i + 1) * width] for i in range(7)]
    return (
        tokens,
        grad_patches,
        vecs[0],
        vecs[1],
        vecs[2],
        grad_attn[:, cols : 2 * cols],
        owned[:cols],
        grad_attn[:, 2 * cols : 3 * cols],
        grad_attn[:, 3 * cols :],
        owned[cols : 2 * cols],
        grad_attn[:, :cols].T,
        vecs[3],
        vecs[4],
        vecs[5],
        grad_up,
        owned[2 * cols :],
        grad_down.T,
        vecs[6],
    )


def solution(mesh):
    rows, rep = P(("dp", "head"), None), P()
    split, side, turned = P("dp", "head"), P("head"), P("head", "dp")
    return jax.shard_map(
        on_device,
        mesh=mesh,
        in_specs=(
            rows, rows, rows, rep, rep, rep, split, side, split, split, side, turned, rep, rep,
            rep, split, side, turned, rep,
        ),
        out_specs=(
            rows, rows, rep, rep, rep, split, side, split, split, side, turned, rep, rep, rep,
            split, side, turned, rep,
        ),
        check_vma=False,
    )
```

```python
import math

import jax
import jax.numpy as jnp
from jax import lax
from jax.experimental import pallas as pl
from jax.experimental.pallas import tpu as pltpu
from jax.sharding import PartitionSpec as P

HEADS = 12
EPS = 1e-06
F32 = jnp.float32
BF16 = jnp.bfloat16
VMEM = pl.BlockSpec(memory_space=pltpu.VMEM)
SMEM = pl.BlockSpec(memory_space=pltpu.SMEM)
WEIGHT = 1.0e10
LIMIT = 20 * 1024 * 1024
INV_SQRT2 = 0.7071067811865476
INV_SQRT2PI = 0.3989422804014327

NN = (((1,), (0,)), ((), ()))
NT = (((1,), (1,)), ((), ()))
TN = (((0,), (0,)), ((), ()))


def dot(a, b, dims=NN):
    return lax.dot_general(a, b, dims, preferred_element_type=F32)


def sds(shape, dtype):
    return jax.ShapeDtypeStruct(shape, dtype)


def call(body, outs, ins, scratch=(), micros=1.0, name=None):
    return pl.pallas_call(
        body,
        out_shape=[o for o, _ in outs],
        in_specs=[s for _, s in ins],
        out_specs=[s for _, s in outs],
        scratch_shapes=list(scratch),
        compiler_params=pltpu.CompilerParams(vmem_limit_bytes=LIMIT),
        cost_estimate=pl.CostEstimate(
            flops=int(micros * WEIGHT), bytes_accessed=0, transcendentals=0
        ),
        name=name,
    )(*[a for a, _ in ins])


def norm_parts(v):
    center = v - jnp.mean(v, axis=-1, keepdims=True)
    spread = jnp.mean(center * center, axis=-1, keepdims=True)
    rstd = lax.rsqrt(spread + EPS)
    return center * rstd, rstd


def norm_back(u, xhat, rstd):
    return rstd * (
        u
        - jnp.mean(u, axis=-1, keepdims=True)
        - xhat * jnp.mean(u * xhat, axis=-1, keepdims=True)
    )


class Plan:
    def __init__(self, rows, seq, images, width, hidden, dp, head):
        self.rows, self.seq, self.images, self.width = rows, seq, images, width
        self.dp, self.head = dp, head
        self.pairs = head // 2
        self.cols = width // head
        self.hid = hidden // head
        self.hd = width // HEADS
        self.local_heads = HEADS // head
        self.piece = width // dp
        self.fast = dp == 8 and head == 4 and self.piece % 16 == 0
        self.base = [seq * i // 16 * 16 for i in range(images)]
        self.win = max(-(-(seq * (i + 1) - self.base[i]) // 16) * 16 for i in range(images))
        self.pad = self.base[-1] + self.win
        self.off = self.cols // 128 * 128
        self.lo = self.cols - self.off
        self.nq = 4 * self.cols - self.off
        self.cw = -(-self.cols // 128) * 128
        self.scale = 1.0 / math.sqrt(self.hd)


def source_rows(p, pos_ref, zz, xx):
    z, x = pos_ref[0], pos_ref[1]
    part = ((z - zz) & 3) * 2 + (x ^ xx)
    return pl.multiple_of(part * p.piece, p.piece)


def piece_list(p, pos_ref, other):
    core = pos_ref[2] ^ other
    found = []
    for b3 in range(2):
        for b2 in range(2):
            yy = jnp.where(core == 0, b3, b2)
            xx = jnp.where(core == 0, b2, b3)
            for zz in range(4):
                found.append((b3, b2, zz, yy, source_rows(p, pos_ref, zz, xx)))
    return found


def gather_blocks(p, refs, buf, pos_ref, other):
    if not p.fast:
        buf[...] = refs[0][...]
        return
    for b3, b2, zz, yy, row in piece_list(p, pos_ref, other):
        buf[yy, pl.ds(row, p.piece), :] = refs[b3][b2, zz]


def spread_blocks(p, buf, refs, pos_ref, other, received=None):
    if not p.fast:
        refs[0][...] = buf[...].astype(BF16)
        return
    for b3, b2, zz, yy, row in piece_list(p, pos_ref, other):
        part = buf[yy, pl.ds(row, p.piece), :]
        if received is not None:
            part = part + received[b3][b2, zz].astype(F32)
        refs[b3][b2, zz] = part.astype(BF16)


def piece_shapes(p):
    if p.fast:
        return [sds((2, 4, p.piece, p.width), BF16)] * 2
    return [sds((2, p.width, p.width), BF16)]


def entry_kernel(p, patches, out_grad, gain_one, shift_one, router):
    def body(x_ref, og_ref, g_ref, s_ref, r_ref, low_ref, gate_ref, down_ref):
        xhat, _ = norm_parts(x_ref[...].astype(F32))
        normed = xhat * g_ref[...] + s_ref[...]
        low_ref[...] = normed.astype(BF16)
        logit = jnp.sum(normed * r_ref[...], axis=-1, keepdims=True)
        gate_ref[...] = 1.0 / (1.0 + jnp.exp(-logit))
        down_ref[...] = jnp.sum(og_ref[...].astype(F32), axis=0, keepdims=True)

    return call(
        body,
        [
            (sds((p.pad, p.width), BF16), VMEM),
            (sds((p.pad, 1), F32), VMEM),
            (sds((1, p.width), F32), VMEM),
        ],
        [(a, VMEM) for a in (patches, out_grad, gain_one, shift_one, router)],
        micros=0.7,
        name="entry",
    )


def attention_forward(p, pos, weights, other, rows_low, bias, key_mask, carry, tail):
    last = tail is not None
    win, pad, lh, hd = p.win, p.pad, p.local_heads, p.hd

    def body(*refs):
        nw = len(weights)
        pos_ref, w_refs = refs[0], refs[1 : 1 + nw]
        rest = list(refs[1 + nw :])
        low_ref, bias_ref, mask_ref = rest[:3]
        rest = rest[3:]
        carry_ref = None
        if carry is not None:
            carry_ref, rest = rest[0], rest[1:]
        if last:
            x_ref, sg_ref, bo_ref, g2_ref, s2_ref = rest[:5]
            rest = rest[5:]
            qkv_ref, prob_ref, ctx_ref, att_ref, mixed_ref, in_ref = rest[:6]
            rest = rest[6:]
        else:
            qkv_ref, prob_ref, ctx_ref, att_ref = rest[:4]
            rest = rest[4:]
        wbuf, ctx = rest
        gather_blocks(p, w_refs, wbuf, pos_ref, other)
        low = low_ref[...]
        total = None
        for b in range(2):
            qkv = dot(low, wbuf[b, :, p.off :]) + bias_ref[b]
            qkv_ref[b] = qkv.astype(BF16)
            ctx[...] = jnp.zeros((pad, p.cw), F32)
            for img in range(p.images):
                first = p.base[img]
                at = lax.broadcasted_iota(jnp.int32, (win, 1), 0) + first
                valid = (at >= p.seq * img) & (at < p.seq * (img + 1))
                seen = mask_ref[img] > 0.0
                got = []
                for j in range(lh):
                    qs = p.lo + hd * j
                    q = qkv_ref[b, first : first + win, qs : qs + hd]
                    k = qkv_ref[b, first : first + win, qs + p.cols : qs + p.cols + hd]
                    v = qkv_ref[b, first : first + win, qs + 2 * p.cols : qs + 2 * p.cols + hd]
                    s = dot(q, k, NT) * p.scale
                    s = jnp.where(seen, s, -1e30)
                    e = jnp.exp(s - jnp.max(s, axis=-1, keepdims=True))
                    prob = e * (1.0 / jnp.sum(e, axis=-1, keepdims=True))
                    prob = jnp.where(valid, prob, 0.0).astype(BF16)
                    prob_ref[(b * p.images + img) * lh + j] = prob
                    got.append(dot(prob, v))
                if p.cw > p.cols:
                    got.append(jnp.zeros((win, p.cw - p.cols), F32))
                ctx[first : first + win, :] += jnp.concatenate(got, axis=1)
            mix = ctx[...].astype(BF16)
            ctx_ref[b] = mix
            part = dot(mix, wbuf[b, :, : p.cw], NT)
            total = part if total is None else total + part
        if carry_ref is not None:
            total = total + carry_ref[...]
        if not last:
            att_ref[...] = total
            return
        attended = total + bo_ref[...]
        att_ref[...] = attended
        mixed = x_ref[...].astype(F32) + sg_ref[...] * attended
        mixed_ref[...] = mixed
        xhat, _ = norm_parts(mixed)
        in_ref[...] = (xhat * g2_ref[...] + s2_ref[...]).astype(BF16)

    ins = [(pos, SMEM)] + [(w, VMEM) for w in weights]
    ins += [(a, VMEM) for a in (rows_low, bias, key_mask)]
    if carry is not None:
        ins.append((carry, VMEM))
    if last:
        ins += [(a, VMEM) for a in tail]
    outs = [
        (sds((2, pad, p.nq), BF16), VMEM),
        (sds((2 * p.images * lh, win, win), BF16), VMEM),
        (sds((2, pad, p.cw), BF16), VMEM),
        (sds((pad, p.width), F32), VMEM),
    ]
    if last:
        outs += [(sds((pad, p.width), F32), VMEM), (sds((pad, p.width), BF16), VMEM)]
    return call(
        body,
        outs,
        ins,
        [
            pltpu.VMEM((2, p.width, 4 * p.cols), BF16),
            pltpu.VMEM((pad, p.cw), F32),
        ],
        micros=5.5,
        name="attn_fwd",
    )


def up_kernel(p, pos, weights, other, mlp_in, bias):
    def body(*refs):
        nw = len(weights)
        pos_ref, w_refs = refs[0], refs[1 : 1 + nw]
        in_ref, b_ref, act_ref, slope_ref, wbuf = refs[1 + nw :]
        gather_blocks(p, w_refs, wbuf, pos_ref, other)
        rows = in_ref[...]
        for b in range(2):
            pre = dot(rows, wbuf[b]) + b_ref[b]
            phi = 0.5 * (1.0 + lax.erf(pre * INV_SQRT2))
            act_ref[b] = (pre * phi).astype(BF16)
            slope_ref[b] = (phi + pre * (jnp.exp(-0.5 * pre * pre) * INV_SQRT2PI)).astype(BF16)

    return call(
        body,
        [(sds((2, p.pad, p.hid), BF16), VMEM)] * 2,
        [(pos, SMEM)] + [(w, VMEM) for w in weights] + [(mlp_in, VMEM), (bias, VMEM)],
        [pltpu.VMEM((2, p.width, p.hid), BF16)],
        micros=2.5,
        name="up",
    )


def weight_grad(p, pos, other, lhs, rhs, received, name):
    def body(*refs):
        pos_ref, l_ref, r_ref = refs[:3]
        rest = list(refs[3:])
        nr = len(received) if received is not None else 0
        got_refs, rest = rest[:nr], rest[nr:]
        no = len(piece_shapes(p))
        out_refs, rest = rest[:no], rest[no:]
        (gbuf,) = rest
        left = l_ref[...]
        for b in range(2):
            gbuf[b] = dot(left, r_ref[b], TN)
        spread_blocks(p, gbuf, out_refs, pos_ref, other, got_refs if nr else None)

    return call(
        body,
        [(s, VMEM) for s in piece_shapes(p)],
        [(pos, SMEM), (lhs, VMEM), (rhs, VMEM)] + [(r, VMEM) for r in received or ()],
        [pltpu.VMEM((2, p.width, p.hid), F32)],
        micros=2.3,
        name=name,
    )


def down_kernel(p, pos, w_up, w_down, other, active, slope, out_grad, carry):
    def body(*refs):
        nw = len(w_up)
        pos_ref, u_refs, d_refs = refs[0], refs[1 : 1 + nw], refs[1 + nw : 1 + 2 * nw]
        act_ref, slope_ref, og_ref = refs[1 + 2 * nw : 4 + 2 * nw]
        rest = list(refs[4 + 2 * nw :])
        if carry is not None:
            out_in, back_in = rest[:2]
            rest = rest[2:]
        out_ref, back_ref, low_ref, bias_ref, ubuf, dbuf = rest
        gather_blocks(p, d_refs, dbuf, pos_ref, other)
        gather_blocks(p, u_refs, ubuf, pos_ref, other)
        og = og_ref[...]
        for b in range(2):
            grad = dot(og, dbuf[b]) * slope_ref[b].astype(F32)
            bias_ref[b] = jnp.sum(grad, axis=0, keepdims=True)
            low = grad.astype(BF16)
            low_ref[b] = low
            back = dot(low, ubuf[b], NT)
            out = dot(act_ref[b], dbuf[b], NT)
            if b == 0 and carry is not None:
                back_ref[...] = back_in[...] + back
                out_ref[...] = out_in[...] + out
            elif b == 0:
                back_ref[...] = back
                out_ref[...] = out
            else:
                back_ref[...] += back
                out_ref[...] += out

    ins = [(pos, SMEM)] + [(w, VMEM) for w in tuple(w_up) + tuple(w_down)]
    ins += [(a, VMEM) for a in (active, slope, out_grad)]
    if carry is not None:
        ins += [(a, VMEM) for a in carry]
    return call(
        body,
        [
            (sds((p.pad, p.width), F32), VMEM),
            (sds((p.pad, p.width), F32), VMEM),
            (sds((2, p.pad, p.hid), BF16), VMEM),
            (sds((2, 1, p.hid), F32), VMEM),
        ],
        ins,
        [
            pltpu.VMEM((2, p.width, p.hid), BF16),
            pltpu.VMEM((2, p.width, p.hid), BF16),
        ],
        micros=5.0,
        name="down",
    )


def middle_kernel(p, patches, out_grad, mixed, out_sum, back_sum, attended, gate, sel, vecs):
    gain_one, shift_one, gain_two, b_down = vecs

    def body(
        x_ref, og_ref, mix_ref, out_ref, back_ref, att_ref, gate_ref, sel_ref,
        g1_ref, s1_ref, g2_ref, bd_ref,
        tok_ref, mg_ref, br_ref, logit_ref, gg_ref, gs_ref, gb_ref, gr_ref,
    ):
        mixed = mix_ref[...]
        tok_ref[...] = (mixed + out_ref[...] + bd_ref[...])[: p.rows].astype(BF16)
        xhat, rstd = norm_parts(mixed)
        back = back_ref[...]
        gg_ref[...] = jnp.sum(back * xhat, axis=0, keepdims=True)
        gs_ref[...] = jnp.sum(back, axis=0, keepdims=True)
        mg = og_ref[...].astype(F32) + norm_back(back * g2_ref[...], xhat, rstd)
        mg_ref[...] = mg
        gate, sel = gate_ref[...], sel_ref[...]
        branch = (gate * sel) * mg
        gb_ref[...] = jnp.sum(branch, axis=0, keepdims=True)
        br_ref[...] = branch.astype(BF16)
        logit = sel * jnp.sum(mg * att_ref[...], axis=-1, keepdims=True) * gate * (1.0 - gate)
        logit_ref[...] = logit
        first, _ = norm_parts(x_ref[...].astype(F32))
        normed = first * g1_ref[...] + s1_ref[...]
        gr_ref[...] = jnp.sum(normed * logit, axis=0, keepdims=True)

    vec = (sds((1, p.width), F32), VMEM)
    return call(
        body,
        [
            (sds((p.rows, p.width), BF16), VMEM),
            (sds((p.pad, p.width), F32), VMEM),
            (sds((p.pad, p.width), BF16), VMEM),
            (sds((p.pad, 1), F32), VMEM),
            vec, vec, vec, vec,
        ],
        [
            (a, VMEM)
            for a in (
                patches, out_grad, mixed, out_sum, back_sum, attended, gate, sel,
                gain_one, shift_one, gain_two, b_down,
            )
        ],
        micros=2.6,
        name="middle",
    )


def attention_backward(p, pos, weights, other, branch, qkv, probs, carry):
    win, pad, lh, hd, cols = p.win, p.pad, p.local_heads, p.hd, p.cols

    def body(*refs):
        nw = len(weights)
        pos_ref, w_refs = refs[0], refs[1 : 1 + nw]
        br_ref, qkv_ref, prob_ref = refs[1 + nw : 4 + nw]
        rest = list(refs[4 + nw :])
        if carry is not None:
            carry_ref, rest = rest[0], rest[1:]
        low_ref, n1_ref, bias_ref, wbuf, gq, dc = rest
        gather_blocks(p, w_refs, wbuf, pos_ref, other)
        branch_low = br_ref[...]
        total = None
        for b in range(2):
            dc[...] = dot(branch_low, wbuf[b, :, : p.cw]).astype(BF16)
            gq[...] = jnp.zeros((pad, p.nq), F32)
            for img in range(p.images):
                first = p.base[img]
                here = slice(first, first + win)
                dqs, dks, dvs = [], [], []
                for j in range(lh):
                    qs = p.lo + hd * j
                    q = qkv_ref[b, here, qs : qs + hd]
                    k = qkv_ref[b, here, qs + cols : qs + cols + hd]
                    v = qkv_ref[b, here, qs + 2 * cols : qs + 2 * cols + hd]
                    d = dc[here, hd * j : hd * j + hd]
                    prob = prob_ref[(b * p.images + img) * lh + j]
                    soft = prob.astype(F32)
                    pg = dot(d, v, NT)
                    row = jnp.sum(soft * pg, axis=-1, keepdims=True)
                    s = (soft * (pg - row) * p.scale).astype(BF16)
                    dqs.append(dot(s, k))
                    dks.append(dot(s, q, TN))
                    dvs.append(dot(prob, d, TN))
                lead = [jnp.zeros((win, p.lo), F32)] if p.lo else []
                gq[here, :] += jnp.concatenate(lead + dqs + dks + dvs, axis=1)
            full = gq[...]
            bias_ref[b] = jnp.sum(full, axis=0, keepdims=True)
            gl = full.astype(BF16)
            low_ref[b] = gl
            part = dot(gl, wbuf[b, :, p.off :], NT)
            total = part if total is None else total + part
        if carry is not None:
            total = total + carry_ref[...]
        n1_ref[...] = total

    ins = [(pos, SMEM)] + [(w, VMEM) for w in weights]
    ins += [(a, VMEM) for a in (branch, qkv, probs)]
    if carry is not None:
        ins.append((carry, VMEM))
    return call(
        body,
        [
            (sds((2, pad, p.nq), BF16), VMEM),
            (sds((pad, p.width), F32), VMEM),
            (sds((2, 1, p.nq), F32), VMEM),
        ],
        ins,
        [
            pltpu.VMEM((2, p.width, 4 * cols), BF16),
            pltpu.VMEM((pad, p.nq), F32),
            pltpu.VMEM((pad, p.cw), BF16),
        ],
        micros=7.5,
        name="attn_bwd",
    )


def attention_grad(p, pos, other, branch, rows_low, ctx, low, received):
    def body(*refs):
        pos_ref, br_ref, rows_ref, ctx_ref, low_ref = refs[:5]
        rest = list(refs[5:])
        nr = len(received) if received is not None else 0
        got_refs, rest = rest[:nr], rest[nr:]
        out_refs, gbuf = rest[:-1], rest[-1]
        for b in range(2):
            g_out = dot(br_ref[...], ctx_ref[b], TN)
            g_qkv = dot(rows_ref[...], low_ref[b], TN)
            gbuf[b, :, : p.off] = g_out[:, : p.off]
            gbuf[b, :, p.off : p.cw] = g_out[:, p.off :] + g_qkv[:, : p.cw - p.off]
            gbuf[b, :, p.cw :] = g_qkv[:, p.cw - p.off :]
        spread_blocks(p, gbuf, out_refs, pos_ref, other, got_refs if nr else None)

    return call(
        body,
        [(s, VMEM) for s in piece_shapes(p)],
        [(pos, SMEM)]
        + [(a, VMEM) for a in (branch, rows_low, ctx, low)]
        + [(r, VMEM) for r in received or ()],
        [pltpu.VMEM((2, p.width, 4 * p.cols), F32)],
        micros=3.0,
        name="attn_grad",
    )


def exit_kernel(p, patches, back, logit, router, gain_one, mixed_grad):
    def body(x_ref, n_ref, l_ref, r_ref, g_ref, mg_ref, out_ref, gg_ref, gs_ref):
        xhat, rstd = norm_parts(x_ref[...].astype(F32))
        grad = n_ref[...] + l_ref[...] * r_ref[...]
        gg_ref[...] = jnp.sum(grad * xhat, axis=0, keepdims=True)
        gs_ref[...] = jnp.sum(grad, axis=0, keepdims=True)
        total = mg_ref[...] + norm_back(grad * g_ref[...], xhat, rstd)
        out_ref[...] = total[: p.rows].astype(BF16)

    vec = (sds((1, p.width), F32), VMEM)
    return call(
        body,
        [(sds((p.rows, p.width), BF16), VMEM), vec, vec],
        [(a, VMEM) for a in (patches, back, logit, router, gain_one, mixed_grad)],
        micros=2.0,
        name="exit",
    )


def flat(z, x, y, c):
    return ((z * 2 + x) * 2 + y) * 2 + c


def table(move):
    pairs = []
    for z in range(4):
        for x in range(2):
            for y in range(2):
                for c in range(2):
                    pairs.append((flat(z, x, y, c), flat(*move(z, x, y, c))))
    return pairs


def send(v, move):
    return lax.ppermute(v, ("dp", "head"), table(move))


def along_z(shift):
    return lambda z, x, y, c: ((z + shift) % 4, x, y, c)


def near(z, x, y, c):
    return (z, x ^ 1, y, c) if c == 0 else (z, x, y ^ 1, c)


def far(z, x, y, c):
    return (z, x, y ^ 1, c) if c == 0 else (z, x ^ 1, y, c)


def core(z, x, y, c):
    return (z, x, y, c ^ 1)


def after(v, *others):
    return lax.optimization_barrier((v,) + others)[0]


def add(a, b):
    return (a.astype(F32) + b.astype(F32)).astype(BF16)


def gather_whole(p, shard):
    full = lax.all_gather(lax.all_gather(shard, "dp", axis=0, tiled=True), "head", axis=0)
    return [(full[2 * i : 2 * i + 2],) for i in range(p.pairs)]


def own_pieces(shard):
    return jnp.stack([shard] + [send(shard, along_z(s)) for s in (1, 2, 3)])


def both_cores(eight, rest, *others):
    eight_out, rest_out = after(eight, *others), after(rest, *others)
    return [(eight, rest), (send(eight_out, core), send(rest_out, core))]


def scatter_whole(p, grads):
    stacked = jnp.concatenate(grads, axis=0)
    part = lax.psum_scatter(stacked, "head", scatter_dimension=0, tiled=False)
    return lax.psum_scatter(part, "dp", scatter_dimension=0, tiled=True).astype(F32)


class Scatter:
    def __init__(self, keep, away):
        self.keep, self.away = keep, away

    def first(self):
        got = send(self.away, far)
        self.mine = add(self.keep[0], got[0])
        self.other = add(self.keep[1], got[1])

    def second(self):
        got = send(self.other, near)
        self.pieces = [add(self.mine[s], got[s]) for s in range(4)]

    def third(self, *others):
        got = [after(send(self.pieces[s], along_z(-s)), *others) for s in (1, 2, 3)]
        return sum([g.astype(F32) for g in got], self.pieces[0].astype(F32))


def gather_head(p, vector):
    if not p.fast:
        return lax.all_gather(vector, "head", axis=0)
    pair = jnp.stack([vector, send(vector, lambda z, x, y, c: (z, x, y ^ 1, c))])
    return jnp.concatenate([pair, send(pair, core)], axis=0)


def sum_vectors(p, common, owned):
    n = common.shape[0]
    if not p.fast:
        total = lax.psum(common, ("dp", "head"))
        mine = lax.psum_scatter(owned, "head", scatter_dimension=0, tiled=False)
        return total, lax.psum(mine, "dp")
    got = send(jnp.concatenate([common, owned[2], owned[3]]), core)
    m = owned.shape[1]
    vec = jnp.concatenate([common, owned[0], owned[1]]) + got
    keep = vec[: n + m]
    got = send(jnp.concatenate([vec[:n], vec[n + m :]]), lambda z, x, y, c: (z, x, y ^ 1, c))
    keep = keep + got
    keep = keep + send(keep, lambda z, x, y, c: (z, x ^ 1, y, c))
    keep = keep + send(keep, lambda z, x, y, c: (z ^ 1, x, y, c))
    keep = keep + send(keep, lambda z, x, y, c: (z ^ 2, x, y, c))
    return keep[:n], keep[n:]


def on_device(
    patches, selected, out_grad, gain_one, shift_one, router_w, w_query, b_query, w_key, w_value,
    b_value, w_out, b_out, gain_two, shift_two, w_up, b_up, w_down, b_down,
):
    images, seq = selected.shape
    rows, width = patches.shape
    dp, head = lax.axis_size("dp"), lax.axis_size("head")
    p = Plan(rows, seq, images, width, b_up.shape[0] * head, dp, head)
    cols, hid = p.cols, p.hid

    dp_pos, head_pos = lax.axis_index("dp"), lax.axis_index("head")
    pos = jnp.stack([dp_pos // 2, dp_pos % 2, head_pos % 2]).astype(jnp.int32)

    attn_shard = jnp.concatenate([w_out.T, w_query, w_key, w_value], axis=1)
    bias_parts = after(jnp.concatenate([b_query, b_value, b_up]), attn_shard)
    biases = gather_head(p, bias_parts).astype(F32)
    zeros = jnp.zeros((head, cols), F32)
    qkv_bias = jnp.concatenate(
        [zeros[:, : p.lo], biases[:, :cols], zeros, biases[:, cols : 2 * cols]], axis=1
    )[:, None, :]
    up_bias = biases[:, 2 * cols :][:, None, :]

    def row(v):
        return v.astype(F32)[None, :]

    more = p.pad - rows
    x_pad = jnp.pad(patches, ((0, more), (0, 0)))
    og_pad = jnp.pad(out_grad, ((0, more), (0, 0)))
    sel = selected.astype(F32)
    sel_col = jnp.pad(sel.reshape(rows, 1), ((0, more), (0, 0)))
    key_mask = jnp.stack(
        [
            jnp.pad(sel[i], (seq * i - p.base[i], p.win - seq - (seq * i - p.base[i])))
            for i in range(images)
        ]
    )[:, None, :]
    gain_one, shift_one, gain_two, shift_two = map(row, (gain_one, shift_one, gain_two, shift_two))
    router, b_out, b_down = row(router_w), row(b_out), row(b_down)

    fast = p.fast
    if fast:
        attn_own = after(own_pieces(attn_shard), biases)
        x_in = after(x_pad, attn_own)
        rows_low, gate, g_down_bias = entry_kernel(p, x_in, og_pad, gain_one, shift_one, router)
        attn_eight = after(jnp.stack([attn_own, send(attn_own, near)]), rows_low)
        attn_rest = send(attn_eight, far)
        attn_w = both_cores(attn_eight, attn_rest)
        up_own = after(own_pieces(after(w_up, attn_own)), attn_eight)
        up_eight = after(jnp.stack([up_own, send(up_own, near)]), attn_rest)
        up_rest = send(up_eight, far)
        down_own = after(own_pieces(after(w_down.T, up_own)), up_eight)
        down_eight = jnp.stack([down_own, send(down_own, near)])
        down_rest = send(down_eight, far)
    else:
        rows_low, gate, g_down_bias = entry_kernel(p, x_pad, og_pad, gain_one, shift_one, router)
        attn_w, up_w, down_w = (gather_whole(p, v) for v in (attn_shard, w_up, w_down.T))
    sel_gate = gate * sel_col

    qkvs, probs, ctxs, carry = [], [], [], None
    for i in range(p.pairs):
        tail = (x_pad, sel_gate, b_out, gain_two, shift_two) if i == p.pairs - 1 else None
        if fast and i == 1:
            rows_low = after(rows_low, up_eight, down_own)
        got = attention_forward(
            p, pos, attn_w[i], i, rows_low, qkv_bias[2 * i : 2 * i + 2], key_mask, carry, tail
        )
        qkvs.append(got[0])
        probs.append(got[1])
        ctxs.append(got[2])
        carry = got[3]
    attended, mixed, mlp_in = got[3], got[4], got[5]

    acts, slopes = [], []
    if fast:
        up_w = both_cores(up_eight, up_rest, mlp_in)
    up_in = after(mlp_in, down_eight) if fast else mlp_in
    for i in range(p.pairs):
        act, slope = up_kernel(p, pos, up_w[i], i, up_in, up_bias[2 * i : 2 * i + 2])
        acts.append(act)
        slopes.append(slope)

    def backward(i, branch, carry):
        return attention_backward(
            p, pos, attn_w[i], i if fast else 0, branch, qkvs[i], probs[i], carry
        )

    def down(i, grad_in, carry):
        return down_kernel(p, pos, up_w[i], down_w[i], i, acts[i], slopes[i], grad_in, carry)

    def middle(back, out):
        return middle_kernel(
            p, x_pad, og_pad, mixed, out, back, attended, gate, sel_col,
            (gain_one, shift_one, gain_two, b_down),
        )

    def leave(back, logit, mixed_grad):
        return exit_kernel(p, x_pad, back, logit, router, gain_one, mixed_grad)

    if fast:
        down_w = both_cores(down_eight, down_rest, acts[1])
        gd1 = weight_grad(p, pos, 1, og_pad, acts[1], None, "grad_down")
        gd1_got = [send(o, core) for o in gd1]
        out_sum, back_sum, low0, sum0 = down(0, after(og_pad, *gd1), None)
        gd0 = weight_grad(p, pos, 0, after(og_pad, low0), acts[0], gd1_got, "grad_down")
        down_sum = Scatter(*gd0)
        out_sum, back_sum, low1, sum1 = down(1, after(og_pad, *gd0), (out_sum, back_sum))
        up_sums = [sum0[:, 0], sum1[:, 0]]
        gu1 = weight_grad(p, pos, 1, mlp_in, low1, None, "grad_up")
        gu1_got = [send(o, core) for o in gu1]
        tokens, mixed_grad, branch, logit, g_gain2, g_shift2, g_out_bias, g_router = middle(
            after(back_sum, *gu1), out_sum
        )
        gu0 = weight_grad(p, pos, 0, after(mlp_in, branch), low0, gu1_got, "grad_up")
        up_sum = Scatter(*gu0)
        down_sum.first()
        low1, carry, bias1 = backward(1, after(branch, down_sum.other, *gu0), None)
        ga1 = attention_grad(p, pos, 1, branch, rows_low, ctxs[1], low1, None)
        ga1_got = [send(o, core) for o in ga1]
        up_sum.first()
        down_sum.second()
        low0, carry, bias0 = backward(0, after(branch, up_sum.other, *ga1, *down_sum.pieces), carry)
        ga0 = attention_grad(p, pos, 0, branch, rows_low, ctxs[0], low0, ga1_got)
        attn_sum = Scatter(*ga0)
        sums = [bias0[:, 0], bias1[:, 0]]
        grad_patches, g_gain1, g_shift1 = leave(after(carry, *ga0), logit, mixed_grad)
        grad_down = down_sum.third(grad_patches)
        up_sum.second()
        attn_sum.first()
        attn_sum.second()
        grad_up = up_sum.third(grad_patches)
        grad_attn = attn_sum.third()
    else:
        carry, lows, up_sums, blocks, sums = None, [], [], [], []
        for i in range(p.pairs):
            got = down(i, og_pad, carry)
            carry = (got[0], got[1])
            lows.append(got[2])
            up_sums.append(got[3][:, 0])
        tokens, mixed_grad, branch, logit, g_gain2, g_shift2, g_out_bias, g_router = middle(
            carry[1], carry[0]
        )
        carry = None
        for i in range(p.pairs):
            low, carry, bias = backward(i, branch, carry)
            blocks += attention_grad(p, pos, 0, branch, rows_low, ctxs[i], low, None)
            sums.append(bias[:, 0])
        grad_patches, g_gain1, g_shift1 = leave(carry, logit, mixed_grad)
        grad_down, grad_up, grad_attn = (
            scatter_whole(p, g)
            for g in (
                [weight_grad(p, pos, 0, og_pad, a, None, "grad_down")[0] for a in acts],
                [weight_grad(p, pos, 0, mlp_in, v, None, "grad_up")[0] for v in lows],
                blocks,
            )
        )

    qkv_sums = jnp.concatenate(sums, axis=0)
    owned = jnp.concatenate(
        [
            qkv_sums[:, p.lo : p.lo + cols],
            qkv_sums[:, p.lo + 2 * cols :],
            jnp.concatenate(up_sums, axis=0),
        ],
        axis=1,
    )
    common = jnp.concatenate(
        [g_gain1, g_shift1, g_router, g_out_bias, g_gain2, g_shift2, g_down_bias], axis=1
    )[0]
    common, owned = sum_vectors(p, common, owned)
    vecs = [common[i * width : (i + 1) * width] for i in range(7)]
    return (
        tokens,
        grad_patches,
        vecs[0],
        vecs[1],
        vecs[2],
        grad_attn[:, cols : 2 * cols],
        owned[:cols],
        grad_attn[:, 2 * cols : 3 * cols],
        grad_attn[:, 3 * cols :],
        owned[cols : 2 * cols],
        grad_attn[:, :cols].T,
        vecs[3],
        vecs[4],
        vecs[5],
        grad_up,
        owned[2 * cols :],
        grad_down.T,
        vecs[6],
    )


def solution(mesh):
    rows, rep = P(("dp", "head"), None), P()
    split, side, turned = P("dp", "head"), P("head"), P("head", "dp")
    return jax.shard_map(
        on_device,
        mesh=mesh,
        in_specs=(
            rows, rows, rows, rep, rep, rep, split, side, split, split, side, turned, rep, rep,
            rep, split, side, turned, rep,
        ),
        out_specs=(
            rows, rows, rep, rep, rep, split, side, split, split, side, turned, rep, rep, rep,
            split, side, turned, rep,
        ),
        check_vma=False,
    )
```

```python
import math

import jax
import jax.numpy as jnp
from jax import lax
from jax.experimental import pallas as pl
from jax.experimental.pallas import tpu as pltpu
from jax.sharding import PartitionSpec as P

HEADS = 12
EPS = 1e-06
F32 = jnp.float32
BF16 = jnp.bfloat16
VMEM = pl.BlockSpec(memory_space=pltpu.VMEM)
SMEM = pl.BlockSpec(memory_space=pltpu.SMEM)
EXIT = 2.0
WEIGHT = 4.0e9
LIMIT = 20 * 1024 * 1024
INV_SQRT2 = 0.7071067811865476
INV_SQRT2PI = 0.3989422804014327

NN = (((1,), (0,)), ((), ()))
NT = (((1,), (1,)), ((), ()))
TN = (((0,), (0,)), ((), ()))


def dot(a, b, dims=NN):
    return lax.dot_general(a, b, dims, preferred_element_type=F32)


def sds(shape, dtype):
    return jax.ShapeDtypeStruct(shape, dtype)


def call(body, outs, ins, scratch=(), micros=1.0, name=None):
    return pl.pallas_call(
        body,
        out_shape=[o for o, _ in outs],
        in_specs=[s for _, s in ins],
        out_specs=[s for _, s in outs],
        scratch_shapes=list(scratch),
        compiler_params=pltpu.CompilerParams(vmem_limit_bytes=LIMIT),
        cost_estimate=pl.CostEstimate(
            flops=int(micros * WEIGHT), bytes_accessed=0, transcendentals=0
        ),
        name=name,
    )(*[a for a, _ in ins])


def norm_parts(v):
    center = v - jnp.mean(v, axis=-1, keepdims=True)
    spread = jnp.mean(center * center, axis=-1, keepdims=True)
    rstd = lax.rsqrt(spread + EPS)
    return center * rstd, rstd


def norm_back(u, xhat, rstd):
    return rstd * (
        u
        - jnp.mean(u, axis=-1, keepdims=True)
        - xhat * jnp.mean(u * xhat, axis=-1, keepdims=True)
    )


class Plan:
    def __init__(self, rows, seq, images, width, hidden, dp, head):
        self.rows, self.seq, self.images, self.width = rows, seq, images, width
        self.dp, self.head = dp, head
        self.pairs = head // 2
        self.cols = width // head
        self.hid = hidden // head
        self.hd = width // HEADS
        self.local_heads = HEADS // head
        self.piece = width // dp
        self.fast = dp == 8 and head == 4 and self.piece % 16 == 0
        self.base = [seq * i // 16 * 16 for i in range(images)]
        self.win = max(-(-(seq * (i + 1) - self.base[i]) // 16) * 16 for i in range(images))
        self.pad = self.base[-1] + self.win
        self.off = self.cols // 128 * 128
        self.lo = self.cols - self.off
        self.nq = 4 * self.cols - self.off
        self.cw = -(-self.cols // 128) * 128
        self.scale = 1.0 / math.sqrt(self.hd)


def source_rows(p, pos_ref, zz, xx):
    z, x = pos_ref[0], pos_ref[1]
    part = ((z - zz) & 3) * 2 + (x ^ xx)
    return pl.multiple_of(part * p.piece, p.piece)


def piece_list(p, pos_ref, other):
    core = pos_ref[2] ^ other
    found = []
    for b3 in range(2):
        for b2 in range(2):
            yy = jnp.where(core == 0, b3, b2)
            xx = jnp.where(core == 0, b2, b3)
            for zz in range(4):
                found.append((b3, b2, zz, yy, source_rows(p, pos_ref, zz, xx)))
    return found


def gather_blocks(p, refs, buf, pos_ref, other, lanes=slice(None), turned=False):
    if not p.fast:
        buf[...] = refs[0][:, :, lanes]
        return
    for b3, b2, zz, yy, row in piece_list(p, pos_ref, other):
        i, j = (zz, b2) if turned else (b2, zz)
        buf[yy, pl.ds(row, p.piece), :] = refs[b3][i, j, :, lanes]


def spread_blocks(p, buf, refs, pos_ref, other, received=None, turned=False):
    if not p.fast:
        refs[0][...] = buf[...].astype(BF16)
        return
    for b3, b2, zz, yy, row in piece_list(p, pos_ref, other):
        i, j = (zz, b2) if turned else (b2, zz)
        part = buf[yy, pl.ds(row, p.piece), :]
        if received is not None:
            part = part + received[b3][i, j].astype(F32)
        refs[b3][i, j] = part.astype(BF16)


def piece_shapes(p, lanes, turned=False):
    if p.fast:
        return [sds(((4, 2) if turned else (2, 4)) + (p.piece, lanes), BF16)] * 2
    return [sds((2, p.width, lanes), BF16)]


def entry_kernel(p, patches, out_grad, gain_one, shift_one, router):
    def body(x_ref, og_ref, g_ref, s_ref, r_ref, low_ref, gate_ref, down_ref):
        xhat, _ = norm_parts(x_ref[...].astype(F32))
        normed = xhat * g_ref[...] + s_ref[...]
        low_ref[...] = normed.astype(BF16)
        logit = jnp.sum(normed * r_ref[...], axis=-1, keepdims=True)
        gate_ref[...] = 1.0 / (1.0 + jnp.exp(-logit))
        down_ref[...] = jnp.sum(og_ref[...].astype(F32), axis=0, keepdims=True)

    return call(
        body,
        [
            (sds((p.pad, p.width), BF16), VMEM),
            (sds((p.pad, 1), F32), VMEM),
            (sds((1, p.width), F32), VMEM),
        ],
        [(a, VMEM) for a in (patches, out_grad, gain_one, shift_one, router)],
        micros=0.7,
        name="entry",
    )


def attention_forward(p, pos, weights, other, rows_low, bias, key_mask, carry, tail):
    last = tail is not None
    win, pad, lh, hd = p.win, p.pad, p.local_heads, p.hd

    def body(*refs):
        nw = len(weights)
        pos_ref, w_refs = refs[0], refs[1 : 1 + nw]
        rest = list(refs[1 + nw :])
        low_ref, bias_ref, mask_ref = rest[:3]
        rest = rest[3:]
        carry_ref = None
        if carry is not None:
            carry_ref, rest = rest[0], rest[1:]
        if last:
            x_ref, sg_ref, bo_ref, g2_ref, s2_ref = rest[:5]
            rest = rest[5:]
            qkv_ref, prob_ref, ctx_ref, att_ref, mixed_ref, in_ref = rest[:6]
            rest = rest[6:]
        else:
            qkv_ref, prob_ref, ctx_ref, att_ref = rest[:4]
            rest = rest[4:]
        wbuf, ctx = rest
        gather_blocks(p, w_refs, wbuf, pos_ref, other)
        low = low_ref[...]
        total = None
        for b in range(2):
            qkv = dot(low, wbuf[b, :, p.off :]) + bias_ref[b]
            qkv_ref[b] = qkv.astype(BF16)
            ctx[...] = jnp.zeros((pad, p.cw), F32)
            for img in range(p.images):
                first = p.base[img]
                at = lax.broadcasted_iota(jnp.int32, (win, 1), 0) + first
                valid = (at >= p.seq * img) & (at < p.seq * (img + 1))
                seen = mask_ref[img] > 0.0
                got = []
                for j in range(lh):
                    qs = p.lo + hd * j
                    q = qkv_ref[b, first : first + win, qs : qs + hd]
                    k = qkv_ref[b, first : first + win, qs + p.cols : qs + p.cols + hd]
                    v = qkv_ref[b, first : first + win, qs + 2 * p.cols : qs + 2 * p.cols + hd]
                    s = dot(q, k, NT) * p.scale
                    s = jnp.where(seen, s, -1e30)
                    e = jnp.exp(s - jnp.max(s, axis=-1, keepdims=True))
                    prob = e * (1.0 / jnp.sum(e, axis=-1, keepdims=True))
                    prob = jnp.where(valid, prob, 0.0).astype(BF16)
                    prob_ref[(b * p.images + img) * lh + j] = prob
                    got.append(dot(prob, v))
                if p.cw > p.cols:
                    got.append(jnp.zeros((win, p.cw - p.cols), F32))
                ctx[first : first + win, :] += jnp.concatenate(got, axis=1)
            mix = ctx[...].astype(BF16)
            ctx_ref[b] = mix
            part = dot(mix, wbuf[b, :, : p.cw], NT)
            total = part if total is None else total + part
        if carry_ref is not None:
            total = total + carry_ref[...]
        if not last:
            att_ref[...] = total
            return
        attended = total + bo_ref[...]
        att_ref[...] = attended
        mixed = x_ref[...].astype(F32) + sg_ref[...] * attended
        mixed_ref[...] = mixed
        xhat, _ = norm_parts(mixed)
        in_ref[...] = (xhat * g2_ref[...] + s2_ref[...]).astype(BF16)

    ins = [(pos, SMEM)] + [(w, VMEM) for w in weights]
    ins += [(a, VMEM) for a in (rows_low, bias, key_mask)]
    if carry is not None:
        ins.append((carry, VMEM))
    if last:
        ins += [(a, VMEM) for a in tail]
    outs = [
        (sds((2, pad, p.nq), BF16), VMEM),
        (sds((2 * p.images * lh, win, win), BF16), VMEM),
        (sds((2, pad, p.cw), BF16), VMEM),
        (sds((pad, p.width), F32), VMEM),
    ]
    if last:
        outs += [(sds((pad, p.width), F32), VMEM), (sds((pad, p.width), BF16), VMEM)]
    return call(
        body,
        outs,
        ins,
        [
            pltpu.VMEM((2, p.width, 4 * p.cols), BF16),
            pltpu.VMEM((pad, p.cw), F32),
        ],
        micros=5.5,
        name="attn_fwd",
    )


def up_kernel(p, pos, weights, other, mlp_in, bias):
    def body(*refs):
        nw = len(weights)
        pos_ref, w_refs = refs[0], refs[1 : 1 + nw]
        in_ref, b_ref, act_ref, slope_ref, wbuf = refs[1 + nw :]
        gather_blocks(p, w_refs, wbuf, pos_ref, other)
        rows = in_ref[...]
        for b in range(2):
            pre = dot(rows, wbuf[b]) + b_ref[b]
            phi = 0.5 * (1.0 + lax.erf(pre * INV_SQRT2))
            act_ref[b] = (pre * phi).astype(BF16)
            slope_ref[b] = (phi + pre * (jnp.exp(-0.5 * pre * pre) * INV_SQRT2PI)).astype(BF16)

    return call(
        body,
        [(sds((2, p.pad, p.hid), BF16), VMEM)] * 2,
        [(pos, SMEM)] + [(w, VMEM) for w in weights] + [(mlp_in, VMEM), (bias, VMEM)],
        [pltpu.VMEM((2, p.width, p.hid), BF16)],
        micros=2.5,
        name="up",
    )


def weight_grad(p, pos, other, pairs, received, name, turned=False):
    lanes = max(at + rhs.shape[2] for _, rhs, at in pairs)
    starts = [at for _, _, at in pairs]

    def body(*refs):
        pos_ref, rest = refs[0], list(refs[1:])
        ops, rest = rest[: 2 * len(pairs)], rest[2 * len(pairs) :]
        nr = len(received) if received is not None else 0
        got_refs, rest = rest[:nr], rest[nr:]
        out_refs, gbuf = rest[:-1], rest[-1]
        for b in range(2):
            done = 0
            for i, at in enumerate(starts):
                g = dot(ops[2 * i][...], ops[2 * i + 1][b], TN)
                end = at + g.shape[1]
                if at < done:
                    gbuf[b, :, at:done] += g[:, : done - at]
                    gbuf[b, :, done:end] = g[:, done - at :]
                else:
                    gbuf[b, :, at:end] = g
                done = end
        spread_blocks(p, gbuf, out_refs, pos_ref, other, got_refs if nr else None, turned)

    return call(
        body,
        [(s, VMEM) for s in piece_shapes(p, lanes, turned)],
        [(pos, SMEM)]
        + [(a, VMEM) for lhs, rhs, _ in pairs for a in (lhs, rhs)]
        + [(r, VMEM) for r in received or ()],
        [pltpu.VMEM((2, p.width, lanes), F32)],
        micros=2.3,
        name=name,
    )


def down_kernel(p, pos, w_up, w_down, other, active, slope, out_grad, carry):
    def body(*refs):
        nw = len(w_up)
        pos_ref, u_refs, d_refs = refs[0], refs[1 : 1 + nw], refs[1 + nw : 1 + 2 * nw]
        act_ref, slope_ref, og_ref = refs[1 + 2 * nw : 4 + 2 * nw]
        rest = list(refs[4 + 2 * nw :])
        if carry is not None:
            out_in, back_in = rest[:2]
            rest = rest[2:]
        out_ref, back_ref, low_ref, bias_ref, ubuf, dbuf = rest
        gather_blocks(p, d_refs, dbuf, pos_ref, other, turned=True)
        gather_blocks(p, u_refs, ubuf, pos_ref, other)
        og = og_ref[...]
        for b in range(2):
            grad = dot(og, dbuf[b]) * slope_ref[b].astype(F32)
            bias_ref[b] = jnp.sum(grad, axis=0, keepdims=True)
            low = grad.astype(BF16)
            low_ref[b] = low
            back = dot(low, ubuf[b], NT)
            out = dot(act_ref[b], dbuf[b], NT)
            if b == 0 and carry is not None:
                back_ref[...] = back_in[...] + back
                out_ref[...] = out_in[...] + out
            elif b == 0:
                back_ref[...] = back
                out_ref[...] = out
            else:
                back_ref[...] += back
                out_ref[...] += out

    ins = [(pos, SMEM)] + [(w, VMEM) for w in tuple(w_up) + tuple(w_down)]
    ins += [(a, VMEM) for a in (active, slope, out_grad)]
    if carry is not None:
        ins += [(a, VMEM) for a in carry]
    return call(
        body,
        [
            (sds((p.pad, p.width), F32), VMEM),
            (sds((p.pad, p.width), F32), VMEM),
            (sds((2, p.pad, p.hid), BF16), VMEM),
            (sds((2, 1, p.hid), F32), VMEM),
        ],
        ins,
        [
            pltpu.VMEM((2, p.width, p.hid), BF16),
            pltpu.VMEM((2, p.width, p.hid), BF16),
        ],
        micros=5.0,
        name="down",
    )


def middle_kernel(p, patches, out_grad, mixed, out_sum, back_sum, attended, gate, sel, vecs):
    gain_one, shift_one, gain_two, b_down = vecs

    def body(
        x_ref, og_ref, mix_ref, out_ref, back_ref, att_ref, gate_ref, sel_ref,
        g1_ref, s1_ref, g2_ref, bd_ref,
        tok_ref, mg_ref, br_ref, logit_ref, gg_ref, gs_ref, gb_ref, gr_ref,
    ):
        mixed = mix_ref[...]
        tok_ref[...] = (mixed + out_ref[...] + bd_ref[...])[: p.rows].astype(BF16)
        xhat, rstd = norm_parts(mixed)
        back = back_ref[...]
        gg_ref[...] = jnp.sum(back * xhat, axis=0, keepdims=True)
        gs_ref[...] = jnp.sum(back, axis=0, keepdims=True)
        mg = og_ref[...].astype(F32) + norm_back(back * g2_ref[...], xhat, rstd)
        mg_ref[...] = mg
        gate, sel = gate_ref[...], sel_ref[...]
        branch = (gate * sel) * mg
        gb_ref[...] = jnp.sum(branch, axis=0, keepdims=True)
        br_ref[...] = branch.astype(BF16)
        logit = sel * jnp.sum(mg * att_ref[...], axis=-1, keepdims=True) * gate * (1.0 - gate)
        logit_ref[...] = logit
        first, _ = norm_parts(x_ref[...].astype(F32))
        normed = first * g1_ref[...] + s1_ref[...]
        gr_ref[...] = jnp.sum(normed * logit, axis=0, keepdims=True)

    vec = (sds((1, p.width), F32), VMEM)
    return call(
        body,
        [
            (sds((p.rows, p.width), BF16), VMEM),
            (sds((p.pad, p.width), F32), VMEM),
            (sds((p.pad, p.width), BF16), VMEM),
            (sds((p.pad, 1), F32), VMEM),
            vec, vec, vec, vec,
        ],
        [
            (a, VMEM)
            for a in (
                patches, out_grad, mixed, out_sum, back_sum, attended, gate, sel,
                gain_one, shift_one, gain_two, b_down,
            )
        ],
        micros=2.6,
        name="middle",
    )


def attention_values(p, pos, weights, other, branch, probs):
    win, pad, lh, hd = p.win, p.pad, p.local_heads, p.hd
    lead = p.cw - p.cols

    def body(*refs):
        nw = len(weights)
        pos_ref, w_refs = refs[0], refs[1 : 1 + nw]
        br_ref, prob_ref, dc_ref, dv_ref, bias_ref, wbuf, gv = refs[1 + nw :]
        gather_blocks(p, w_refs, wbuf, pos_ref, other, slice(0, p.cw))
        for b in range(2):
            dc_ref[b] = dot(br_ref[...], wbuf[b]).astype(BF16)
            gv[...] = jnp.zeros((pad, p.cw), F32)
            for img in range(p.images):
                here = slice(p.base[img], p.base[img] + win)
                got = [jnp.zeros((win, lead), F32)] if lead else []
                for j in range(lh):
                    prob = prob_ref[(b * p.images + img) * lh + j]
                    got.append(dot(prob, dc_ref[b, here, hd * j : hd * j + hd], TN))
                gv[here, :] += jnp.concatenate(got, axis=1)
            full = gv[...]
            bias_ref[b] = jnp.sum(full, axis=0, keepdims=True)
            dv_ref[b] = full.astype(BF16)

    return call(
        body,
        [
            (sds((2, pad, p.cw), BF16), VMEM),
            (sds((2, pad, p.cw), BF16), VMEM),
            (sds((2, 1, p.cw), F32), VMEM),
        ],
        [(pos, SMEM)] + [(w, VMEM) for w in weights] + [(branch, VMEM), (probs, VMEM)],
        [pltpu.VMEM((2, p.width, p.cw), BF16), pltpu.VMEM((pad, p.cw), F32)],
        micros=2.5,
        name="attn_values",
    )


def attention_backward(p, pos, weights, other, dc, dv, qkv, probs, carry):
    win, pad, lh, hd, cols = p.win, p.pad, p.local_heads, p.hd, p.cols
    lead = p.cw - p.cols

    def body(*refs):
        nw = len(weights)
        pos_ref, w_refs = refs[0], refs[1 : 1 + nw]
        dc_ref, dv_ref, qkv_ref, prob_ref = refs[1 + nw : 5 + nw]
        rest = list(refs[5 + nw :])
        if carry is not None:
            carry_ref, rest = rest[0], rest[1:]
        low_ref, n1_ref, bias_ref, wbuf, gq = rest
        gather_blocks(p, w_refs, wbuf, pos_ref, other, slice(p.off, None))
        total = None
        for b in range(2):
            gq[...] = jnp.zeros((pad, 2 * cols), F32)
            for img in range(p.images):
                first = p.base[img]
                here = slice(first, first + win)
                dqs, dks = [], []
                for j in range(lh):
                    qs = p.lo + hd * j
                    q = qkv_ref[b, here, qs : qs + hd]
                    k = qkv_ref[b, here, qs + cols : qs + cols + hd]
                    v = qkv_ref[b, here, qs + 2 * cols : qs + 2 * cols + hd]
                    d = dc_ref[b, here, hd * j : hd * j + hd]
                    soft = prob_ref[(b * p.images + img) * lh + j].astype(F32)
                    pg = dot(d, v, NT)
                    row = jnp.sum(soft * pg, axis=-1, keepdims=True)
                    s = (soft * (pg - row) * p.scale).astype(BF16)
                    dqs.append(dot(s, k))
                    dks.append(dot(s, q, TN))
                gq[here, :] += jnp.concatenate(dqs + dks, axis=1)
            full = gq[...]
            bias_ref[b] = jnp.sum(full, axis=0, keepdims=True)
            low = full.astype(BF16)
            low_ref[b] = low
            start = [jnp.zeros((pad, p.lo), BF16)] if p.lo else []
            gl = jnp.concatenate(start + [low, dv_ref[b][:, lead:]], axis=1)
            part = dot(gl, wbuf[b], NT)
            total = part if total is None else total + part
        if carry is not None:
            total = total + carry_ref[...]
        n1_ref[...] = total

    ins = [(pos, SMEM)] + [(w, VMEM) for w in weights]
    ins += [(a, VMEM) for a in (dc, dv, qkv, probs)]
    if carry is not None:
        ins.append((carry, VMEM))
    return call(
        body,
        [
            (sds((2, pad, 2 * cols), BF16), VMEM),
            (sds((pad, p.width), F32), VMEM),
            (sds((2, 1, 2 * cols), F32), VMEM),
        ],
        ins,
        [pltpu.VMEM((2, p.width, p.nq), BF16), pltpu.VMEM((pad, 2 * cols), F32)],
        micros=6.0,
        name="attn_bwd",
    )


def exit_kernel(p, patches, back, logit, router, gain_one, mixed_grad, common, query, value, up):
    half = p.cols
    at = p.cw - p.cols

    def body(*refs):
        x_ref, n_ref, l_ref, r_ref, g_ref, mg_ref = refs[:6]
        c_refs = refs[6 : 6 + len(common)]
        rest = list(refs[6 + len(common) :])
        q_refs, v_refs, u_refs = (rest[i * p.pairs : (i + 1) * p.pairs] for i in range(3))
        out_ref, *vec_refs = rest[3 * p.pairs :]
        xhat, rstd = norm_parts(x_ref[...].astype(F32))
        grad = n_ref[...] + l_ref[...] * r_ref[...]
        g_gain = jnp.sum(grad * xhat, axis=0, keepdims=True)
        g_shift = jnp.sum(grad, axis=0, keepdims=True)
        total = mg_ref[...] + norm_back(grad * g_ref[...], xhat, rstd)
        out_ref[...] = total[: p.rows].astype(BF16)
        for i in range(p.pairs):
            vec = vec_refs[i]
            vec[...] = jnp.zeros(vec.shape, F32)
            for j, r in enumerate([g_gain, g_shift] + [c[...] for c in c_refs]):
                vec[j : j + 1, :] = r
            for b in range(2):
                row = 8 + 2 * b
                vec[row : row + 1, : 2 * half] = q_refs[i][b]
                vec[row : row + 1, half : 2 * half] = v_refs[i][b][:, at:]
                vec[row + 1 : row + 2, :] = u_refs[i][b]

    return call(
        body,
        [(sds((p.rows, p.width), BF16), VMEM)] + [(sds((12, p.width), F32), VMEM)] * p.pairs,
        [
            (a, VMEM)
            for a in (
                [patches, back, logit, router, gain_one, mixed_grad]
                + list(common)
                + list(query)
                + list(value)
                + list(up)
            )
        ],
        micros=EXIT,
        name="exit",
    )


def halves_kernel(keep, got):
    def body(k_ref, g_ref, mine_ref, other_ref):
        mine_ref[...] = (k_ref[0].astype(F32) + g_ref[0].astype(F32)).astype(BF16)
        other_ref[...] = (k_ref[1].astype(F32) + g_ref[1].astype(F32)).astype(BF16)

    return call(
        body,
        [(sds(keep.shape[1:], BF16), VMEM)] * 2,
        [(keep, VMEM), (got, VMEM)],
        micros=4.0,
        name="halves",
    )


def parts_kernel(mine, got):
    def body(m_ref, g_ref, *part_refs):
        for i, ref in enumerate(part_refs):
            ref[...] = (m_ref[i].astype(F32) + g_ref[i].astype(F32)).astype(BF16)

    return call(
        body,
        [(sds(mine.shape[1:], BF16), VMEM)] * 4,
        [(mine, VMEM), (got, VMEM)],
        micros=4.0,
        name="parts",
    )


def flat(z, x, y, c):
    return ((z * 2 + x) * 2 + y) * 2 + c


def table(move):
    pairs = []
    for z in range(4):
        for x in range(2):
            for y in range(2):
                for c in range(2):
                    pairs.append((flat(z, x, y, c), flat(*move(z, x, y, c))))
    return pairs


def send(v, move):
    return lax.ppermute(v, ("dp", "head"), table(move))


def along_z(shift):
    return lambda z, x, y, c: ((z + shift) % 4, x, y, c)


def near(z, x, y, c):
    return (z, x ^ 1, y, c) if c == 0 else (z, x, y ^ 1, c)


def far(z, x, y, c):
    return (z, x, y ^ 1, c) if c == 0 else (z, x ^ 1, y, c)


def core(z, x, y, c):
    return (z, x, y, c ^ 1)


def after(v, *others):
    return lax.optimization_barrier((v,) + others)[0]


def add(a, b):
    return (a.astype(F32) + b.astype(F32)).astype(BF16)


def gather_whole(p, shard):
    full = lax.all_gather(lax.all_gather(shard, "dp", axis=0, tiled=True), "head", axis=0)
    return [(full[2 * i : 2 * i + 2],) for i in range(p.pairs)]


def own_pieces(shard):
    return jnp.stack([shard] + [send(shard, along_z(s)) for s in (1, 2, 3)])


def both_cores(eight, rest, *others):
    eight_out, rest_out = after(eight, *others), after(rest, *others)
    return [(eight, rest), (send(eight_out, core), send(rest_out, core))]


def scatter_whole(p, grads):
    stacked = jnp.concatenate(grads, axis=0)
    part = lax.psum_scatter(stacked, "head", scatter_dimension=0, tiled=False)
    return lax.psum_scatter(part, "dp", scatter_dimension=0, tiled=True).astype(F32)


class Scatter:
    def __init__(self, keep, away):
        self.keep, self.away = keep, away

    def first(self, *others):
        got = after(send(self.away, far), *others)
        self.mine, self.other = halves_kernel(self.keep, got)

    def second(self, *others):
        got = after(send(self.other, near), *others)
        self.pieces = parts_kernel(self.mine, got)


def along_chips(pieces, *others):
    got = [after(send(pieces[s], along_z(-s)), *others) for s in (1, 2, 3)]
    return sum([g.astype(F32) for g in got], pieces[0].astype(F32))


def gather_head(p, vector):
    if not p.fast:
        return lax.all_gather(vector, "head", axis=0)
    pair = jnp.stack([vector, send(vector, lambda z, x, y, c: (z, x, y ^ 1, c))])
    return jnp.concatenate([pair, send(pair, core)], axis=0)


def sum_vectors(p, vecs):
    total = lax.psum(vecs[0][:8], ("dp", "head"))
    owned = jnp.concatenate([v[8:] for v in vecs]).reshape(p.head, 2, p.width)
    mine = lax.psum_scatter(owned, "head", scatter_dimension=0, tiled=False)
    return jnp.concatenate([total, lax.psum(mine, "dp")])


class VectorSum:
    def __init__(self, vecs):
        self.keep, self.away = vecs

    def over_cores(self, *others):
        self.vec = self.keep + after(send(self.away, core), *others)

    def over_z(self, step, *others):
        got = send(self.vec, lambda z, x, y, c: (z ^ step, x, y, c))
        self.vec = self.vec + after(got, *others)

    def over_xy(self, *others):
        mine, away = self.vec[:10], jnp.concatenate([self.vec[:8], self.vec[10:]])
        along_x = send(mine, lambda z, x, y, c: (z, x ^ 1, y, c))
        along_y = send(away, lambda z, x, y, c: (z, x, y ^ 1, c))
        across = send(away, lambda z, x, y, c: (z, x ^ 1, y ^ 1, c))
        along_x, along_y, across = (after(v, *others) for v in (along_x, along_y, across))
        return (mine + along_x) + (along_y + across)


def on_device(
    patches, selected, out_grad, gain_one, shift_one, router_w, w_query, b_query, w_key, w_value,
    b_value, w_out, b_out, gain_two, shift_two, w_up, b_up, w_down, b_down,
):
    images, seq = selected.shape
    rows, width = patches.shape
    dp, head = lax.axis_size("dp"), lax.axis_size("head")
    p = Plan(rows, seq, images, width, b_up.shape[0] * head, dp, head)
    cols, hid = p.cols, p.hid

    dp_pos, head_pos = lax.axis_index("dp"), lax.axis_index("head")
    pos = jnp.stack([dp_pos // 2, dp_pos % 2, head_pos % 2]).astype(jnp.int32)

    attn_shard = jnp.concatenate([w_out.T, w_query, w_key, w_value], axis=1)
    bias_parts = after(jnp.concatenate([b_query, b_value, b_up]), attn_shard)
    biases = gather_head(p, bias_parts).astype(F32)
    zeros = jnp.zeros((head, cols), F32)
    qkv_bias = jnp.concatenate(
        [zeros[:, : p.lo], biases[:, :cols], zeros, biases[:, cols : 2 * cols]], axis=1
    )[:, None, :]
    up_bias = biases[:, 2 * cols :][:, None, :]

    def row(v):
        return v.astype(F32)[None, :]

    more = p.pad - rows
    x_pad = jnp.pad(patches, ((0, more), (0, 0)))
    og_pad = jnp.pad(out_grad, ((0, more), (0, 0)))
    sel = selected.astype(F32)
    sel_col = jnp.pad(sel.reshape(rows, 1), ((0, more), (0, 0)))
    key_mask = jnp.stack(
        [
            jnp.pad(sel[i], (seq * i - p.base[i], p.win - seq - (seq * i - p.base[i])))
            for i in range(images)
        ]
    )[:, None, :]
    gain_one, shift_one, gain_two, shift_two = map(row, (gain_one, shift_one, gain_two, shift_two))
    router, b_out, b_down = row(router_w), row(b_out), row(b_down)

    fast = p.fast
    if fast:
        down_one = w_down.T
        down_near = send(down_one, near)
        attn_own = after(own_pieces(attn_shard), biases, down_near)
        x_in = after(x_pad, attn_own)
        rows_low, gate, g_down_bias = entry_kernel(p, x_in, og_pad, gain_one, shift_one, router)
        up_one = after(w_up, attn_own)
        up_z = [send(up_one, along_z(s)) for s in (1, 2, 3)]
        attn_eight = after(jnp.stack([attn_own, send(attn_own, near)]), rows_low, up_z[0])
        attn_rest = send(attn_eight, far)
        attn_w = both_cores(attn_eight, attn_rest)
        up_own = after(jnp.stack([w_up] + up_z), attn_eight)
        down_pair = after(jnp.stack([down_one, down_near]), up_own)
        down_z = [send(down_pair, along_z(s)) for s in (1, 2, 3)]
        up_eight = after(jnp.stack([up_own, send(up_own, near)]), attn_rest)
        up_rest = send(up_eight, far)
        attn_w[1] = tuple(after(w, up_rest) for w in attn_w[1])
        up_w = both_cores(up_eight, up_rest)
    else:
        rows_low, gate, g_down_bias = entry_kernel(p, x_pad, og_pad, gain_one, shift_one, router)
        attn_w, up_w, down_w = (gather_whole(p, v) for v in (attn_shard, w_up, w_down.T))
    sel_gate = gate * sel_col

    qkvs, probs, ctxs, carry = [], [], [], None
    for i in range(p.pairs):
        tail = (x_pad, sel_gate, b_out, gain_two, shift_two) if i == p.pairs - 1 else None
        if fast and i == 1:
            down_eight = jnp.stack([down_pair] + [after(v, carry) for v in down_z])
            down_rest = send(down_eight, far)
        got = attention_forward(
            p, pos, attn_w[i], i, rows_low, qkv_bias[2 * i : 2 * i + 2], key_mask, carry, tail
        )
        qkvs.append(got[0])
        probs.append(got[1])
        ctxs.append(got[2])
        carry = got[3]
    attended, mixed, mlp_in = got[3], got[4], got[5]

    acts, slopes = [], []
    up_in = mlp_in
    for i in range(p.pairs):
        act, slope = up_kernel(p, pos, up_w[i], i, up_in, up_bias[2 * i : 2 * i + 2])
        acts.append(act)
        slopes.append(slope)

    def values(i, branch):
        return attention_values(p, pos, attn_w[i], i if fast else 0, branch, probs[i])

    def backward(i, dc, dv, carry):
        return attention_backward(
            p, pos, attn_w[i], i if fast else 0, dc, dv, qkvs[i], probs[i], carry
        )

    def grads(pairs, received, name, other, turned=False):
        return weight_grad(p, pos, other, pairs, received, name, turned)

    def attention_pairs(i, dv, low):
        return [(branch, ctxs[i], 0), (rows_low, dv, p.off), (rows_low, low, 2 * cols)]

    def down(i, grad_in, carry):
        return down_kernel(p, pos, up_w[i], down_w[i], i, acts[i], slopes[i], grad_in, carry)

    def middle(back, out):
        return middle_kernel(
            p, x_pad, og_pad, mixed, out, back, attended, gate, sel_col,
            (gain_one, shift_one, gain_two, b_down),
        )

    def leave(back, qsums, vsums, up_sums):
        common = (g_router, g_out_bias, g_gain2, g_shift2, g_down_bias)
        return exit_kernel(
            p, x_pad, back, logit, router, gain_one, mixed_grad, common, qsums, vsums, up_sums
        )

    if fast:
        down_w = both_cores(down_eight, down_rest, acts[1])
        gd1 = grads([(og_pad, acts[1], 0)], None, "grad_down", 1)
        gd1_got = [send(o, core) for o in gd1]
        out_sum, back_sum, low0, sum0 = down(0, after(og_pad, *gd1), None)
        gd0 = grads([(after(og_pad, low0), acts[0], 0)], gd1_got, "grad_down", 0)
        down_sum = Scatter(*gd0)
        out_sum, back_sum, low1, sum1 = down(1, after(og_pad, *gd0), (out_sum, back_sum))
        tokens, mixed_grad, branch, logit, g_gain2, g_shift2, g_out_bias, g_router = middle(
            back_sum, out_sum
        )
        gu1 = grads([(after(mlp_in, branch), low1, 0)], None, "grad_up", 1)
        gu1_got = [send(o, core) for o in gu1]
        dc1, dv1, vsum1 = values(1, after(branch, *gu1))
        dc0, dv0, vsum0 = values(0, after(branch, dv1))
        down_sum.first()
        gu1_got = [after(g, dv0, down_sum.other) for g in gu1_got]
        gu0 = grads([(mlp_in, low0, 0)], gu1_got, "grad_up", 0)
        up_sum = Scatter(*gu0)
        low1, carry, qsum1 = backward(1, after(dc1, *gu0), dv1, None)
        ga1 = grads(attention_pairs(1, dv1, low1), None, "grad_attn", 1)
        ga1_got = [send(o, core) for o in ga1]
        down_sum.second()
        low0, carry, qsum0 = backward(0, after(dc0, *ga1, *down_sum.pieces), dv0, carry)
        up_sum.first(low0)
        ga1_got = [after(g, up_sum.other) for g in ga1_got]
        ga0 = grads(attention_pairs(0, dv0, low0), ga1_got, "grad_attn", 0)
        attn_sum = Scatter(*ga0)
        carry = after(carry, *ga0)
        grad_patches, *vecs = leave(carry, (qsum0, qsum1), (vsum0, vsum1), (sum0, sum1))
        vec_sum = VectorSum(vecs)
        grad_down = along_chips(down_sum.pieces, grad_patches)
        vec_sum.over_cores(grad_down)
        up_sum.second(vec_sum.vec)
        vec_sum.vec = after(vec_sum.vec, *up_sum.pieces)
        attn_sum.first(*up_sum.pieces)
        grad_up = along_chips(up_sum.pieces, attn_sum.other)
        vec_sum.over_z(1, grad_up)
        attn_sum.second(vec_sum.vec)
        vec_sum.over_z(2, *attn_sum.pieces)
        grad_attn = along_chips(attn_sum.pieces, vec_sum.vec)
        summed = vec_sum.over_xy(grad_attn)
    else:
        carry, lows, up_sums = None, [], []
        for i in range(p.pairs):
            got = down(i, og_pad, carry)
            carry = (got[0], got[1])
            lows.append(got[2])
            up_sums.append(got[3])
        tokens, mixed_grad, branch, logit, g_gain2, g_shift2, g_out_bias, g_router = middle(
            carry[1], carry[0]
        )
        carry, blocks, vsums, qsums = None, [], [], []
        for i in range(p.pairs):
            dc, dv, vsum = values(i, branch)
            low, carry, qsum = backward(i, dc, dv, carry)
            blocks += grads(attention_pairs(i, dv, low), None, "grad_attn", 0)
            vsums.append(vsum)
            qsums.append(qsum)
        grad_patches, *vecs = leave(carry, qsums, vsums, up_sums)
        grad_down, grad_up, grad_attn = (
            scatter_whole(p, g)
            for g in (
                [grads([(og_pad, a, 0)], None, "grad_down", 0)[0] for a in acts],
                [grads([(mlp_in, v, 0)], None, "grad_up", 0)[0] for v in lows],
                blocks,
            )
        )
        summed = sum_vectors(p, vecs)

    vecs = [summed[i] for i in range(7)]
    owned, hidden_sum = summed[8], summed[9]
    return (
        tokens,
        grad_patches,
        vecs[0],
        vecs[1],
        vecs[2],
        grad_attn[:, 2 * cols : 3 * cols],
        owned[:cols],
        grad_attn[:, 3 * cols :],
        grad_attn[:, cols : 2 * cols],
        owned[cols : 2 * cols],
        grad_attn[:, :cols].T,
        vecs[3],
        vecs[4],
        vecs[5],
        grad_up,
        hidden_sum,
        grad_down.T,
        vecs[6],
    )


def solution(mesh):
    rows, rep = P(("dp", "head"), None), P()
    split, side, turned = P("dp", "head"), P("head"), P("head", "dp")
    return jax.shard_map(
        on_device,
        mesh=mesh,
        in_specs=(
            rows, rows, rows, rep, rep, rep, split, side, split, split, side, turned, rep, rep,
            rep, split, side, turned, rep,
        ),
        out_specs=(
            rows, rows, rep, rep, rep, split, side, split, split, side, turned, rep, rep, rep,
            split, side, turned, rep,
        ),
        check_vma=False,
    )
```

```python
import math

import jax
import jax.numpy as jnp
from jax import lax
from jax.experimental import pallas as pl
from jax.experimental.pallas import tpu as pltpu
from jax.sharding import PartitionSpec as P

HEADS = 12
EPS = 1e-06
F32 = jnp.float32
BF16 = jnp.bfloat16
VMEM = pl.BlockSpec(memory_space=pltpu.VMEM)
SMEM = pl.BlockSpec(memory_space=pltpu.SMEM)
EXIT = 2.0
WEIGHT = 4.0e9
LIMIT = 20 * 1024 * 1024
INV_SQRT2 = 0.7071067811865476
INV_SQRT2PI = 0.3989422804014327

NN = (((1,), (0,)), ((), ()))
NT = (((1,), (1,)), ((), ()))
TN = (((0,), (0,)), ((), ()))


def dot(a, b, dims=NN):
    return lax.dot_general(a, b, dims, preferred_element_type=F32)


def sds(shape, dtype):
    return jax.ShapeDtypeStruct(shape, dtype)


def call(body, outs, ins, scratch=(), micros=1.0, name=None):
    return pl.pallas_call(
        body,
        out_shape=[o for o, _ in outs],
        in_specs=[s for _, s in ins],
        out_specs=[s for _, s in outs],
        scratch_shapes=list(scratch),
        compiler_params=pltpu.CompilerParams(vmem_limit_bytes=LIMIT),
        cost_estimate=pl.CostEstimate(
            flops=int(micros * WEIGHT), bytes_accessed=0, transcendentals=0
        ),
        name=name,
    )(*[a for a, _ in ins])


def norm_parts(v):
    center = v - jnp.mean(v, axis=-1, keepdims=True)
    spread = jnp.mean(center * center, axis=-1, keepdims=True)
    rstd = lax.rsqrt(spread + EPS)
    return center * rstd, rstd


def norm_back(u, xhat, rstd):
    return rstd * (
        u
        - jnp.mean(u, axis=-1, keepdims=True)
        - xhat * jnp.mean(u * xhat, axis=-1, keepdims=True)
    )


class Plan:
    def __init__(self, rows, seq, images, width, hidden, dp, head):
        self.rows, self.seq, self.images, self.width = rows, seq, images, width
        self.dp, self.head = dp, head
        self.pairs = head // 2
        self.cols = width // head
        self.hid = hidden // head
        self.hd = width // HEADS
        self.local_heads = HEADS // head
        self.piece = width // dp
        self.fast = dp == 8 and head == 4 and self.piece % 16 == 0
        self.base = [seq * i // 16 * 16 for i in range(images)]
        self.win = max(-(-(seq * (i + 1) - self.base[i]) // 16) * 16 for i in range(images))
        self.pad = self.base[-1] + self.win
        self.off = self.cols // 128 * 128
        self.lo = self.cols - self.off
        self.nq = 4 * self.cols - self.off
        self.cw = -(-self.cols // 128) * 128
        self.scale = 1.0 / math.sqrt(self.hd)
        self.exact = math.log2(self.scale).is_integer()


def source_rows(p, pos_ref, zz, xx):
    z, x = pos_ref[0], pos_ref[1]
    part = ((z - zz) & 3) * 2 + (x ^ xx)
    return pl.multiple_of(part * p.piece, p.piece)


def piece_list(p, pos_ref, other):
    core = pos_ref[2] ^ other
    found = []
    for b3 in range(2):
        for b2 in range(2):
            yy = jnp.where(core == 0, b3, b2)
            xx = jnp.where(core == 0, b2, b3)
            for zz in range(4):
                found.append((b3, b2, zz, yy, source_rows(p, pos_ref, zz, xx)))
    return found


def gather_blocks(p, refs, buf, pos_ref, other, lanes=slice(None), turned=False):
    if not p.fast:
        buf[...] = refs[0][:, :, lanes]
        return
    for b3, b2, zz, yy, row in piece_list(p, pos_ref, other):
        i, j = (zz, b2) if turned else (b2, zz)
        buf[yy, pl.ds(row, p.piece), :] = refs[b3][i, j, :, lanes]


def spread_blocks(p, buf, refs, pos_ref, other, received=None, turned=False):
    if not p.fast:
        refs[0][...] = buf[...].astype(BF16)
        return
    for b3, b2, zz, yy, row in piece_list(p, pos_ref, other):
        i, j = (zz, b2) if turned else (b2, zz)
        part = buf[yy, pl.ds(row, p.piece), :]
        if received is not None:
            part = part + received[b3][i, j].astype(F32)
        refs[b3][i, j] = part.astype(BF16)


def piece_shapes(p, lanes, turned=False):
    if p.fast:
        return [sds(((4, 2) if turned else (2, 4)) + (p.piece, lanes), BF16)] * 2
    return [sds((2, p.width, lanes), BF16)]


def entry_kernel(p, patches, out_grad, gain_one, shift_one, router):
    def body(x_ref, og_ref, g_ref, s_ref, r_ref, low_ref, gate_ref, down_ref):
        xhat, _ = norm_parts(x_ref[...].astype(F32))
        normed = xhat * g_ref[...] + s_ref[...]
        low_ref[...] = normed.astype(BF16)
        logit = jnp.sum(normed * r_ref[...], axis=-1, keepdims=True)
        gate_ref[...] = 1.0 / (1.0 + jnp.exp(-logit))
        down_ref[...] = jnp.sum(og_ref[...].astype(F32), axis=0, keepdims=True)

    return call(
        body,
        [
            (sds((p.pad, p.width), BF16), VMEM),
            (sds((p.pad, 1), F32), VMEM),
            (sds((1, p.width), F32), VMEM),
        ],
        [(a, VMEM) for a in (patches, out_grad, gain_one, shift_one, router)],
        micros=0.7,
        name="entry",
    )


def attention_forward(p, pos, weights, other, rows_low, bias, key_mask, carry, tail):
    last = tail is not None
    win, pad, lh, hd = p.win, p.pad, p.local_heads, p.hd

    def body(*refs):
        nw = len(weights)
        pos_ref, w_refs = refs[0], refs[1 : 1 + nw]
        rest = list(refs[1 + nw :])
        low_ref, bias_ref, mask_ref = rest[:3]
        rest = rest[3:]
        carry_ref = None
        if carry is not None:
            carry_ref, rest = rest[0], rest[1:]
        if last:
            x_ref, sg_ref, bo_ref, g2_ref, s2_ref = rest[:5]
            rest = rest[5:]
            qkv_ref, prob_ref, ctx_ref, att_ref, wbuf, mixed_ref, in_ref = rest[:7]
        else:
            qkv_ref, prob_ref, ctx_ref, att_ref, wbuf = rest[:5]
        ctx = rest[-1]
        gather_blocks(p, w_refs, wbuf, pos_ref, other)
        low = low_ref[...]
        total = None
        for b in range(2):
            qkv = dot(low, wbuf[b, :, p.off :]) + bias_ref[b]
            qkv_ref[b] = qkv.astype(BF16)
            ctx[...] = jnp.zeros((pad, p.cw), F32)
            for img in range(p.images):
                first = p.base[img]
                at = lax.broadcasted_iota(jnp.int32, (win, 1), 0) + first
                valid = (at >= p.seq * img) & (at < p.seq * (img + 1))
                seen = mask_ref[img] > 0.0
                got = []
                for j in range(lh):
                    qs = p.lo + hd * j
                    q = qkv_ref[b, first : first + win, qs : qs + hd]
                    k = qkv_ref[b, first : first + win, qs + p.cols : qs + p.cols + hd]
                    v = qkv_ref[b, first : first + win, qs + 2 * p.cols : qs + 2 * p.cols + hd]
                    if p.exact:
                        s = dot(q * jnp.asarray(p.scale, BF16), k, NT)
                    else:
                        s = dot(q, k, NT) * p.scale
                    s = jnp.where(seen, s, -1e30)
                    e = jnp.exp(s - jnp.max(s, axis=-1, keepdims=True))
                    share = jnp.where(valid, 1.0 / jnp.sum(e, axis=-1, keepdims=True), 0.0)
                    prob = (e * share).astype(BF16)
                    prob_ref[(b * p.images + img) * lh + j] = prob
                    got.append(dot(prob, v))
                if p.cw > p.cols:
                    got.append(jnp.zeros((win, p.cw - p.cols), F32))
                ctx[first : first + win, :] += jnp.concatenate(got, axis=1)
            mix = ctx[...].astype(BF16)
            ctx_ref[b] = mix
            part = dot(mix, wbuf[b, :, : p.cw], NT)
            total = part if total is None else total + part
        if carry_ref is not None:
            total = total + carry_ref[...]
        if not last:
            att_ref[...] = total
            return
        attended = total + bo_ref[...]
        att_ref[...] = attended
        mixed = x_ref[...].astype(F32) + sg_ref[...] * attended
        mixed_ref[...] = mixed
        xhat, _ = norm_parts(mixed)
        in_ref[...] = (xhat * g2_ref[...] + s2_ref[...]).astype(BF16)

    ins = [(pos, SMEM)] + [(w, VMEM) for w in weights]
    ins += [(a, VMEM) for a in (rows_low, bias, key_mask)]
    if carry is not None:
        ins.append((carry, VMEM))
    if last:
        ins += [(a, VMEM) for a in tail]
    outs = [
        (sds((2, pad, p.nq), BF16), VMEM),
        (sds((2 * p.images * lh, win, win), BF16), VMEM),
        (sds((2, pad, p.cw), BF16), VMEM),
        (sds((pad, p.width), F32), VMEM),
        (sds((2, p.width, 4 * p.cols), BF16), VMEM),
    ]
    if last:
        outs += [(sds((pad, p.width), F32), VMEM), (sds((pad, p.width), BF16), VMEM)]
    return call(
        body,
        outs,
        ins,
        [pltpu.VMEM((pad, p.cw), F32)],
        micros=5.5,
        name="attn_fwd",
    )


def up_kernel(p, pos, weights, other, mlp_in, bias):
    def body(*refs):
        nw = len(weights)
        pos_ref, w_refs = refs[0], refs[1 : 1 + nw]
        in_ref, b_ref, act_ref, slope_ref, wbuf = refs[1 + nw :]
        gather_blocks(p, w_refs, wbuf, pos_ref, other)
        rows = in_ref[...]
        for b in range(2):
            pre = dot(rows, wbuf[b]) + b_ref[b]
            phi = 0.5 * (1.0 + lax.erf(pre * INV_SQRT2))
            act_ref[b] = (pre * phi).astype(BF16)
            slope_ref[b] = (phi + pre * (jnp.exp(-0.5 * pre * pre) * INV_SQRT2PI)).astype(BF16)

    return call(
        body,
        [(sds((2, p.pad, p.hid), BF16), VMEM)] * 2 + [(sds((2, p.width, p.hid), BF16), VMEM)],
        [(pos, SMEM)] + [(w, VMEM) for w in weights] + [(mlp_in, VMEM), (bias, VMEM)],
        micros=2.5,
        name="up",
    )


def weight_grad(p, pos, other, pairs, received, name, turned=False):
    lanes = max(at + rhs.shape[2] for _, rhs, at in pairs)
    starts = [at for _, _, at in pairs]

    def body(*refs):
        pos_ref, rest = refs[0], list(refs[1:])
        ops, rest = rest[: 2 * len(pairs)], rest[2 * len(pairs) :]
        nr = len(received) if received is not None else 0
        got_refs, rest = rest[:nr], rest[nr:]
        out_refs, gbuf = rest[:-1], rest[-1]
        turned_lhs = {}
        for i, (lhs, _, _) in enumerate(pairs):
            if id(lhs) not in turned_lhs:
                turned_lhs[id(lhs)] = ops[2 * i][...].T
        for b in range(2):
            done = 0
            for i, at in enumerate(starts):
                g = dot(turned_lhs[id(pairs[i][0])], ops[2 * i + 1][b])
                end = at + g.shape[1]
                if at < done:
                    gbuf[b, :, at:done] += g[:, : done - at]
                    gbuf[b, :, done:end] = g[:, done - at :]
                else:
                    gbuf[b, :, at:end] = g
                done = end
        spread_blocks(p, gbuf, out_refs, pos_ref, other, got_refs if nr else None, turned)

    return call(
        body,
        [(s, VMEM) for s in piece_shapes(p, lanes, turned)],
        [(pos, SMEM)]
        + [(a, VMEM) for lhs, rhs, _ in pairs for a in (lhs, rhs)]
        + [(r, VMEM) for r in received or ()],
        [pltpu.VMEM((2, p.width, lanes), F32)],
        micros=2.3,
        name=name,
    )


def down_kernel(p, pos, w_up, w_down, other, active, slope, out_grad, carry):
    def body(*refs):
        nw = len(w_down)
        pos_ref, d_refs = refs[0], refs[1 : 1 + nw]
        ubuf, act_ref, slope_ref, og_ref = refs[1 + nw : 5 + nw]
        rest = list(refs[5 + nw :])
        if carry is not None:
            out_in, back_in = rest[:2]
            rest = rest[2:]
        out_ref, back_ref, low_ref, bias_ref, dbuf = rest
        gather_blocks(p, d_refs, dbuf, pos_ref, other, turned=True)
        og = og_ref[...]
        for b in range(2):
            grad = dot(og, dbuf[b]) * slope_ref[b].astype(F32)
            bias_ref[b] = jnp.sum(grad, axis=0, keepdims=True)
            low = grad.astype(BF16)
            low_ref[b] = low
            back = dot(low, ubuf[b], NT)
            out = dot(act_ref[b], dbuf[b], NT)
            if b == 0 and carry is not None:
                back_ref[...] = back_in[...] + back
                out_ref[...] = out_in[...] + out
            elif b == 0:
                back_ref[...] = back
                out_ref[...] = out
            else:
                back_ref[...] += back
                out_ref[...] += out

    ins = [(pos, SMEM)] + [(w, VMEM) for w in w_down]
    ins += [(a, VMEM) for a in (w_up, active, slope, out_grad)]
    if carry is not None:
        ins += [(a, VMEM) for a in carry]
    return call(
        body,
        [
            (sds((p.pad, p.width), F32), VMEM),
            (sds((p.pad, p.width), F32), VMEM),
            (sds((2, p.pad, p.hid), BF16), VMEM),
            (sds((2, 1, p.hid), F32), VMEM),
        ],
        ins,
        [pltpu.VMEM((2, p.width, p.hid), BF16)],
        micros=5.0,
        name="down",
    )


def middle_kernel(p, out_grad, mixed, back_sum, sel_gate, gain_two):
    def body(og_ref, mix_ref, back_ref, sg_ref, g2_ref, mg_ref, br_ref):
        xhat, rstd = norm_parts(mix_ref[...])
        mg = og_ref[...].astype(F32) + norm_back(back_ref[...] * g2_ref[...], xhat, rstd)
        mg_ref[...] = mg
        br_ref[...] = (sg_ref[...] * mg).astype(BF16)

    return call(
        body,
        [(sds((p.pad, p.width), F32), VMEM), (sds((p.pad, p.width), BF16), VMEM)],
        [(a, VMEM) for a in (out_grad, mixed, back_sum, sel_gate, gain_two)],
        micros=2.0,
        name="middle",
    )


def attention_values(p, weights, branch, probs):
    win, pad, lh, hd = p.win, p.pad, p.local_heads, p.hd
    lead = p.cw - p.cols

    def body(w_ref, br_ref, prob_ref, dc_ref, dv_ref, bias_ref, gv):
        for b in range(2):
            dc_ref[b] = dot(br_ref[...], w_ref[b, :, : p.cw]).astype(BF16)
            gv[...] = jnp.zeros((pad, p.cw), F32)
            for img in range(p.images):
                here = slice(p.base[img], p.base[img] + win)
                got = [jnp.zeros((win, lead), F32)] if lead else []
                for j in range(lh):
                    prob = prob_ref[(b * p.images + img) * lh + j]
                    got.append(dot(prob, dc_ref[b, here, hd * j : hd * j + hd], TN))
                gv[here, :] += jnp.concatenate(got, axis=1)
            full = gv[...]
            bias_ref[b] = jnp.sum(full, axis=0, keepdims=True)
            dv_ref[b] = full.astype(BF16)

    return call(
        body,
        [
            (sds((2, pad, p.cw), BF16), VMEM),
            (sds((2, pad, p.cw), BF16), VMEM),
            (sds((2, 1, p.cw), F32), VMEM),
        ],
        [(a, VMEM) for a in (weights, branch, probs)],
        [pltpu.VMEM((pad, p.cw), F32)],
        micros=2.5,
        name="attn_values",
    )


def attention_backward(p, weights, dc, dv, qkv, probs, carry):
    win, pad, lh, hd, cols = p.win, p.pad, p.local_heads, p.hd, p.cols
    lead = p.cw - p.cols

    def body(*refs):
        w_ref, dc_ref, dv_ref, qkv_ref, prob_ref = refs[:5]
        rest = list(refs[5:])
        if carry is not None:
            carry_ref, rest = rest[0], rest[1:]
        low_ref, n1_ref, bias_ref, gq = rest
        total = None
        for b in range(2):
            gq[...] = jnp.zeros((pad, 2 * cols), F32)
            for img in range(p.images):
                first = p.base[img]
                here = slice(first, first + win)
                dqs, dks = [], []
                for j in range(lh):
                    qs = p.lo + hd * j
                    q = qkv_ref[b, here, qs : qs + hd]
                    k = qkv_ref[b, here, qs + cols : qs + cols + hd]
                    v = qkv_ref[b, here, qs + 2 * cols : qs + 2 * cols + hd]
                    d = dc_ref[b, here, hd * j : hd * j + hd]
                    soft = prob_ref[(b * p.images + img) * lh + j].astype(F32)
                    if p.exact:
                        pg = dot(d * jnp.asarray(p.scale, BF16), v, NT)
                    else:
                        pg = dot(d, v, NT) * p.scale
                    row = jnp.sum(soft * pg, axis=-1, keepdims=True)
                    s = (soft * (pg - row)).astype(BF16)
                    dqs.append(dot(s, k))
                    dks.append(dot(s, q, TN))
                gq[here, :] += jnp.concatenate(dqs + dks, axis=1)
            full = gq[...]
            bias_ref[b] = jnp.sum(full, axis=0, keepdims=True)
            low = full.astype(BF16)
            low_ref[b] = low
            start = [jnp.zeros((pad, p.lo), BF16)] if p.lo else []
            gl = jnp.concatenate(start + [low, dv_ref[b][:, lead:]], axis=1)
            part = dot(gl, w_ref[b, :, p.off :], NT)
            total = part if total is None else total + part
        if carry is not None:
            total = total + carry_ref[...]
        n1_ref[...] = total

    ins = [(a, VMEM) for a in (weights, dc, dv, qkv, probs)]
    if carry is not None:
        ins.append((carry, VMEM))
    return call(
        body,
        [
            (sds((2, pad, 2 * cols), BF16), VMEM),
            (sds((pad, p.width), F32), VMEM),
            (sds((2, 1, 2 * cols), F32), VMEM),
        ],
        ins,
        [pltpu.VMEM((pad, 2 * cols), F32)],
        micros=6.0,
        name="attn_bwd",
    )


def exit_kernel(p, arrays, query, value, up):
    names = tuple(arrays)
    half = p.cols
    at = p.cw - p.cols

    def body(*refs):
        a = dict(zip(names, refs))
        rest = list(refs[len(names) :])
        q_refs, v_refs, u_refs = (rest[i * p.pairs : (i + 1) * p.pairs] for i in range(3))
        tok_ref, out_ref, *vec_refs = rest[3 * p.pairs :]
        mixed = a["mixed"][...]
        tok_ref[...] = (mixed + a["out"][...] + a["b_down"][...])[: p.rows].astype(BF16)
        xhat, _ = norm_parts(mixed)
        back = a["back"][...]
        g_gain2 = jnp.sum(back * xhat, axis=0, keepdims=True)
        g_shift2 = jnp.sum(back, axis=0, keepdims=True)
        mg, gate, sel = a["mixed_grad"][...], a["gate"][...], a["sel"][...]
        g_out = jnp.sum((sel * gate) * mg, axis=0, keepdims=True)
        rows = jnp.sum(mg * a["attended"][...], axis=-1, keepdims=True)
        logit = sel * rows * gate * (1.0 - gate)
        xhat, rstd = norm_parts(a["patches"][...].astype(F32))
        normed = xhat * a["gain_one"][...] + a["shift_one"][...]
        g_router = jnp.sum(normed * logit, axis=0, keepdims=True)
        grad = a["input"][...] + logit * a["router"][...]
        g_gain1 = jnp.sum(grad * xhat, axis=0, keepdims=True)
        g_shift1 = jnp.sum(grad, axis=0, keepdims=True)
        total = mg + norm_back(grad * a["gain_one"][...], xhat, rstd)
        out_ref[...] = total[: p.rows].astype(BF16)
        common = [g_gain1, g_shift1, g_router, g_out, g_gain2, g_shift2, a["g_down"][...]]
        for i in range(p.pairs):
            vec = vec_refs[i]
            vec[...] = jnp.zeros(vec.shape, F32)
            for j, r in enumerate(common):
                vec[j : j + 1, :] = r
            for b in range(2):
                row = 8 + 2 * b
                vec[row : row + 1, : 2 * half] = q_refs[i][b]
                vec[row : row + 1, half : 2 * half] = v_refs[i][b][:, at:]
                vec[row + 1 : row + 2, :] = u_refs[i][b]

    return call(
        body,
        [(sds((p.rows, p.width), BF16), VMEM)] * 2
        + [(sds((12, p.width), F32), VMEM)] * p.pairs,
        [(v, VMEM) for v in list(arrays.values()) + list(query) + list(value) + list(up)],
        micros=5.0,
        name="exit",
    )


def halves_kernel(keep, got):
    def body(k_ref, g_ref, mine_ref, other_ref):
        mine_ref[...] = (k_ref[0].astype(F32) + g_ref[0].astype(F32)).astype(BF16)
        other_ref[...] = (k_ref[1].astype(F32) + g_ref[1].astype(F32)).astype(BF16)

    return call(
        body,
        [(sds(keep.shape[1:], BF16), VMEM)] * 2,
        [(keep, VMEM), (got, VMEM)],
        micros=4.0,
        name="halves",
    )


def parts_kernel(mine, got):
    def body(m_ref, g_ref, *part_refs):
        for i, ref in enumerate(part_refs):
            ref[...] = (m_ref[i].astype(F32) + g_ref[i].astype(F32)).astype(BF16)

    return call(
        body,
        [(sds(mine.shape[1:], BF16), VMEM)] * 4,
        [(mine, VMEM), (got, VMEM)],
        micros=4.0,
        name="parts",
    )


def total_kernel(pieces, cuts):
    def body(*refs):
        total = sum((r[...].astype(F32) for r in refs[1:4]), refs[0][...].astype(F32))
        for (first, last, turned), ref in zip(cuts, refs[4:]):
            part = total[:, first:last]
            ref[...] = part.T if turned else part

    rows = pieces[0].shape[0]
    return call(
        body,
        [(sds((b - a, rows) if t else (rows, b - a), F32), VMEM) for a, b, t in cuts],
        [(v, VMEM) for v in pieces],
        micros=4.0,
        name="total",
    )


def flat(z, x, y, c):
    return ((z * 2 + x) * 2 + y) * 2 + c


def table(move):
    pairs = []
    for z in range(4):
        for x in range(2):
            for y in range(2):
                for c in range(2):
                    pairs.append((flat(z, x, y, c), flat(*move(z, x, y, c))))
    return pairs


def send(v, move):
    return lax.ppermute(v, ("dp", "head"), table(move))


def along_z(shift):
    return lambda z, x, y, c: ((z + shift) % 4, x, y, c)


def near(z, x, y, c):
    return (z, x ^ 1, y, c) if c == 0 else (z, x, y ^ 1, c)


def far(z, x, y, c):
    return (z, x, y ^ 1, c) if c == 0 else (z, x ^ 1, y, c)


def core(z, x, y, c):
    return (z, x, y, c ^ 1)


def after(v, *others):
    return lax.optimization_barrier((v,) + others)[0]


def add(a, b):
    return (a.astype(F32) + b.astype(F32)).astype(BF16)


def gather_whole(p, shard):
    full = lax.all_gather(lax.all_gather(shard, "dp", axis=0, tiled=True), "head", axis=0)
    return [(full[2 * i : 2 * i + 2],) for i in range(p.pairs)]


def own_pieces(shard):
    return jnp.stack([shard] + [send(shard, along_z(s)) for s in (1, 2, 3)])


def both_cores(eight, rest, *others):
    eight_out, rest_out = after(eight, *others), after(rest, *others)
    return [(eight, rest), (send(eight_out, core), send(rest_out, core))]


def scatter_whole(p, grads):
    stacked = jnp.concatenate(grads, axis=0)
    part = lax.psum_scatter(stacked, "head", scatter_dimension=0, tiled=False)
    return lax.psum_scatter(part, "dp", scatter_dimension=0, tiled=True).astype(F32)


class Scatter:
    def __init__(self, keep, away):
        self.keep, self.away = keep, away

    def first(self, *others):
        got = after(send(self.away, far), *others)
        self.mine, self.other = halves_kernel(self.keep, got)

    def second(self, *others):
        got = after(send(self.other, near), *others)
        self.pieces = parts_kernel(self.mine, got)


def along_chips(pieces, *others):
    return [pieces[0]] + [after(send(pieces[s], along_z(-s)), *others) for s in (1, 2, 3)]


def gather_head(p, vector):
    if not p.fast:
        return lax.all_gather(vector, "head", axis=0)
    pair = jnp.stack([vector, send(vector, lambda z, x, y, c: (z, x, y ^ 1, c))])
    return jnp.concatenate([pair, send(pair, core)], axis=0)


def sum_vectors(p, vecs):
    total = lax.psum(vecs[0][:8], ("dp", "head"))
    owned = jnp.concatenate([v[8:] for v in vecs]).reshape(p.head, 2, p.width)
    mine = lax.psum_scatter(owned, "head", scatter_dimension=0, tiled=False)
    return jnp.concatenate([total, lax.psum(mine, "dp")])


class VectorSum:
    def __init__(self, vecs):
        self.keep, self.away = vecs

    def over_cores(self, *others):
        self.vec = self.keep + send(after(self.away, *others), core)

    def over_z(self, step, *others):
        got = send(self.vec, lambda z, x, y, c: (z ^ step, x, y, c))
        self.vec = self.vec + after(got, *others)

    def over_xy(self, *others):
        mine, away = self.vec[:10], jnp.concatenate([self.vec[:8], self.vec[10:]])
        along_x = send(mine, lambda z, x, y, c: (z, x ^ 1, y, c))
        along_y = send(away, lambda z, x, y, c: (z, x, y ^ 1, c))
        across = send(away, lambda z, x, y, c: (z, x ^ 1, y ^ 1, c))
        along_x, along_y, across = (after(v, *others) for v in (along_x, along_y, across))
        return (mine + along_x) + (along_y + across)


def on_device(
    patches, selected, out_grad, gain_one, shift_one, router_w, w_query, b_query, w_key, w_value,
    b_value, w_out, b_out, gain_two, shift_two, w_up, b_up, w_down, b_down,
):
    images, seq = selected.shape
    rows, width = patches.shape
    dp, head = lax.axis_size("dp"), lax.axis_size("head")
    p = Plan(rows, seq, images, width, b_up.shape[0] * head, dp, head)
    cols, hid = p.cols, p.hid

    dp_pos, head_pos = lax.axis_index("dp"), lax.axis_index("head")
    pos = jnp.stack([dp_pos // 2, dp_pos % 2, head_pos % 2]).astype(jnp.int32)

    attn_shard = jnp.concatenate([w_out.T, w_query, w_key, w_value], axis=1)
    bias_parts = after(jnp.concatenate([b_query, b_value, b_up]), attn_shard)
    biases = gather_head(p, bias_parts).astype(F32)
    zeros = jnp.zeros((head, cols), F32)
    qkv_bias = jnp.concatenate(
        [zeros[:, : p.lo], biases[:, :cols], zeros, biases[:, cols : 2 * cols]], axis=1
    )[:, None, :]
    up_bias = biases[:, 2 * cols :][:, None, :]

    def row(v):
        return v.astype(F32)[None, :]

    more = p.pad - rows
    x_pad = jnp.pad(patches, ((0, more), (0, 0)))
    og_pad = jnp.pad(out_grad, ((0, more), (0, 0)))
    sel = selected.astype(F32)
    sel_col = jnp.pad(sel.reshape(rows, 1), ((0, more), (0, 0)))
    key_mask = jnp.stack(
        [
            jnp.pad(sel[i], (seq * i - p.base[i], p.win - seq - (seq * i - p.base[i])))
            for i in range(images)
        ]
    )[:, None, :]
    gain_one, shift_one, gain_two, shift_two = map(row, (gain_one, shift_one, gain_two, shift_two))
    router, b_out, b_down = row(router_w), row(b_out), row(b_down)

    fast = p.fast
    if fast:
        down_one = w_down.T
        down_near = send(down_one, near)
        attn_own = after(own_pieces(attn_shard), biases, down_near)
        x_in = after(x_pad, attn_own)
        rows_low, gate, g_down_bias = entry_kernel(p, x_in, og_pad, gain_one, shift_one, router)
        up_one = after(w_up, attn_own)
        up_z = [send(up_one, along_z(s)) for s in (1, 2, 3)]
        attn_eight = after(jnp.stack([attn_own, send(attn_own, near)]), rows_low, up_z[0])
        attn_rest = send(attn_eight, far)
        attn_w = both_cores(attn_eight, attn_rest)
        up_own = after(jnp.stack([w_up] + up_z), attn_eight)
        down_pair = after(jnp.stack([down_one, down_near]), up_own)
        down_z = [send(down_pair, along_z(s)) for s in (1, 2, 3)]
        up_eight = after(jnp.stack([up_own, send(up_own, near)]), attn_rest)
        up_rest = send(up_eight, far)
        attn_w[1] = tuple(after(w, up_rest) for w in attn_w[1])
        up_w = both_cores(up_eight, up_rest)
    else:
        rows_low, gate, g_down_bias = entry_kernel(p, x_pad, og_pad, gain_one, shift_one, router)
        attn_w, up_w, down_w = (gather_whole(p, v) for v in (attn_shard, w_up, w_down.T))
    sel_gate = gate * sel_col

    qkvs, probs, ctxs, attn_full, carry = [], [], [], [], None
    for i in range(p.pairs):
        tail = (x_pad, sel_gate, b_out, gain_two, shift_two) if i == p.pairs - 1 else None
        if fast and i == 1:
            down_eight = jnp.stack([down_pair] + [after(v, carry) for v in down_z])
            down_rest = send(down_eight, far)
        got = attention_forward(
            p, pos, attn_w[i], i, rows_low, qkv_bias[2 * i : 2 * i + 2], key_mask, carry, tail
        )
        qkvs.append(got[0])
        probs.append(got[1])
        ctxs.append(got[2])
        carry = got[3]
        attn_full.append(got[4])
    attended, mixed, mlp_in = got[3], got[5], got[6]

    def up(i, rows):
        return up_kernel(p, pos, up_w[i], i, rows, up_bias[2 * i : 2 * i + 2])

    def values(i, branch):
        return attention_values(p, attn_full[i], branch, probs[i])

    def backward(i, dc, dv, carry):
        return attention_backward(p, attn_full[i], dc, dv, qkvs[i], probs[i], carry)

    def grads(pairs, received, name, other):
        return weight_grad(p, pos, other, pairs, received, name)

    def attention_pairs(i, dv, low):
        return [(branch, ctxs[i], 0), (rows_low, dv, p.off), (rows_low, low, 2 * cols)]

    def down(i, grad_in, carry):
        return down_kernel(p, pos, up_full[i], down_w[i], i, acts[i], slopes[i], grad_in, carry)

    def leave(back, qsums, vsums, up_sums):
        arrays = dict(
            patches=x_pad, mixed=mixed, out=out_sum, back=back_sum, mixed_grad=mixed_grad,
            attended=attended, input=back, gate=gate, sel=sel_col, gain_one=gain_one,
            shift_one=shift_one, router=router, b_down=b_down, g_down=g_down_bias,
        )
        return exit_kernel(p, arrays, qsums, vsums, up_sums)

    if fast:
        act1, slope1, full1 = up(1, mlp_in)
        gd1 = grads([(og_pad, act1, 0)], None, "grad_down", 1)
        gd1_got = [send(o, core) for o in gd1]
        act0, slope0, full0 = up(0, after(mlp_in, *gd1))
        acts, slopes, up_full = (act0, act1), (slope0, slope1), (full0, full1)
        down_w = both_cores(down_eight, down_rest, act0)
        gd0 = grads([(og_pad, act0, 0)], gd1_got, "grad_down", 0)
        out_sum, back_sum, low0, sum0 = down(0, after(og_pad, *gd0), None)
        down_sum = Scatter(*gd0)
        out_sum, back_sum, low1, sum1 = down(1, after(og_pad, *gd0), (out_sum, back_sum))
        mixed_grad, branch = middle_kernel(p, og_pad, mixed, back_sum, sel_gate, gain_two)
        gu1 = grads([(after(mlp_in, branch), low1, 0)], None, "grad_up", 1)
        gu1_got = [send(o, core) for o in gu1]
        dc1, dv1, vsum1 = values(1, after(branch, *gu1))
        dc0, dv0, vsum0 = values(0, after(branch, dv1))
        down_sum.first()
        gu1_got = [after(g, dv0, down_sum.other) for g in gu1_got]
        gu0 = grads([(mlp_in, low0, 0)], gu1_got, "grad_up", 0)
        up_sum = Scatter(*gu0)
        low1, carry, qsum1 = backward(1, after(dc1, *gu0), dv1, None)
        ga1 = grads(attention_pairs(1, dv1, low1), None, "grad_attn", 1)
        ga1_got = [send(o, core) for o in ga1]
        down_sum.second()
        low0, carry, qsum0 = backward(0, after(dc0, *ga1, *down_sum.pieces), dv0, carry)
        up_sum.first(low0)
        ga1_got = [after(g, up_sum.other) for g in ga1_got]
        ga0 = grads(attention_pairs(0, dv0, low0), ga1_got, "grad_attn", 0)
        attn_sum = Scatter(*ga0)
        carry = after(carry, *ga0)
        tokens, grad_patches, *vecs = leave(carry, (qsum0, qsum1), (vsum0, vsum1), (sum0, sum1))
        vec_sum = VectorSum(vecs)
        down_parts = along_chips(down_sum.pieces, grad_patches)
        up_sum.second(*down_parts)
        vec_sum.over_cores(*up_sum.pieces)
        attn_sum.first(vec_sum.vec)
        down_parts[0] = after(down_parts[0], attn_sum.other)
        (grad_down,) = total_kernel(down_parts, [(0, p.hid, True)])
        up_parts = along_chips(up_sum.pieces, grad_down)
        vec_sum.over_z(1, *up_parts)
        attn_sum.second(vec_sum.vec)
        vec_sum.over_z(2, *attn_sum.pieces)
        up_parts[0] = after(up_parts[0], *attn_sum.pieces)
        (grad_up,) = total_kernel(up_parts, [(0, p.hid, False)])
        attn_parts = along_chips(attn_sum.pieces, grad_up)
        summed = vec_sum.over_xy(grad_up)
        grad_out, grad_value, grad_query, grad_key = total_kernel(
            attn_parts, [(i * cols, (i + 1) * cols, i == 0) for i in range(4)]
        )
    else:
        acts, slopes, up_full = zip(*(up(i, mlp_in) for i in range(p.pairs)))
        carry, lows, up_sums = None, [], []
        for i in range(p.pairs):
            got = down(i, og_pad, carry)
            carry = (got[0], got[1])
            lows.append(got[2])
            up_sums.append(got[3])
        out_sum, back_sum = carry
        mixed_grad, branch = middle_kernel(p, og_pad, mixed, back_sum, sel_gate, gain_two)
        carry, blocks, vsums, qsums = None, [], [], []
        for i in range(p.pairs):
            dc, dv, vsum = values(i, branch)
            low, carry, qsum = backward(i, dc, dv, carry)
            blocks += grads(attention_pairs(i, dv, low), None, "grad_attn", 0)
            vsums.append(vsum)
            qsums.append(qsum)
        tokens, grad_patches, *vecs = leave(carry, qsums, vsums, up_sums)
        grad_down, grad_up, grad_attn = (
            scatter_whole(p, g)
            for g in (
                [grads([(og_pad, a, 0)], None, "grad_down", 0)[0] for a in acts],
                [grads([(mlp_in, v, 0)], None, "grad_up", 0)[0] for v in lows],
                blocks,
            )
        )
        grad_down = grad_down.T
        grad_out, grad_value, grad_query, grad_key = (
            grad_attn[:, i * cols : (i + 1) * cols] for i in range(4)
        )
        grad_out = grad_out.T
        summed = sum_vectors(p, vecs)

    vecs = [summed[i] for i in range(7)]
    owned, hidden_sum = summed[8], summed[9]
    return (
        tokens,
        grad_patches,
        vecs[0],
        vecs[1],
        vecs[2],
        grad_query,
        owned[:cols],
        grad_key,
        grad_value,
        owned[cols : 2 * cols],
        grad_out,
        vecs[3],
        vecs[4],
        vecs[5],
        grad_up,
        hidden_sum,
        grad_down,
        vecs[6],
    )


def solution(mesh):
    rows, rep = P(("dp", "head"), None), P()
    split, side, turned = P("dp", "head"), P("head"), P("head", "dp")
    return jax.shard_map(
        on_device,
        mesh=mesh,
        in_specs=(
            rows, rows, rows, rep, rep, rep, split, side, split, split, side, turned, rep, rep,
            rep, split, side, turned, rep,
        ),
        out_specs=(
            rows, rows, rep, rep, rep, split, side, split, split, side, turned, rep, rep, rep,
            split, side, turned, rep,
        ),
        check_vma=False,
    )
```

```python
import math

import jax
import jax.numpy as jnp
from jax import lax
from jax.experimental import pallas as pl
from jax.experimental.pallas import tpu as pltpu
from jax.sharding import PartitionSpec as P

HEADS = 12
EPS = 1e-06
F32 = jnp.float32
BF16 = jnp.bfloat16
VMEM = pl.BlockSpec(memory_space=pltpu.VMEM)
SMEM = pl.BlockSpec(memory_space=pltpu.SMEM)
EXIT = 2.0
WEIGHT = 4.0e9
LIMIT = 20 * 1024 * 1024
INV_SQRT2 = 0.7071067811865476
INV_SQRT2PI = 0.3989422804014327

NN = (((1,), (0,)), ((), ()))
NT = (((1,), (1,)), ((), ()))
TN = (((0,), (0,)), ((), ()))


def dot(a, b, dims=NN):
    return lax.dot_general(a, b, dims, preferred_element_type=F32)


def sds(shape, dtype):
    return jax.ShapeDtypeStruct(shape, dtype)


def call(body, outs, ins, scratch=(), micros=1.0, name=None):
    return pl.pallas_call(
        body,
        out_shape=[o for o, _ in outs],
        in_specs=[s for _, s in ins],
        out_specs=[s for _, s in outs],
        scratch_shapes=list(scratch),
        compiler_params=pltpu.CompilerParams(vmem_limit_bytes=LIMIT),
        cost_estimate=pl.CostEstimate(
            flops=int(micros * WEIGHT), bytes_accessed=0, transcendentals=0
        ),
        name=name,
    )(*[a for a, _ in ins])


def norm_parts(v):
    center = v - jnp.mean(v, axis=-1, keepdims=True)
    spread = jnp.mean(center * center, axis=-1, keepdims=True)
    rstd = lax.rsqrt(spread + EPS)
    return center * rstd, rstd


def norm_back(u, xhat, rstd):
    return rstd * (
        u
        - jnp.mean(u, axis=-1, keepdims=True)
        - xhat * jnp.mean(u * xhat, axis=-1, keepdims=True)
    )


class Plan:
    def __init__(self, rows, seq, images, width, hidden, dp, head):
        self.rows, self.seq, self.images, self.width = rows, seq, images, width
        self.dp, self.head = dp, head
        self.pairs = head // 2
        self.cols = width // head
        self.hid = hidden // head
        self.hd = width // HEADS
        self.local_heads = HEADS // head
        self.piece = width // dp
        self.fast = dp == 8 and head == 4 and self.piece % 16 == 0
        self.base = [seq * i // 16 * 16 for i in range(images)]
        self.win = max(-(-(seq * (i + 1) - self.base[i]) // 16) * 16 for i in range(images))
        self.pad = self.base[-1] + self.win
        self.off = self.cols // 128 * 128
        self.lo = self.cols - self.off
        self.nq = 4 * self.cols - self.off
        self.cw = -(-self.cols // 128) * 128
        self.scale = 1.0 / math.sqrt(self.hd)
        self.exact = math.log2(self.scale).is_integer()


def source_rows(p, pos_ref, zz, xx):
    z, x = pos_ref[0], pos_ref[1]
    part = ((z - zz) & 3) * 2 + (x ^ xx)
    return pl.multiple_of(part * p.piece, p.piece)


def piece_list(p, pos_ref, other):
    core = pos_ref[2] ^ other
    found = []
    for b3 in range(2):
        for b2 in range(2):
            yy = jnp.where(core == 0, b3, b2)
            xx = jnp.where(core == 0, b2, b3)
            for zz in range(4):
                found.append((b3, b2, zz, yy, source_rows(p, pos_ref, zz, xx)))
    return found


def gather_blocks(p, refs, buf, pos_ref, other, lanes=slice(None), turned=False):
    if not p.fast:
        buf[...] = refs[0][:, :, lanes]
        return
    for b3, b2, zz, yy, row in piece_list(p, pos_ref, other):
        i, j = (zz, b2) if turned else (b2, zz)
        buf[yy, pl.ds(row, p.piece), :] = refs[b3][i, j, :, lanes]


def spread_blocks(p, buf, refs, pos_ref, other, received=None, turned=False):
    if not p.fast:
        refs[0][...] = buf[...].astype(BF16)
        return
    for b3, b2, zz, yy, row in piece_list(p, pos_ref, other):
        i, j = (zz, b2) if turned else (b2, zz)
        part = buf[yy, pl.ds(row, p.piece), :]
        if received is not None:
            part = part + received[b3][i, j].astype(F32)
        refs[b3][i, j] = part.astype(BF16)


def piece_shapes(p, lanes, turned=False):
    if p.fast:
        return [sds(((4, 2) if turned else (2, 4)) + (p.piece, lanes), BF16)] * 2
    return [sds((2, p.width, lanes), BF16)]


def entry_kernel(p, patches, out_grad, gain_one, shift_one, router):
    def body(x_ref, og_ref, g_ref, s_ref, r_ref, low_ref, gate_ref, down_ref):
        xhat, _ = norm_parts(x_ref[...].astype(F32))
        normed = xhat * g_ref[...] + s_ref[...]
        low_ref[...] = normed.astype(BF16)
        logit = jnp.sum(normed * r_ref[...], axis=-1, keepdims=True)
        gate_ref[...] = 1.0 / (1.0 + jnp.exp(-logit))
        down_ref[...] = jnp.sum(og_ref[...].astype(F32), axis=0, keepdims=True)

    return call(
        body,
        [
            (sds((p.pad, p.width), BF16), VMEM),
            (sds((p.pad, 1), F32), VMEM),
            (sds((1, p.width), F32), VMEM),
        ],
        [(a, VMEM) for a in (patches, out_grad, gain_one, shift_one, router)],
        micros=0.7,
        name="entry",
    )


def attention_forward(p, pos, weights, other, rows_low, bias, key_mask, carry, tail):
    last = tail is not None
    win, pad, lh, hd = p.win, p.pad, p.local_heads, p.hd

    def body(*refs):
        nw = len(weights)
        pos_ref, w_refs = refs[0], refs[1 : 1 + nw]
        rest = list(refs[1 + nw :])
        low_ref, bias_ref, mask_ref = rest[:3]
        rest = rest[3:]
        carry_ref = None
        if carry is not None:
            carry_ref, rest = rest[0], rest[1:]
        if last:
            x_ref, sg_ref, bo_ref, g2_ref, s2_ref = rest[:5]
            rest = rest[5:]
            qkv_ref, prob_ref, ctx_ref, att_ref, wbuf, mixed_ref, in_ref = rest[:7]
        else:
            qkv_ref, prob_ref, ctx_ref, att_ref, wbuf = rest[:5]
        ctx = rest[-1]
        gather_blocks(p, w_refs, wbuf, pos_ref, other)
        low = low_ref[...]
        total = None
        for b in range(2):
            qkv = dot(low, wbuf[b, :, p.off :]) + bias_ref[b]
            qkv_ref[b] = qkv.astype(BF16)
            ctx[...] = jnp.zeros((pad, p.cw), F32)
            for img in range(p.images):
                first = p.base[img]
                at = lax.broadcasted_iota(jnp.int32, (win, 1), 0) + first
                valid = (at >= p.seq * img) & (at < p.seq * (img + 1))
                seen = mask_ref[img] > 0.0
                got = []
                for j in range(lh):
                    qs = p.lo + hd * j
                    q = qkv_ref[b, first : first + win, qs : qs + hd]
                    k = qkv_ref[b, first : first + win, qs + p.cols : qs + p.cols + hd]
                    v = qkv_ref[b, first : first + win, qs + 2 * p.cols : qs + 2 * p.cols + hd]
                    if p.exact:
                        s = dot(q * jnp.asarray(p.scale, BF16), k, NT)
                    else:
                        s = dot(q, k, NT) * p.scale
                    s = jnp.where(seen, s, -1e30)
                    e = jnp.exp(s - jnp.max(s, axis=-1, keepdims=True))
                    share = jnp.where(valid, 1.0 / jnp.sum(e, axis=-1, keepdims=True), 0.0)
                    prob = (e * share).astype(BF16)
                    prob_ref[(b * p.images + img) * lh + j] = prob
                    got.append(dot(prob, v))
                if p.cw > p.cols:
                    got.append(jnp.zeros((win, p.cw - p.cols), F32))
                ctx[first : first + win, :] += jnp.concatenate(got, axis=1)
            mix = ctx[...].astype(BF16)
            ctx_ref[b] = mix
            part = dot(mix, wbuf[b, :, : p.cw], NT)
            total = part if total is None else total + part
        if carry_ref is not None:
            total = total + carry_ref[...]
        if not last:
            att_ref[...] = total
            return
        attended = total + bo_ref[...]
        att_ref[...] = attended
        mixed = x_ref[...].astype(F32) + sg_ref[...] * attended
        mixed_ref[...] = mixed
        xhat, _ = norm_parts(mixed)
        in_ref[...] = (xhat * g2_ref[...] + s2_ref[...]).astype(BF16)

    ins = [(pos, SMEM)] + [(w, VMEM) for w in weights]
    ins += [(a, VMEM) for a in (rows_low, bias, key_mask)]
    if carry is not None:
        ins.append((carry, VMEM))
    if last:
        ins += [(a, VMEM) for a in tail]
    outs = [
        (sds((2, pad, p.nq), BF16), VMEM),
        (sds((2 * p.images * lh, win, win), BF16), VMEM),
        (sds((2, pad, p.cw), BF16), VMEM),
        (sds((pad, p.width), F32), VMEM),
        (sds((2, p.width, 4 * p.cols), BF16), VMEM),
    ]
    if last:
        outs += [(sds((pad, p.width), F32), VMEM), (sds((pad, p.width), BF16), VMEM)]
    return call(
        body,
        outs,
        ins,
        [pltpu.VMEM((pad, p.cw), F32)],
        micros=5.5,
        name="attn_fwd",
    )


def up_kernel(p, pos, weights, other, mlp_in, bias):
    def body(*refs):
        nw = len(weights)
        pos_ref, w_refs = refs[0], refs[1 : 1 + nw]
        in_ref, b_ref, act_ref, slope_ref, wbuf = refs[1 + nw :]
        gather_blocks(p, w_refs, wbuf, pos_ref, other)
        rows = in_ref[...]
        for b in range(2):
            pre = dot(rows, wbuf[b]) + b_ref[b]
            phi = 0.5 * (1.0 + lax.erf(pre * INV_SQRT2))
            act_ref[b] = (pre * phi).astype(BF16)
            slope_ref[b] = (phi + pre * (jnp.exp(-0.5 * pre * pre) * INV_SQRT2PI)).astype(BF16)

    return call(
        body,
        [(sds((2, p.pad, p.hid), BF16), VMEM)] * 2 + [(sds((2, p.width, p.hid), BF16), VMEM)],
        [(pos, SMEM)] + [(w, VMEM) for w in weights] + [(mlp_in, VMEM), (bias, VMEM)],
        micros=2.5,
        name="up",
    )


def weight_grad(p, pos, other, pairs, received, name, turned=False):
    lanes = max(at + rhs.shape[2] for _, rhs, at in pairs)
    starts = [at for _, _, at in pairs]

    def body(*refs):
        pos_ref, rest = refs[0], list(refs[1:])
        ops, rest = rest[: 2 * len(pairs)], rest[2 * len(pairs) :]
        nr = len(received) if received is not None else 0
        got_refs, rest = rest[:nr], rest[nr:]
        out_refs, gbuf = rest[:-1], rest[-1]
        turned_lhs = {}
        for i, (lhs, _, _) in enumerate(pairs):
            if id(lhs) not in turned_lhs:
                turned_lhs[id(lhs)] = ops[2 * i][...].T
        for b in range(2):
            done = 0
            for i, at in enumerate(starts):
                g = dot(turned_lhs[id(pairs[i][0])], ops[2 * i + 1][b])
                end = at + g.shape[1]
                if at < done:
                    gbuf[b, :, at:done] += g[:, : done - at]
                    gbuf[b, :, done:end] = g[:, done - at :]
                else:
                    gbuf[b, :, at:end] = g
                done = end
        spread_blocks(p, gbuf, out_refs, pos_ref, other, got_refs if nr else None, turned)

    return call(
        body,
        [(s, VMEM) for s in piece_shapes(p, lanes, turned)],
        [(pos, SMEM)]
        + [(a, VMEM) for lhs, rhs, _ in pairs for a in (lhs, rhs)]
        + [(r, VMEM) for r in received or ()],
        [pltpu.VMEM((2, p.width, lanes), F32)],
        micros=2.3,
        name=name,
    )


def down_kernel(p, pos, w_up, w_down, other, active, slope, out_grad, carry):
    def body(*refs):
        nw = len(w_down)
        pos_ref, d_refs = refs[0], refs[1 : 1 + nw]
        ubuf, act_ref, slope_ref, og_ref = refs[1 + nw : 5 + nw]
        rest = list(refs[5 + nw :])
        if carry is not None:
            out_in, back_in = rest[:2]
            rest = rest[2:]
        out_ref, back_ref, low_ref, bias_ref, dbuf = rest
        gather_blocks(p, d_refs, dbuf, pos_ref, other, turned=True)
        og = og_ref[...]
        for b in range(2):
            grad = dot(og, dbuf[b]) * slope_ref[b].astype(F32)
            bias_ref[b] = jnp.sum(grad, axis=0, keepdims=True)
            low = grad.astype(BF16)
            low_ref[b] = low
            back = dot(low, ubuf[b], NT)
            out = dot(act_ref[b], dbuf[b], NT)
            if b == 0 and carry is not None:
                back_ref[...] = back_in[...] + back
                out_ref[...] = out_in[...] + out
            elif b == 0:
                back_ref[...] = back
                out_ref[...] = out
            else:
                back_ref[...] += back
                out_ref[...] += out

    ins = [(pos, SMEM)] + [(w, VMEM) for w in w_down]
    ins += [(a, VMEM) for a in (w_up, active, slope, out_grad)]
    if carry is not None:
        ins += [(a, VMEM) for a in carry]
    return call(
        body,
        [
            (sds((p.pad, p.width), F32), VMEM),
            (sds((p.pad, p.width), F32), VMEM),
            (sds((2, p.pad, p.hid), BF16), VMEM),
            (sds((2, 1, p.hid), F32), VMEM),
        ],
        ins,
        [pltpu.VMEM((2, p.width, p.hid), BF16)],
        micros=5.0,
        name="down",
    )


def middle_kernel(p, out_grad, mixed, back_sum, sel_gate, gain_two):
    def body(og_ref, mix_ref, back_ref, sg_ref, g2_ref, mg_ref, br_ref):
        xhat, rstd = norm_parts(mix_ref[...])
        mg = og_ref[...].astype(F32) + norm_back(back_ref[...] * g2_ref[...], xhat, rstd)
        mg_ref[...] = mg
        br_ref[...] = (sg_ref[...] * mg).astype(BF16)

    return call(
        body,
        [(sds((p.pad, p.width), F32), VMEM), (sds((p.pad, p.width), BF16), VMEM)],
        [(a, VMEM) for a in (out_grad, mixed, back_sum, sel_gate, gain_two)],
        micros=2.0,
        name="middle",
    )


def attention_values(p, weights, branch, probs):
    win, pad, lh, hd = p.win, p.pad, p.local_heads, p.hd
    lead = p.cw - p.cols

    def body(w_ref, br_ref, prob_ref, dc_ref, dv_ref, bias_ref, gv):
        for b in range(2):
            dc_ref[b] = dot(br_ref[...], w_ref[b, :, : p.cw]).astype(BF16)
            gv[...] = jnp.zeros((pad, p.cw), F32)
            for img in range(p.images):
                here = slice(p.base[img], p.base[img] + win)
                got = [jnp.zeros((win, lead), F32)] if lead else []
                for j in range(lh):
                    prob = prob_ref[(b * p.images + img) * lh + j]
                    got.append(dot(prob, dc_ref[b, here, hd * j : hd * j + hd], TN))
                gv[here, :] += jnp.concatenate(got, axis=1)
            full = gv[...]
            bias_ref[b] = jnp.sum(full, axis=0, keepdims=True)
            dv_ref[b] = full.astype(BF16)

    return call(
        body,
        [
            (sds((2, pad, p.cw), BF16), VMEM),
            (sds((2, pad, p.cw), BF16), VMEM),
            (sds((2, 1, p.cw), F32), VMEM),
        ],
        [(a, VMEM) for a in (weights, branch, probs)],
        [pltpu.VMEM((pad, p.cw), F32)],
        micros=2.5,
        name="attn_values",
    )


def attention_backward(p, weights, dc, dv, qkv, probs, carry):
    win, pad, lh, hd, cols = p.win, p.pad, p.local_heads, p.hd, p.cols
    lead = p.cw - p.cols

    def body(*refs):
        w_ref, dc_ref, dv_ref, qkv_ref, prob_ref = refs[:5]
        rest = list(refs[5:])
        if carry is not None:
            carry_ref, rest = rest[0], rest[1:]
        low_ref, n1_ref, bias_ref, gq = rest
        total = None
        for b in range(2):
            gq[...] = jnp.zeros((pad, 2 * cols), F32)
            for img in range(p.images):
                first = p.base[img]
                here = slice(first, first + win)
                dqs, dks = [], []
                for j in range(lh):
                    qs = p.lo + hd * j
                    q = qkv_ref[b, here, qs : qs + hd]
                    k = qkv_ref[b, here, qs + cols : qs + cols + hd]
                    v = qkv_ref[b, here, qs + 2 * cols : qs + 2 * cols + hd]
                    d = dc_ref[b, here, hd * j : hd * j + hd]
                    soft = prob_ref[(b * p.images + img) * lh + j].astype(F32)
                    if p.exact:
                        pg = dot(d * jnp.asarray(p.scale, BF16), v, NT)
                    else:
                        pg = dot(d, v, NT) * p.scale
                    row = jnp.sum(soft * pg, axis=-1, keepdims=True)
                    s = (soft * (pg - row)).astype(BF16)
                    dqs.append(dot(s, k))
                    dks.append(dot(s, q, TN))
                gq[here, :] += jnp.concatenate(dqs + dks, axis=1)
            full = gq[...]
            bias_ref[b] = jnp.sum(full, axis=0, keepdims=True)
            low = full.astype(BF16)
            low_ref[b] = low
            start = [jnp.zeros((pad, p.lo), BF16)] if p.lo else []
            gl = jnp.concatenate(start + [low, dv_ref[b][:, lead:]], axis=1)
            part = dot(gl, w_ref[b, :, p.off :], NT)
            total = part if total is None else total + part
        if carry is not None:
            total = total + carry_ref[...]
        n1_ref[...] = total

    ins = [(a, VMEM) for a in (weights, dc, dv, qkv, probs)]
    if carry is not None:
        ins.append((carry, VMEM))
    return call(
        body,
        [
            (sds((2, pad, 2 * cols), BF16), VMEM),
            (sds((pad, p.width), F32), VMEM),
            (sds((2, 1, 2 * cols), F32), VMEM),
        ],
        ins,
        [pltpu.VMEM((pad, 2 * cols), F32)],
        micros=6.0,
        name="attn_bwd",
    )


def exit_kernel(p, arrays, query, value, up):
    names = tuple(arrays)
    half = p.cols
    at = p.cw - p.cols

    def body(*refs):
        a = dict(zip(names, refs))
        rest = list(refs[len(names) :])
        q_refs, v_refs, u_refs = (rest[i * p.pairs : (i + 1) * p.pairs] for i in range(3))
        tok_ref, out_ref, *vec_refs = rest[3 * p.pairs :]
        mixed = a["mixed"][...]
        tok_ref[...] = (mixed + a["out"][...] + a["b_down"][...])[: p.rows].astype(BF16)
        xhat, _ = norm_parts(mixed)
        back = a["back"][...]
        g_gain2 = jnp.sum(back * xhat, axis=0, keepdims=True)
        g_shift2 = jnp.sum(back, axis=0, keepdims=True)
        mg, gate, sel = a["mixed_grad"][...], a["gate"][...], a["sel"][...]
        g_out = jnp.sum((sel * gate) * mg, axis=0, keepdims=True)
        rows = jnp.sum(mg * a["attended"][...], axis=-1, keepdims=True)
        logit = sel * rows * gate * (1.0 - gate)
        xhat, rstd = norm_parts(a["patches"][...].astype(F32))
        normed = xhat * a["gain_one"][...] + a["shift_one"][...]
        g_router = jnp.sum(normed * logit, axis=0, keepdims=True)
        grad = a["input"][...] + logit * a["router"][...]
        g_gain1 = jnp.sum(grad * xhat, axis=0, keepdims=True)
        g_shift1 = jnp.sum(grad, axis=0, keepdims=True)
        total = mg + norm_back(grad * a["gain_one"][...], xhat, rstd)
        out_ref[...] = total[: p.rows].astype(BF16)
        common = [g_gain1, g_shift1, g_router, g_out, g_gain2, g_shift2, a["g_down"][...]]
        for i in range(p.pairs):
            vec = vec_refs[i]
            vec[...] = jnp.zeros(vec.shape, F32)
            for j, r in enumerate(common):
                vec[j : j + 1, :] = r
            for b in range(2):
                row = 8 + 2 * b
                vec[row : row + 1, : 2 * half] = q_refs[i][b]
                vec[row : row + 1, half : 2 * half] = v_refs[i][b][:, at:]
                vec[row + 1 : row + 2, :] = u_refs[i][b]

    return call(
        body,
        [(sds((p.rows, p.width), BF16), VMEM)] * 2
        + [(sds((12, p.width), F32), VMEM)] * p.pairs,
        [(v, VMEM) for v in list(arrays.values()) + list(query) + list(value) + list(up)],
        micros=5.0,
        name="exit",
    )


def halves_kernel(keep, got):
    def body(k_ref, g_ref, mine_ref, other_ref):
        mine_ref[...] = (k_ref[0].astype(F32) + g_ref[0].astype(F32)).astype(BF16)
        other_ref[...] = (k_ref[1].astype(F32) + g_ref[1].astype(F32)).astype(BF16)

    return call(
        body,
        [(sds(keep.shape[1:], BF16), VMEM)] * 2,
        [(keep, VMEM), (got, VMEM)],
        micros=4.0,
        name="halves",
    )


def parts_kernel(mine, got):
    def body(m_ref, g_ref, *part_refs):
        for i, ref in enumerate(part_refs):
            ref[...] = (m_ref[i].astype(F32) + g_ref[i].astype(F32)).astype(BF16)

    return call(
        body,
        [(sds(mine.shape[1:], BF16), VMEM)] * 4,
        [(mine, VMEM), (got, VMEM)],
        micros=4.0,
        name="parts",
    )


def total_kernel(pieces, cuts):
    def body(*refs):
        total = sum((r[...].astype(F32) for r in refs[1:4]), refs[0][...].astype(F32))
        for (first, last, turned), ref in zip(cuts, refs[4:]):
            part = total[:, first:last]
            ref[...] = part.T if turned else part

    rows = pieces[0].shape[0]
    return call(
        body,
        [(sds((b - a, rows) if t else (rows, b - a), F32), VMEM) for a, b, t in cuts],
        [(v, VMEM) for v in pieces],
        micros=4.0,
        name="total",
    )


def flat(z, x, y, c):
    return ((z * 2 + x) * 2 + y) * 2 + c


def table(move):
    pairs = []
    for z in range(4):
        for x in range(2):
            for y in range(2):
                for c in range(2):
                    pairs.append((flat(z, x, y, c), flat(*move(z, x, y, c))))
    return pairs


def send(v, move):
    return lax.ppermute(v, ("dp", "head"), table(move))


def along_z(shift):
    return lambda z, x, y, c: ((z + shift) % 4, x, y, c)


def near(z, x, y, c):
    return (z, x ^ 1, y, c) if c == 0 else (z, x, y ^ 1, c)


def far(z, x, y, c):
    return (z, x, y ^ 1, c) if c == 0 else (z, x ^ 1, y, c)


def core(z, x, y, c):
    return (z, x, y, c ^ 1)


def after(v, *others):
    return lax.optimization_barrier((v,) + others)[0]


def add(a, b):
    return (a.astype(F32) + b.astype(F32)).astype(BF16)


def gather_whole(p, shard):
    full = lax.all_gather(lax.all_gather(shard, "dp", axis=0, tiled=True), "head", axis=0)
    return [(full[2 * i : 2 * i + 2],) for i in range(p.pairs)]


def own_pieces(shard):
    return jnp.stack([shard] + [send(shard, along_z(s)) for s in (1, 2, 3)])


def both_cores(eight, rest, *others):
    eight_out, rest_out = after(eight, *others), after(rest, *others)
    return [(eight, rest), (send(eight_out, core), send(rest_out, core))]


def scatter_whole(p, grads):
    stacked = jnp.concatenate(grads, axis=0)
    part = lax.psum_scatter(stacked, "head", scatter_dimension=0, tiled=False)
    return lax.psum_scatter(part, "dp", scatter_dimension=0, tiled=True).astype(F32)


class Scatter:
    def __init__(self, keep, away):
        self.keep, self.away = keep, away

    def first(self, *others):
        got = after(send(self.away, far), *others)
        self.mine, self.other = halves_kernel(self.keep, got)

    def second(self, *others):
        got = after(send(self.other, near), *others)
        self.pieces = parts_kernel(self.mine, got)


def along_chips(pieces, *others):
    return [pieces[0]] + [after(send(pieces[s], along_z(-s)), *others) for s in (1, 2, 3)]


def gather_head(p, vector):
    if not p.fast:
        return lax.all_gather(vector, "head", axis=0)
    pair = jnp.stack([vector, send(vector, lambda z, x, y, c: (z, x, y ^ 1, c))])
    return jnp.concatenate([pair, send(pair, core)], axis=0)


def sum_vectors(p, vecs):
    total = lax.psum(vecs[0][:8], ("dp", "head"))
    owned = jnp.concatenate([v[8:] for v in vecs]).reshape(p.head, 2, p.width)
    mine = lax.psum_scatter(owned, "head", scatter_dimension=0, tiled=False)
    return jnp.concatenate([total, lax.psum(mine, "dp")])


class VectorSum:
    def __init__(self, vecs):
        self.keep, self.away = vecs

    def over_cores(self, *others):
        self.vec = self.keep + send(after(self.away, *others), core)

    def over_z(self, step, *others):
        got = send(self.vec, lambda z, x, y, c: (z ^ step, x, y, c))
        self.vec = self.vec + after(got, *others)

    def over_xy(self, *others):
        mine, away = self.vec[:10], jnp.concatenate([self.vec[:8], self.vec[10:]])
        along_x = send(mine, lambda z, x, y, c: (z, x ^ 1, y, c))
        along_y = send(away, lambda z, x, y, c: (z, x, y ^ 1, c))
        across = send(away, lambda z, x, y, c: (z, x ^ 1, y ^ 1, c))
        along_x, along_y, across = (after(v, *others) for v in (along_x, along_y, across))
        return (mine + along_x) + (along_y + across)


def on_device(
    patches, selected, out_grad, gain_one, shift_one, router_w, w_query, b_query, w_key, w_value,
    b_value, w_out, b_out, gain_two, shift_two, w_up, b_up, w_down, b_down,
):
    images, seq = selected.shape
    rows, width = patches.shape
    dp, head = lax.axis_size("dp"), lax.axis_size("head")
    p = Plan(rows, seq, images, width, b_up.shape[0] * head, dp, head)
    cols, hid = p.cols, p.hid

    dp_pos, head_pos = lax.axis_index("dp"), lax.axis_index("head")
    pos = jnp.stack([dp_pos // 2, dp_pos % 2, head_pos % 2]).astype(jnp.int32)

    attn_shard = jnp.concatenate([w_out.T, w_query, w_key, w_value], axis=1)
    bias_parts = after(jnp.concatenate([b_query, b_value, b_up]), attn_shard)
    biases = gather_head(p, bias_parts).astype(F32)
    zeros = jnp.zeros((head, cols), F32)
    qkv_bias = jnp.concatenate(
        [zeros[:, : p.lo], biases[:, :cols], zeros, biases[:, cols : 2 * cols]], axis=1
    )[:, None, :]
    up_bias = biases[:, 2 * cols :][:, None, :]

    def row(v):
        return v.astype(F32)[None, :]

    more = p.pad - rows
    x_pad = jnp.pad(patches, ((0, more), (0, 0)))
    og_pad = jnp.pad(out_grad, ((0, more), (0, 0)))
    sel = selected.astype(F32)
    sel_col = jnp.pad(sel.reshape(rows, 1), ((0, more), (0, 0)))
    key_mask = jnp.stack(
        [
            jnp.pad(sel[i], (seq * i - p.base[i], p.win - seq - (seq * i - p.base[i])))
            for i in range(images)
        ]
    )[:, None, :]
    gain_one, shift_one, gain_two, shift_two = map(row, (gain_one, shift_one, gain_two, shift_two))
    router, b_out, b_down = row(router_w), row(b_out), row(b_down)

    fast = p.fast
    if fast:
        down_one = w_down.T
        down_near = send(down_one, near)
        attn_own = after(own_pieces(attn_shard), biases, down_near)
        x_in = after(x_pad, attn_own)
        rows_low, gate, g_down_bias = entry_kernel(p, x_in, og_pad, gain_one, shift_one, router)
        up_one = after(w_up, attn_own)
        up_z = [send(up_one, along_z(s)) for s in (1, 2, 3)]
        attn_eight = after(jnp.stack([attn_own, send(attn_own, near)]), rows_low, up_z[0])
        attn_rest = send(attn_eight, far)
        attn_w = both_cores(attn_eight, attn_rest)
        up_own = after(jnp.stack([w_up] + up_z), attn_eight)
        down_pair = after(jnp.stack([down_one, down_near]), up_own)
        down_z = [send(down_pair, along_z(s)) for s in (1, 2, 3)]
        up_eight = after(jnp.stack([up_own, send(up_own, near)]), attn_rest)
        up_rest = send(up_eight, far)
        attn_w[1] = tuple(after(w, up_rest) for w in attn_w[1])
        up_w = both_cores(up_eight, up_rest)
    else:
        rows_low, gate, g_down_bias = entry_kernel(p, x_pad, og_pad, gain_one, shift_one, router)
        attn_w, up_w, down_w = (gather_whole(p, v) for v in (attn_shard, w_up, w_down.T))
    sel_gate = gate * sel_col

    qkvs, probs, ctxs, attn_full, carry = [], [], [], [], None
    for i in range(p.pairs):
        tail = (x_pad, sel_gate, b_out, gain_two, shift_two) if i == p.pairs - 1 else None
        if fast and i == 1:
            down_eight = jnp.stack([down_pair] + [after(v, carry) for v in down_z])
            down_rest = send(down_eight, far)
        got = attention_forward(
            p, pos, attn_w[i], i, rows_low, qkv_bias[2 * i : 2 * i + 2], key_mask, carry, tail
        )
        qkvs.append(got[0])
        probs.append(got[1])
        ctxs.append(got[2])
        carry = got[3]
        attn_full.append(got[4])
    attended, mixed, mlp_in = got[3], got[5], got[6]

    def up(i, rows):
        return up_kernel(p, pos, up_w[i], i, rows, up_bias[2 * i : 2 * i + 2])

    def values(i, branch):
        return attention_values(p, attn_full[i], branch, probs[i])

    def backward(i, dc, dv, carry):
        return attention_backward(p, attn_full[i], dc, dv, qkvs[i], probs[i], carry)

    def grads(pairs, received, name, other):
        return weight_grad(p, pos, other, pairs, received, name)

    def attention_pairs(i, dv, low):
        return [(branch, ctxs[i], 0), (rows_low, dv, p.off), (rows_low, low, 2 * cols)]

    def down(i, grad_in, carry):
        return down_kernel(p, pos, up_full[i], down_w[i], i, acts[i], slopes[i], grad_in, carry)

    def leave(back, qsums, vsums, up_sums):
        arrays = dict(
            patches=x_pad, mixed=mixed, out=out_sum, back=back_sum, mixed_grad=mixed_grad,
            attended=attended, input=back, gate=gate, sel=sel_col, gain_one=gain_one,
            shift_one=shift_one, router=router, b_down=b_down, g_down=g_down_bias,
        )
        return exit_kernel(p, arrays, qsums, vsums, up_sums)

    if fast:
        act1, slope1, full1 = up(1, mlp_in)
        gd1 = grads([(og_pad, act1, 0)], None, "grad_down", 1)
        gd1_got = [send(o, core) for o in gd1]
        act0, slope0, full0 = up(0, after(mlp_in, *gd1))
        acts, slopes, up_full = (act0, act1), (slope0, slope1), (full0, full1)
        down_w = both_cores(down_eight, down_rest, act0)
        gd0 = grads([(og_pad, act0, 0)], gd1_got, "grad_down", 0)
        out_sum, back_sum, low0, sum0 = down(0, after(og_pad, *gd0), None)
        down_sum = Scatter(*gd0)
        out_sum, back_sum, low1, sum1 = down(1, after(og_pad, *gd0), (out_sum, back_sum))
        mixed_grad, branch = middle_kernel(p, og_pad, mixed, back_sum, sel_gate, gain_two)
        gu1 = grads([(after(mlp_in, branch), low1, 0)], None, "grad_up", 1)
        gu1_got = [send(o, core) for o in gu1]
        dc1, dv1, vsum1 = values(1, after(branch, *gu1))
        dc0, dv0, vsum0 = values(0, after(branch, dv1))
        down_sum.first()
        gu1_got = [after(g, dv0, down_sum.other) for g in gu1_got]
        gu0 = grads([(mlp_in, low0, 0)], gu1_got, "grad_up", 0)
        up_sum = Scatter(*gu0)
        low1, carry, qsum1 = backward(1, after(dc1, *gu0), dv1, None)
        ga1 = grads(attention_pairs(1, dv1, low1), None, "grad_attn", 1)
        ga1_got = [send(o, core) for o in ga1]
        low0, carry, qsum0 = backward(0, after(dc0, *ga1), dv0, carry)
        down_sum.second(low0)
        up_sum.first(*down_sum.pieces)
        ga1_got = [after(g, up_sum.other) for g in ga1_got]
        ga0 = grads(attention_pairs(0, dv0, low0), ga1_got, "grad_attn", 0)
        attn_sum = Scatter(*ga0)
        carry = after(carry, *ga0)
        tokens, grad_patches, *vecs = leave(carry, (qsum0, qsum1), (vsum0, vsum1), (sum0, sum1))
        vec_sum = VectorSum(vecs)
        down_parts = along_chips(down_sum.pieces, grad_patches)
        up_sum.second(*down_parts)
        vec_sum.over_cores(*up_sum.pieces)
        attn_sum.first(vec_sum.vec)
        down_parts[0] = after(down_parts[0], attn_sum.other)
        (grad_down,) = total_kernel(down_parts, [(0, p.hid, True)])
        up_parts = along_chips(up_sum.pieces, grad_down)
        vec_sum.over_z(1, *up_parts)
        attn_sum.second(vec_sum.vec)
        vec_sum.over_z(2, *attn_sum.pieces)
        up_parts[0] = after(up_parts[0], *attn_sum.pieces)
        (grad_up,) = total_kernel(up_parts, [(0, p.hid, False)])
        attn_parts = along_chips(attn_sum.pieces, grad_up)
        summed = vec_sum.over_xy(grad_up)
        grad_out, grad_value, grad_query, grad_key = total_kernel(
            attn_parts, [(i * cols, (i + 1) * cols, i == 0) for i in range(4)]
        )
    else:
        acts, slopes, up_full = zip(*(up(i, mlp_in) for i in range(p.pairs)))
        carry, lows, up_sums = None, [], []
        for i in range(p.pairs):
            got = down(i, og_pad, carry)
            carry = (got[0], got[1])
            lows.append(got[2])
            up_sums.append(got[3])
        out_sum, back_sum = carry
        mixed_grad, branch = middle_kernel(p, og_pad, mixed, back_sum, sel_gate, gain_two)
        carry, blocks, vsums, qsums = None, [], [], []
        for i in range(p.pairs):
            dc, dv, vsum = values(i, branch)
            low, carry, qsum = backward(i, dc, dv, carry)
            blocks += grads(attention_pairs(i, dv, low), None, "grad_attn", 0)
            vsums.append(vsum)
            qsums.append(qsum)
        tokens, grad_patches, *vecs = leave(carry, qsums, vsums, up_sums)
        grad_down, grad_up, grad_attn = (
            scatter_whole(p, g)
            for g in (
                [grads([(og_pad, a, 0)], None, "grad_down", 0)[0] for a in acts],
                [grads([(mlp_in, v, 0)], None, "grad_up", 0)[0] for v in lows],
                blocks,
            )
        )
        grad_down = grad_down.T
        grad_out, grad_value, grad_query, grad_key = (
            grad_attn[:, i * cols : (i + 1) * cols] for i in range(4)
        )
        grad_out = grad_out.T
        summed = sum_vectors(p, vecs)

    vecs = [summed[i] for i in range(7)]
    owned, hidden_sum = summed[8], summed[9]
    return (
        tokens,
        grad_patches,
        vecs[0],
        vecs[1],
        vecs[2],
        grad_query,
        owned[:cols],
        grad_key,
        grad_value,
        owned[cols : 2 * cols],
        grad_out,
        vecs[3],
        vecs[4],
        vecs[5],
        grad_up,
        hidden_sum,
        grad_down,
        vecs[6],
    )


def solution(mesh):
    rows, rep = P(("dp", "head"), None), P()
    split, side, turned = P("dp", "head"), P("head"), P("head", "dp")
    return jax.shard_map(
        on_device,
        mesh=mesh,
        in_specs=(
            rows, rows, rows, rep, rep, rep, split, side, split, split, side, turned, rep, rep,
            rep, split, side, turned, rep,
        ),
        out_specs=(
            rows, rows, rep, rep, rep, split, side, split, split, side, turned, rep, rep, rep,
            split, side, turned, rep,
        ),
        check_vma=False,
    )
```

```python
import math

import jax
import jax.numpy as jnp
from jax import lax
from jax.experimental import pallas as pl
from jax.experimental.pallas import tpu as pltpu
from jax.sharding import PartitionSpec as P

HEADS = 12
EPS = 1e-06
F32 = jnp.float32
BF16 = jnp.bfloat16
VMEM = pl.BlockSpec(memory_space=pltpu.VMEM)
SMEM = pl.BlockSpec(memory_space=pltpu.SMEM)
EXIT = 2.0
WEIGHT = 4.0e9
LIMIT = 20 * 1024 * 1024
INV_SQRT2 = 0.7071067811865476
INV_SQRT2PI = 0.3989422804014327

NN = (((1,), (0,)), ((), ()))
NT = (((1,), (1,)), ((), ()))
TN = (((0,), (0,)), ((), ()))


def dot(a, b, dims=NN):
    return lax.dot_general(a, b, dims, preferred_element_type=F32)


def sds(shape, dtype):
    return jax.ShapeDtypeStruct(shape, dtype)


def call(body, outs, ins, scratch=(), micros=1.0, name=None):
    return pl.pallas_call(
        body,
        out_shape=[o for o, _ in outs],
        in_specs=[s for _, s in ins],
        out_specs=[s for _, s in outs],
        scratch_shapes=list(scratch),
        compiler_params=pltpu.CompilerParams(vmem_limit_bytes=LIMIT),
        cost_estimate=pl.CostEstimate(
            flops=int(micros * WEIGHT), bytes_accessed=0, transcendentals=0
        ),
        name=name,
    )(*[a for a, _ in ins])


def norm_parts(v):
    center = v - jnp.mean(v, axis=-1, keepdims=True)
    spread = jnp.mean(center * center, axis=-1, keepdims=True)
    rstd = lax.rsqrt(spread + EPS)
    return center * rstd, rstd


def norm_back(u, xhat, rstd):
    return rstd * (
        u
        - jnp.mean(u, axis=-1, keepdims=True)
        - xhat * jnp.mean(u * xhat, axis=-1, keepdims=True)
    )


class Plan:
    def __init__(self, rows, seq, images, width, hidden, dp, head):
        self.rows, self.seq, self.images, self.width = rows, seq, images, width
        self.dp, self.head = dp, head
        self.pairs = head // 2
        self.cols = width // head
        self.hid = hidden // head
        self.hd = width // HEADS
        self.local_heads = HEADS // head
        self.piece = width // dp
        self.fast = dp == 8 and head == 4 and self.piece % 16 == 0
        self.base = [seq * i // 16 * 16 for i in range(images)]
        self.win = max(-(-(seq * (i + 1) - self.base[i]) // 16) * 16 for i in range(images))
        self.pad = self.base[-1] + self.win
        self.off = self.cols // 128 * 128
        self.lo = self.cols - self.off
        self.nq = 4 * self.cols - self.off
        self.cw = -(-self.cols // 128) * 128
        self.scale = 1.0 / math.sqrt(self.hd)
        self.exact = math.log2(self.scale).is_integer()


def source_rows(p, pos_ref, zz, xx):
    z, x = pos_ref[0], pos_ref[1]
    part = ((z - zz) & 3) * 2 + (x ^ xx)
    return pl.multiple_of(part * p.piece, p.piece)


def piece_list(p, pos_ref, other):
    core = pos_ref[2] ^ other
    found = []
    for b3 in range(2):
        for b2 in range(2):
            yy = jnp.where(core == 0, b3, b2)
            xx = jnp.where(core == 0, b2, b3)
            for zz in range(4):
                found.append((b3, b2, zz, yy, source_rows(p, pos_ref, zz, xx)))
    return found


def gather_blocks(p, refs, buf, pos_ref, other, lanes=slice(None), turned=False):
    if not p.fast:
        buf[...] = refs[0][:, :, lanes]
        return
    for b3, b2, zz, yy, row in piece_list(p, pos_ref, other):
        i, j = (zz, b2) if turned else (b2, zz)
        buf[yy, pl.ds(row, p.piece), :] = refs[b3][i, j, :, lanes]


def spread_blocks(p, buf, refs, pos_ref, other, received=None, turned=False):
    if not p.fast:
        refs[0][...] = buf[...].astype(BF16)
        return
    for b3, b2, zz, yy, row in piece_list(p, pos_ref, other):
        i, j = (zz, b2) if turned else (b2, zz)
        part = buf[yy, pl.ds(row, p.piece), :]
        if received is not None:
            part = part + received[b3][i, j].astype(F32)
        refs[b3][i, j] = part.astype(BF16)


def piece_shapes(p, lanes, turned=False):
    if p.fast:
        return [sds(((4, 2) if turned else (2, 4)) + (p.piece, lanes), BF16)] * 2
    return [sds((2, p.width, lanes), BF16)]


def entry_kernel(p, patches, out_grad, gain_one, shift_one, router):
    def body(x_ref, og_ref, g_ref, s_ref, r_ref, low_ref, gate_ref, down_ref):
        xhat, _ = norm_parts(x_ref[...].astype(F32))
        normed = xhat * g_ref[...] + s_ref[...]
        low_ref[...] = normed.astype(BF16)
        logit = jnp.sum(normed * r_ref[...], axis=-1, keepdims=True)
        gate_ref[...] = 1.0 / (1.0 + jnp.exp(-logit))
        down_ref[...] = jnp.sum(og_ref[...].astype(F32), axis=0, keepdims=True)

    return call(
        body,
        [
            (sds((p.pad, p.width), BF16), VMEM),
            (sds((p.pad, 1), F32), VMEM),
            (sds((1, p.width), F32), VMEM),
        ],
        [(a, VMEM) for a in (patches, out_grad, gain_one, shift_one, router)],
        micros=0.7,
        name="entry",
    )


def attention_forward(p, pos, weights, other, rows_low, bias, key_mask, carry, tail):
    last = tail is not None
    win, pad, lh, hd = p.win, p.pad, p.local_heads, p.hd

    def body(*refs):
        nw = len(weights)
        pos_ref, w_refs = refs[0], refs[1 : 1 + nw]
        rest = list(refs[1 + nw :])
        low_ref, bias_ref, mask_ref = rest[:3]
        rest = rest[3:]
        carry_ref = None
        if carry is not None:
            carry_ref, rest = rest[0], rest[1:]
        if last:
            x_ref, sg_ref, bo_ref, g2_ref, s2_ref = rest[:5]
            rest = rest[5:]
            qkv_ref, prob_ref, ctx_ref, att_ref, wbuf, mixed_ref, in_ref = rest[:7]
        else:
            qkv_ref, prob_ref, ctx_ref, att_ref, wbuf = rest[:5]
        ctx = rest[-1]
        gather_blocks(p, w_refs, wbuf, pos_ref, other)
        low = low_ref[...]
        total = None
        for b in range(2):
            qkv = dot(low, wbuf[b, :, p.off :]) + bias_ref[b]
            qkv_ref[b] = qkv.astype(BF16)
            ctx[...] = jnp.zeros((pad, p.cw), F32)
            for img in range(p.images):
                first = p.base[img]
                at = lax.broadcasted_iota(jnp.int32, (win, 1), 0) + first
                valid = (at >= p.seq * img) & (at < p.seq * (img + 1))
                seen = mask_ref[img] > 0.0
                got = []
                for j in range(lh):
                    qs = p.lo + hd * j
                    q = qkv_ref[b, first : first + win, qs : qs + hd]
                    k = qkv_ref[b, first : first + win, qs + p.cols : qs + p.cols + hd]
                    v = qkv_ref[b, first : first + win, qs + 2 * p.cols : qs + 2 * p.cols + hd]
                    if p.exact:
                        s = dot(q * jnp.asarray(p.scale, BF16), k, NT)
                    else:
                        s = dot(q, k, NT) * p.scale
                    s = jnp.where(seen, s, -1e30)
                    e = jnp.exp(s - jnp.max(s, axis=-1, keepdims=True))
                    share = jnp.where(valid, 1.0 / jnp.sum(e, axis=-1, keepdims=True), 0.0)
                    prob = (e * share).astype(BF16)
                    prob_ref[(b * p.images + img) * lh + j] = prob
                    got.append(dot(prob, v))
                if p.cw > p.cols:
                    got.append(jnp.zeros((win, p.cw - p.cols), F32))
                ctx[first : first + win, :] += jnp.concatenate(got, axis=1)
            mix = ctx[...].astype(BF16)
            ctx_ref[b] = mix
            part = dot(mix, wbuf[b, :, : p.cw], NT)
            total = part if total is None else total + part
        if carry_ref is not None:
            total = total + carry_ref[...]
        if not last:
            att_ref[...] = total
            return
        attended = total + bo_ref[...]
        att_ref[...] = attended
        mixed = x_ref[...].astype(F32) + sg_ref[...] * attended
        mixed_ref[...] = mixed
        xhat, _ = norm_parts(mixed)
        in_ref[...] = (xhat * g2_ref[...] + s2_ref[...]).astype(BF16)

    ins = [(pos, SMEM)] + [(w, VMEM) for w in weights]
    ins += [(a, VMEM) for a in (rows_low, bias, key_mask)]
    if carry is not None:
        ins.append((carry, VMEM))
    if last:
        ins += [(a, VMEM) for a in tail]
    outs = [
        (sds((2, pad, p.nq), BF16), VMEM),
        (sds((2 * p.images * lh, win, win), BF16), VMEM),
        (sds((2, pad, p.cw), BF16), VMEM),
        (sds((pad, p.width), F32), VMEM),
        (sds((2, p.width, 4 * p.cols), BF16), VMEM),
    ]
    if last:
        outs += [(sds((pad, p.width), F32), VMEM), (sds((pad, p.width), BF16), VMEM)]
    return call(
        body,
        outs,
        ins,
        [pltpu.VMEM((pad, p.cw), F32)],
        micros=5.5,
        name="attn_fwd",
    )


def up_kernel(p, pos, weights, other, mlp_in, bias):
    def body(*refs):
        nw = len(weights)
        pos_ref, w_refs = refs[0], refs[1 : 1 + nw]
        in_ref, b_ref, act_ref, slope_ref, wbuf = refs[1 + nw :]
        gather_blocks(p, w_refs, wbuf, pos_ref, other)
        rows = in_ref[...]
        for b in range(2):
            pre = dot(rows, wbuf[b]) + b_ref[b]
            phi = 0.5 * (1.0 + lax.erf(pre * INV_SQRT2))
            act_ref[b] = (pre * phi).astype(BF16)
            slope_ref[b] = (phi + pre * (jnp.exp(-0.5 * pre * pre) * INV_SQRT2PI)).astype(BF16)

    return call(
        body,
        [(sds((2, p.pad, p.hid), BF16), VMEM)] * 2 + [(sds((2, p.width, p.hid), BF16), VMEM)],
        [(pos, SMEM)] + [(w, VMEM) for w in weights] + [(mlp_in, VMEM), (bias, VMEM)],
        micros=2.5,
        name="up",
    )


def weight_grad(p, pos, other, pairs, received, name, turned=False):
    lanes = max(at + rhs.shape[2] for _, rhs, at in pairs)
    starts = [at for _, _, at in pairs]

    def body(*refs):
        pos_ref, rest = refs[0], list(refs[1:])
        ops, rest = rest[: 2 * len(pairs)], rest[2 * len(pairs) :]
        nr = len(received) if received is not None else 0
        got_refs, rest = rest[:nr], rest[nr:]
        out_refs, gbuf = rest[:-1], rest[-1]
        turned_lhs = {}
        for i, (lhs, _, _) in enumerate(pairs):
            if id(lhs) not in turned_lhs:
                turned_lhs[id(lhs)] = ops[2 * i][...].T
        for b in range(2):
            done = 0
            for i, at in enumerate(starts):
                g = dot(turned_lhs[id(pairs[i][0])], ops[2 * i + 1][b])
                end = at + g.shape[1]
                if at < done:
                    gbuf[b, :, at:done] += g[:, : done - at]
                    gbuf[b, :, done:end] = g[:, done - at :]
                else:
                    gbuf[b, :, at:end] = g
                done = end
        spread_blocks(p, gbuf, out_refs, pos_ref, other, got_refs if nr else None, turned)

    return call(
        body,
        [(s, VMEM) for s in piece_shapes(p, lanes, turned)],
        [(pos, SMEM)]
        + [(a, VMEM) for lhs, rhs, _ in pairs for a in (lhs, rhs)]
        + [(r, VMEM) for r in received or ()],
        [pltpu.VMEM((2, p.width, lanes), F32)],
        micros=2.3,
        name=name,
    )


def down_kernel(p, pos, w_up, w_down, other, active, slope, out_grad, carry):
    def body(*refs):
        nw = len(w_down)
        pos_ref, d_refs = refs[0], refs[1 : 1 + nw]
        ubuf, act_ref, slope_ref, og_ref = refs[1 + nw : 5 + nw]
        rest = list(refs[5 + nw :])
        if carry is not None:
            out_in, back_in = rest[:2]
            rest = rest[2:]
        out_ref, back_ref, low_ref, bias_ref, dbuf = rest
        gather_blocks(p, d_refs, dbuf, pos_ref, other, turned=True)
        og = og_ref[...]
        for b in range(2):
            grad = dot(og, dbuf[b]) * slope_ref[b].astype(F32)
            bias_ref[b] = jnp.sum(grad, axis=0, keepdims=True)
            low = grad.astype(BF16)
            low_ref[b] = low
            back = dot(low, ubuf[b], NT)
            out = dot(act_ref[b], dbuf[b], NT)
            if b == 0 and carry is not None:
                back_ref[...] = back_in[...] + back
                out_ref[...] = out_in[...] + out
            elif b == 0:
                back_ref[...] = back
                out_ref[...] = out
            else:
                back_ref[...] += back
                out_ref[...] += out

    ins = [(pos, SMEM)] + [(w, VMEM) for w in w_down]
    ins += [(a, VMEM) for a in (w_up, active, slope, out_grad)]
    if carry is not None:
        ins += [(a, VMEM) for a in carry]
    return call(
        body,
        [
            (sds((p.pad, p.width), F32), VMEM),
            (sds((p.pad, p.width), F32), VMEM),
            (sds((2, p.pad, p.hid), BF16), VMEM),
            (sds((2, 1, p.hid), F32), VMEM),
        ],
        ins,
        [pltpu.VMEM((2, p.width, p.hid), BF16)],
        micros=5.0,
        name="down",
    )


def middle_kernel(p, out_grad, mixed, back_sum, sel_gate, gain_two):
    def body(og_ref, mix_ref, back_ref, sg_ref, g2_ref, mg_ref, br_ref):
        xhat, rstd = norm_parts(mix_ref[...])
        mg = og_ref[...].astype(F32) + norm_back(back_ref[...] * g2_ref[...], xhat, rstd)
        mg_ref[...] = mg
        br_ref[...] = (sg_ref[...] * mg).astype(BF16)

    return call(
        body,
        [(sds((p.pad, p.width), F32), VMEM), (sds((p.pad, p.width), BF16), VMEM)],
        [(a, VMEM) for a in (out_grad, mixed, back_sum, sel_gate, gain_two)],
        micros=2.0,
        name="middle",
    )


def attention_values(p, weights, branch, probs):
    win, pad, lh, hd = p.win, p.pad, p.local_heads, p.hd
    lead = p.cw - p.cols

    def body(w_ref, br_ref, prob_ref, dc_ref, dv_ref, bias_ref, gv):
        for b in range(2):
            dc_ref[b] = dot(br_ref[...], w_ref[b, :, : p.cw]).astype(BF16)
            gv[...] = jnp.zeros((pad, p.cw), F32)
            for img in range(p.images):
                here = slice(p.base[img], p.base[img] + win)
                got = [jnp.zeros((win, lead), F32)] if lead else []
                for j in range(lh):
                    prob = prob_ref[(b * p.images + img) * lh + j]
                    got.append(dot(prob, dc_ref[b, here, hd * j : hd * j + hd], TN))
                gv[here, :] += jnp.concatenate(got, axis=1)
            full = gv[...]
            bias_ref[b] = jnp.sum(full, axis=0, keepdims=True)
            dv_ref[b] = full.astype(BF16)

    return call(
        body,
        [
            (sds((2, pad, p.cw), BF16), VMEM),
            (sds((2, pad, p.cw), BF16), VMEM),
            (sds((2, 1, p.cw), F32), VMEM),
        ],
        [(a, VMEM) for a in (weights, branch, probs)],
        [pltpu.VMEM((pad, p.cw), F32)],
        micros=2.5,
        name="attn_values",
    )


def attention_backward(p, weights, dc, dv, qkv, probs, carry):
    win, pad, lh, hd, cols = p.win, p.pad, p.local_heads, p.hd, p.cols
    lead = p.cw - p.cols

    def body(*refs):
        w_ref, dc_ref, dv_ref, qkv_ref, prob_ref = refs[:5]
        rest = list(refs[5:])
        if carry is not None:
            carry_ref, rest = rest[0], rest[1:]
        low_ref, n1_ref, bias_ref, gq = rest
        total = None
        for b in range(2):
            gq[...] = jnp.zeros((pad, 2 * cols), F32)
            for img in range(p.images):
                first = p.base[img]
                here = slice(first, first + win)
                dqs, dks = [], []
                for j in range(lh):
                    qs = p.lo + hd * j
                    q = qkv_ref[b, here, qs : qs + hd]
                    k = qkv_ref[b, here, qs + cols : qs + cols + hd]
                    v = qkv_ref[b, here, qs + 2 * cols : qs + 2 * cols + hd]
                    d = dc_ref[b, here, hd * j : hd * j + hd]
                    soft = prob_ref[(b * p.images + img) * lh + j].astype(F32)
                    if p.exact:
                        pg = dot(d * jnp.asarray(p.scale, BF16), v, NT)
                    else:
                        pg = dot(d, v, NT) * p.scale
                    row = jnp.sum(soft * pg, axis=-1, keepdims=True)
                    s = (soft * (pg - row)).astype(BF16)
                    dqs.append(dot(s, k))
                    dks.append(dot(s, q, TN))
                gq[here, :] += jnp.concatenate(dqs + dks, axis=1)
            full = gq[...]
            bias_ref[b] = jnp.sum(full, axis=0, keepdims=True)
            low = full.astype(BF16)
            low_ref[b] = low
            start = [jnp.zeros((pad, p.lo), BF16)] if p.lo else []
            gl = jnp.concatenate(start + [low, dv_ref[b][:, lead:]], axis=1)
            part = dot(gl, w_ref[b, :, p.off :], NT)
            total = part if total is None else total + part
        if carry is not None:
            total = total + carry_ref[...]
        n1_ref[...] = total

    ins = [(a, VMEM) for a in (weights, dc, dv, qkv, probs)]
    if carry is not None:
        ins.append((carry, VMEM))
    return call(
        body,
        [
            (sds((2, pad, 2 * cols), BF16), VMEM),
            (sds((pad, p.width), F32), VMEM),
            (sds((2, 1, 2 * cols), F32), VMEM),
        ],
        ins,
        [pltpu.VMEM((pad, 2 * cols), F32)],
        micros=6.0,
        name="attn_bwd",
    )


def exit_kernel(p, arrays, query, value, up):
    names = tuple(arrays)
    half = p.cols
    at = p.cw - p.cols

    def body(*refs):
        a = dict(zip(names, refs))
        rest = list(refs[len(names) :])
        q_refs, v_refs, u_refs = (rest[i * p.pairs : (i + 1) * p.pairs] for i in range(3))
        tok_ref, out_ref, *vec_refs = rest[3 * p.pairs :]
        mixed = a["mixed"][...]
        tok_ref[...] = (mixed + a["out"][...] + a["b_down"][...])[: p.rows].astype(BF16)
        xhat, _ = norm_parts(mixed)
        back = a["back"][...]
        g_gain2 = jnp.sum(back * xhat, axis=0, keepdims=True)
        g_shift2 = jnp.sum(back, axis=0, keepdims=True)
        mg, gate, sel = a["mixed_grad"][...], a["gate"][...], a["sel"][...]
        g_out = jnp.sum((sel * gate) * mg, axis=0, keepdims=True)
        rows = jnp.sum(mg * a["attended"][...], axis=-1, keepdims=True)
        logit = sel * rows * gate * (1.0 - gate)
        xhat, rstd = norm_parts(a["patches"][...].astype(F32))
        normed = xhat * a["gain_one"][...] + a["shift_one"][...]
        g_router = jnp.sum(normed * logit, axis=0, keepdims=True)
        grad = a["input"][...] + logit * a["router"][...]
        g_gain1 = jnp.sum(grad * xhat, axis=0, keepdims=True)
        g_shift1 = jnp.sum(grad, axis=0, keepdims=True)
        total = mg + norm_back(grad * a["gain_one"][...], xhat, rstd)
        out_ref[...] = total[: p.rows].astype(BF16)
        common = [g_gain1, g_shift1, g_router, g_out, g_gain2, g_shift2, a["g_down"][...]]
        for i in range(p.pairs):
            vec = vec_refs[i]
            vec[...] = jnp.zeros(vec.shape, F32)
            for j, r in enumerate(common):
                vec[j : j + 1, :] = r
            for b in range(2):
                row = 8 + 2 * b
                vec[row : row + 1, : 2 * half] = q_refs[i][b]
                vec[row : row + 1, half : 2 * half] = v_refs[i][b][:, at:]
                vec[row + 1 : row + 2, :] = u_refs[i][b]

    return call(
        body,
        [(sds((p.rows, p.width), BF16), VMEM)] * 2
        + [(sds((12, p.width), F32), VMEM)] * p.pairs,
        [(v, VMEM) for v in list(arrays.values()) + list(query) + list(value) + list(up)],
        micros=5.0,
        name="exit",
    )


def halves_kernel(keep, got):
    def body(k_ref, g_ref, mine_ref, other_ref):
        mine_ref[...] = (k_ref[0].astype(F32) + g_ref[0].astype(F32)).astype(BF16)
        other_ref[...] = (k_ref[1].astype(F32) + g_ref[1].astype(F32)).astype(BF16)

    return call(
        body,
        [(sds(keep.shape[1:], BF16), VMEM)] * 2,
        [(keep, VMEM), (got, VMEM)],
        micros=4.0,
        name="halves",
    )


def parts_kernel(mine, got):
    def body(m_ref, g_ref, *part_refs):
        for i, ref in enumerate(part_refs):
            ref[...] = (m_ref[i].astype(F32) + g_ref[i].astype(F32)).astype(BF16)

    return call(
        body,
        [(sds(mine.shape[1:], BF16), VMEM)] * 4,
        [(mine, VMEM), (got, VMEM)],
        micros=4.0,
        name="parts",
    )


def total_kernel(pieces, cuts):
    def body(*refs):
        total = sum((r[...].astype(F32) for r in refs[1:4]), refs[0][...].astype(F32))
        for (first, last, turned), ref in zip(cuts, refs[4:]):
            part = total[:, first:last]
            ref[...] = part.T if turned else part

    rows = pieces[0].shape[0]
    return call(
        body,
        [(sds((b - a, rows) if t else (rows, b - a), F32), VMEM) for a, b, t in cuts],
        [(v, VMEM) for v in pieces],
        micros=4.0,
        name="total",
    )


def flat(z, x, y, c):
    return ((z * 2 + x) * 2 + y) * 2 + c


def table(move):
    pairs = []
    for z in range(4):
        for x in range(2):
            for y in range(2):
                for c in range(2):
                    pairs.append((flat(z, x, y, c), flat(*move(z, x, y, c))))
    return pairs


def send(v, move):
    return lax.ppermute(v, ("dp", "head"), table(move))


def along_z(shift):
    return lambda z, x, y, c: ((z + shift) % 4, x, y, c)


def near(z, x, y, c):
    return (z, x ^ 1, y, c) if c == 0 else (z, x, y ^ 1, c)


def far(z, x, y, c):
    return (z, x, y ^ 1, c) if c == 0 else (z, x ^ 1, y, c)


def core(z, x, y, c):
    return (z, x, y, c ^ 1)


def after(v, *others):
    return lax.optimization_barrier((v,) + others)[0]


def add(a, b):
    return (a.astype(F32) + b.astype(F32)).astype(BF16)


def gather_whole(p, shard):
    full = lax.all_gather(lax.all_gather(shard, "dp", axis=0, tiled=True), "head", axis=0)
    return [(full[2 * i : 2 * i + 2],) for i in range(p.pairs)]


def own_pieces(shard):
    return jnp.stack([shard] + [send(shard, along_z(s)) for s in (1, 2, 3)])


def both_cores(eight, rest, *others):
    eight_out, rest_out = after(eight, *others), after(rest, *others)
    return [(eight, rest), (send(eight_out, core), send(rest_out, core))]


def scatter_whole(p, grads):
    stacked = jnp.concatenate(grads, axis=0)
    part = lax.psum_scatter(stacked, "head", scatter_dimension=0, tiled=False)
    return lax.psum_scatter(part, "dp", scatter_dimension=0, tiled=True).astype(F32)


class Scatter:
    def __init__(self, keep, away):
        self.keep, self.away = keep, away

    def first(self, *others):
        got = after(send(self.away, far), *others)
        self.mine, self.other = halves_kernel(self.keep, got)

    def second(self, *others):
        got = after(send(self.other, near), *others)
        self.pieces = parts_kernel(self.mine, got)


def along_chips(pieces, *others):
    return [pieces[0]] + [after(send(pieces[s], along_z(-s)), *others) for s in (1, 2, 3)]


def gather_head(p, vector):
    if not p.fast:
        return lax.all_gather(vector, "head", axis=0)
    pair = jnp.stack([vector, send(vector, lambda z, x, y, c: (z, x, y ^ 1, c))])
    return jnp.concatenate([pair, send(pair, core)], axis=0)


def sum_vectors(p, vecs):
    total = lax.psum(vecs[0][:8], ("dp", "head"))
    owned = jnp.concatenate([v[8:] for v in vecs]).reshape(p.head, 2, p.width)
    mine = lax.psum_scatter(owned, "head", scatter_dimension=0, tiled=False)
    return jnp.concatenate([total, lax.psum(mine, "dp")])


class VectorSum:
    def __init__(self, vecs):
        self.keep, self.away = vecs

    def over_cores(self, *others):
        self.vec = self.keep + send(after(self.away, *others), core)

    def over_z(self, step, *others):
        got = send(self.vec, lambda z, x, y, c: (z ^ step, x, y, c))
        self.vec = self.vec + after(got, *others)

    def over_xy(self, *others):
        mine, away = self.vec[:10], jnp.concatenate([self.vec[:8], self.vec[10:]])
        along_x = send(mine, lambda z, x, y, c: (z, x ^ 1, y, c))
        along_y = send(away, lambda z, x, y, c: (z, x, y ^ 1, c))
        across = send(away, lambda z, x, y, c: (z, x ^ 1, y ^ 1, c))
        along_x, along_y, across = (after(v, *others) for v in (along_x, along_y, across))
        return (mine + along_x) + (along_y + across)


def on_device(
    patches, selected, out_grad, gain_one, shift_one, router_w, w_query, b_query, w_key, w_value,
    b_value, w_out, b_out, gain_two, shift_two, w_up, b_up, w_down, b_down,
):
    images, seq = selected.shape
    rows, width = patches.shape
    dp, head = lax.axis_size("dp"), lax.axis_size("head")
    p = Plan(rows, seq, images, width, b_up.shape[0] * head, dp, head)
    cols, hid = p.cols, p.hid

    dp_pos, head_pos = lax.axis_index("dp"), lax.axis_index("head")
    pos = jnp.stack([dp_pos // 2, dp_pos % 2, head_pos % 2]).astype(jnp.int32)

    attn_shard = jnp.concatenate([w_out.T, w_query, w_key, w_value], axis=1)
    bias_parts = after(jnp.concatenate([b_query, b_value, b_up]), attn_shard)
    biases = gather_head(p, bias_parts).astype(F32)
    zeros = jnp.zeros((head, cols), F32)
    qkv_bias = jnp.concatenate(
        [zeros[:, : p.lo], biases[:, :cols], zeros, biases[:, cols : 2 * cols]], axis=1
    )[:, None, :]
    up_bias = biases[:, 2 * cols :][:, None, :]

    def row(v):
        return v.astype(F32)[None, :]

    more = p.pad - rows
    x_pad = jnp.pad(patches, ((0, more), (0, 0)))
    og_pad = jnp.pad(out_grad, ((0, more), (0, 0)))
    sel = selected.astype(F32)
    sel_col = jnp.pad(sel.reshape(rows, 1), ((0, more), (0, 0)))
    key_mask = jnp.stack(
        [
            jnp.pad(sel[i], (seq * i - p.base[i], p.win - seq - (seq * i - p.base[i])))
            for i in range(images)
        ]
    )[:, None, :]
    gain_one, shift_one, gain_two, shift_two = map(row, (gain_one, shift_one, gain_two, shift_two))
    router, b_out, b_down = row(router_w), row(b_out), row(b_down)

    fast = p.fast
    if fast:
        down_one = w_down.T
        down_near = send(down_one, near)
        attn_own = after(own_pieces(attn_shard), biases, down_near)
        x_in = after(x_pad, attn_own)
        rows_low, gate, g_down_bias = entry_kernel(p, x_in, og_pad, gain_one, shift_one, router)
        up_one = after(w_up, attn_own)
        up_z = [send(up_one, along_z(s)) for s in (1, 2, 3)]
        attn_eight = after(jnp.stack([attn_own, send(attn_own, near)]), rows_low, up_z[0])
        attn_rest = send(attn_eight, far)
        attn_w = both_cores(attn_eight, attn_rest)
        up_own = after(jnp.stack([w_up] + up_z), attn_eight)
        down_pair = after(jnp.stack([down_one, down_near]), up_own)
        down_z = [send(down_pair, along_z(s)) for s in (1, 2, 3)]
        up_eight = after(jnp.stack([up_own, send(up_own, near)]), attn_rest)
        up_rest = send(up_eight, far)
        attn_w[1] = tuple(after(w, up_rest) for w in attn_w[1])
        up_w = both_cores(up_eight, up_rest)
    else:
        rows_low, gate, g_down_bias = entry_kernel(p, x_pad, og_pad, gain_one, shift_one, router)
        attn_w, up_w, down_w = (gather_whole(p, v) for v in (attn_shard, w_up, w_down.T))
    sel_gate = gate * sel_col

    qkvs, probs, ctxs, attn_full, carry = [], [], [], [], None
    for i in range(p.pairs):
        tail = (x_pad, sel_gate, b_out, gain_two, shift_two) if i == p.pairs - 1 else None
        if fast and i == 1:
            down_eight = jnp.stack([down_pair] + [after(v, carry) for v in down_z])
            down_rest = send(down_eight, far)
        got = attention_forward(
            p, pos, attn_w[i], i, rows_low, qkv_bias[2 * i : 2 * i + 2], key_mask, carry, tail
        )
        qkvs.append(got[0])
        probs.append(got[1])
        ctxs.append(got[2])
        carry = got[3]
        attn_full.append(got[4])
    attended, mixed, mlp_in = got[3], got[5], got[6]

    def up(i, rows):
        return up_kernel(p, pos, up_w[i], i, rows, up_bias[2 * i : 2 * i + 2])

    def values(i, branch):
        return attention_values(p, attn_full[i], branch, probs[i])

    def backward(i, dc, dv, carry):
        return attention_backward(p, attn_full[i], dc, dv, qkvs[i], probs[i], carry)

    def grads(pairs, received, name, other):
        return weight_grad(p, pos, other, pairs, received, name)

    def attention_pairs(i, dv, low):
        return [(branch, ctxs[i], 0), (rows_low, dv, p.off), (rows_low, low, 2 * cols)]

    def down(i, grad_in, carry):
        return down_kernel(p, pos, up_full[i], down_w[i], i, acts[i], slopes[i], grad_in, carry)

    def leave(back, qsums, vsums, up_sums):
        arrays = dict(
            patches=x_pad, mixed=mixed, out=out_sum, back=back_sum, mixed_grad=mixed_grad,
            attended=attended, input=back, gate=gate, sel=sel_col, gain_one=gain_one,
            shift_one=shift_one, router=router, b_down=b_down, g_down=g_down_bias,
        )
        return exit_kernel(p, arrays, qsums, vsums, up_sums)

    if fast:
        act1, slope1, full1 = up(1, mlp_in)
        gd1 = grads([(og_pad, act1, 0)], None, "grad_down", 1)
        gd1_got = [send(o, core) for o in gd1]
        act0, slope0, full0 = up(0, after(mlp_in, *gd1))
        acts, slopes, up_full = (act0, act1), (slope0, slope1), (full0, full1)
        down_w = both_cores(down_eight, down_rest, act0)
        gd0 = grads([(og_pad, act0, 0)], gd1_got, "grad_down", 0)
        out_sum, back_sum, low0, sum0 = down(0, after(og_pad, *gd0), None)
        down_sum = Scatter(*gd0)
        out_sum, back_sum, low1, sum1 = down(1, after(og_pad, *gd0), (out_sum, back_sum))
        mixed_grad, branch = middle_kernel(p, og_pad, mixed, back_sum, sel_gate, gain_two)
        gu1 = grads([(after(mlp_in, branch), low1, 0)], None, "grad_up", 1)
        gu1_got = [send(o, core) for o in gu1]
        dc1, dv1, vsum1 = values(1, after(branch, *gu1))
        dc0, dv0, vsum0 = values(0, after(branch, dv1))
        down_sum.first()
        gu1_got = [after(g, dv0, down_sum.other) for g in gu1_got]
        gu0 = grads([(mlp_in, low0, 0)], gu1_got, "grad_up", 0)
        up_sum = Scatter(*gu0)
        low1, carry, qsum1 = backward(1, after(dc1, *gu0), dv1, None)
        ga1 = grads(attention_pairs(1, dv1, low1), None, "grad_attn", 1)
        ga1_got = [send(o, core) for o in ga1]
        low0, carry, qsum0 = backward(0, after(dc0, *ga1), dv0, carry)
        down_sum.second(low0)
        up_sum.first(*down_sum.pieces)
        ga1_got = [after(g, up_sum.other) for g in ga1_got]
        ga0 = grads(attention_pairs(0, dv0, low0), ga1_got, "grad_attn", 0)
        attn_sum = Scatter(*ga0)
        carry = after(carry, *ga0)
        tokens, grad_patches, *vecs = leave(carry, (qsum0, qsum1), (vsum0, vsum1), (sum0, sum1))
        vec_sum = VectorSum(vecs)
        down_parts = along_chips(down_sum.pieces, grad_patches)
        up_sum.second(*down_parts)
        vec_sum.over_cores(*up_sum.pieces)
        attn_sum.first(vec_sum.vec)
        down_parts[0] = after(down_parts[0], attn_sum.other)
        (grad_down,) = total_kernel(down_parts, [(0, p.hid, True)])
        up_parts = along_chips(up_sum.pieces, grad_down)
        vec_sum.over_z(1, *up_parts)
        attn_sum.second(vec_sum.vec)
        vec_sum.over_z(2, *attn_sum.pieces)
        up_parts[0] = after(up_parts[0], *attn_sum.pieces)
        (grad_up,) = total_kernel(up_parts, [(0, p.hid, False)])
        attn_parts = along_chips(attn_sum.pieces, grad_up)
        summed = vec_sum.over_xy(*attn_parts)
        grad_out, grad_value, grad_query, grad_key = total_kernel(
            attn_parts, [(i * cols, (i + 1) * cols, i == 0) for i in range(4)]
        )
    else:
        acts, slopes, up_full = zip(*(up(i, mlp_in) for i in range(p.pairs)))
        carry, lows, up_sums = None, [], []
        for i in range(p.pairs):
            got = down(i, og_pad, carry)
            carry = (got[0], got[1])
            lows.append(got[2])
            up_sums.append(got[3])
        out_sum, back_sum = carry
        mixed_grad, branch = middle_kernel(p, og_pad, mixed, back_sum, sel_gate, gain_two)
        carry, blocks, vsums, qsums = None, [], [], []
        for i in range(p.pairs):
            dc, dv, vsum = values(i, branch)
            low, carry, qsum = backward(i, dc, dv, carry)
            blocks += grads(attention_pairs(i, dv, low), None, "grad_attn", 0)
            vsums.append(vsum)
            qsums.append(qsum)
        tokens, grad_patches, *vecs = leave(carry, qsums, vsums, up_sums)
        grad_down, grad_up, grad_attn = (
            scatter_whole(p, g)
            for g in (
                [grads([(og_pad, a, 0)], None, "grad_down", 0)[0] for a in acts],
                [grads([(mlp_in, v, 0)], None, "grad_up", 0)[0] for v in lows],
                blocks,
            )
        )
        grad_down = grad_down.T
        grad_out, grad_value, grad_query, grad_key = (
            grad_attn[:, i * cols : (i + 1) * cols] for i in range(4)
        )
        grad_out = grad_out.T
        summed = sum_vectors(p, vecs)

    vecs = [summed[i] for i in range(7)]
    owned, hidden_sum = summed[8], summed[9]
    return (
        tokens,
        grad_patches,
        vecs[0],
        vecs[1],
        vecs[2],
        grad_query,
        owned[:cols],
        grad_key,
        grad_value,
        owned[cols : 2 * cols],
        grad_out,
        vecs[3],
        vecs[4],
        vecs[5],
        grad_up,
        hidden_sum,
        grad_down,
        vecs[6],
    )


def solution(mesh):
    rows, rep = P(("dp", "head"), None), P()
    split, side, turned = P("dp", "head"), P("head"), P("head", "dp")
    return jax.shard_map(
        on_device,
        mesh=mesh,
        in_specs=(
            rows, rows, rows, rep, rep, rep, split, side, split, split, side, turned, rep, rep,
            rep, split, side, turned, rep,
        ),
        out_specs=(
            rows, rows, rep, rep, rep, split, side, split, split, side, turned, rep, rep, rep,
            split, side, turned, rep,
        ),
        check_vma=False,
    )
```
